32 devices in a mesh: group: 4 (over y, x), dp: 2 (over core), expert: 4 (over z).
Axes of the slice: x: 2, y: 2, z: 4, core: 2. Of those that a mesh axis runs over, the one named last changes fastest.
Arguments:
- tokens: bfloat16 [64, 1024, 512], P(('group', 'dp'), 'expert'), may hold values from -6 to 6
- segments: int32 [64, 1024], P(('group', 'dp')), may hold values from 0 to 2, as said below
- routes: int32 [4, 64, 256, 2], P(None, ('group', 'dp')), may hold values from 0 to 3, all different within a row; in each aligned block of 256 rows (0 to 255, 256 to 511, ..., all dimensions but the last counted through in order) at most 160 rows name the same one
- gate_values: float32 [64, 1024, 2], P(('group', 'dp'), 'expert'), may hold values from 0.25 to 0.75
- gain_one: float32 [512], replicated, may hold values from 0.5 to 1.5
- gain_two: float32 [512], replicated, may hold values from 0.5 to 1.5
- kv_weight: bfloat16 [512, 128], replicated, may hold values from -0.25 to 0.25
- query_weight: bfloat16 [4, 512, 64], P('expert'), may hold values from -0.25 to 0.25
- output_weight: bfloat16 [4, 64, 512], P('expert'), may hold values from -9 to 9
- up_weight: bfloat16 [512, 2048], replicated, may hold values from -0.25 to 0.25
- down_weight: bfloat16 [2048, 512], replicated, may hold values from -0.125 to 0.125
- out_grad: bfloat16 [64, 1024, 512], P(('group', 'dp'), 'expert'), may hold values from -6 to 6
Outputs:
- output: bfloat16 [64, 1024, 512], P(('group', 'dp'), 'expert')
- token_grad: float32 [64, 1024, 512], P(('group', 'dp'), 'expert')
- gain_one_grad: float32 [512], replicated
- gain_two_grad: float32 [512], replicated
- kv_weight_grad: float32 [512, 128], replicated
- query_weight_grad: float32 [4, 512, 64], P('expert')
- output_weight_grad: float32 [4, 64, 512], P('expert')
- up_weight_grad: float32 [512, 2048], replicated
- down_weight_grad: float32 [2048, 512], replicated
The draws below stay inside these ranges and needn't reach their ends.
Inputs may be any that keep to these rules, and one draw needn't show every extreme that they name: `segments`: within a row the numbers never fall; number 1 begins within the first 256 positions and number 2 begins within the last 256 positions, so every row has three documents. `routes`: each token's 2 experts differ. Over the 256 tokens of one row on one device (one index of the first dimension and one row, an aligned block) no expert is named more than 160 times, and that bound is reached in some block.
All inputs are finite; a program needn't handle non-finite values.
Results may differ from the reference program's by a relative error of at most 0.015.
Values may be sent and summed in bfloat16 or wider, within the bound.
A program may use at most 192 MiB of HBM per device.

```python
import math
import jax
import jax.numpy as jnp
import numpy as np
from jax import lax

D = 512
DH = 64
FF = 2048
SEQ = 1024
TOP = 2
EXPERTS = 4
SLICE = 256
ROWS = 64
CAP = 160
N_EXPERT = 4


def draw_segments(key, part):
    key = jax.random.fold_in(key, 7)
    first_key, second_key = jax.random.split(key)
    first_cut = jax.random.randint(first_key, (ROWS, 1), 1, SLICE)
    second_cut = jax.random.randint(second_key, (ROWS, 1), SEQ - SLICE + 1, SEQ)
    places = jnp.arange(SEQ, dtype=jnp.int32)[None, :]
    return (places >= first_cut).astype(jnp.int32) + (places >= second_cut).astype(jnp.int32)


def steps_of(stream_key, extent, cuts, least, largest):
    def one(axis_at, blocks):
        steps = jax.random.uniform(jax.random.fold_in(jax.random.fold_in(stream_key, 6), axis_at), (blocks,), jnp.float32, least / len(cuts), largest / len(cuts))
        return jnp.repeat(jnp.exp(steps), extent[axis_at] // blocks).reshape((-1,) + (1,) * (len(extent) - axis_at - 1))

    factor_of = one(*cuts[0])
    for cut in cuts[1:]:
        factor_of = factor_of * one(*cut)
    return factor_of


def shared_out(rng, own, number, rows, amount, top, reach, slope):
    ranking = jax.random.permutation(rng, amount)
    crowded, ordinary = portions_of(amount, rows * top, reach, slope, True), portions_of(amount, rows * top, reach, slope, False)
    places = jnp.arange(amount)

    def named(lengths, turn):
        used = int((lengths > 0).sum())
        fixed = max(1, used // 4)
        passed = fixed + (places - fixed + turn * (used - fixed)) % max(1, amount - fixed)
        return jnp.zeros((amount,), jnp.int32).at[ranking[jnp.where(places < fixed, places, passed)]].set(jnp.asarray(lengths, jnp.int32))

    lengths = jnp.where(number % 4 == 0, named(crowded, number // 4), named(ordinary, number - number // 4 - 1))
    mixed = jax.random.permutation(jax.random.fold_in(own, 3), amount)
    giver, receiver = mixed[0:amount // 2 * 2:2], mixed[1:amount // 2 * 2:2]
    margin = jnp.minimum(lengths[giver] - 1, reach - lengths[receiver]) // 2
    margin = jnp.where((giver == ranking[0]) | (receiver == ranking[0]) | (lengths[receiver] == 0), 0, jnp.maximum(margin, 0))
    passed = jax.random.randint(jax.random.fold_in(own, 4), (amount // 2,), 0, 1 << 20) % (margin + 1)
    lengths = lengths.at[giver].add(-passed).at[receiver].add(passed)
    labels = jnp.searchsorted(jnp.cumsum(lengths), jnp.arange(rows * top), side="right").astype(jnp.int32)
    listing = labels.reshape(top, rows).T
    listing = listing[jax.random.permutation(jax.random.fold_in(own, 1), rows)]
    turn = jax.random.randint(jax.random.fold_in(own, 2), (rows, 1), 0, top)
    return jnp.take_along_axis(listing, (jnp.arange(top)[None, :] + turn) % top, axis=1)


def portions_of(amount, total, most, skew, full):
    weights = [(1 << 20) // math.isqrt(grade ** skew) + 1 for grade in range(1, amount + 1)]
    largest = most if full else min(most, max(-(-total // amount), total * weights[0] // sum(weights)))
    least = 1 if total - largest >= amount - 1 else 0
    counts, surplus = [largest] + [least] * (amount - 1), total - largest - least * (amount - 1)
    while surplus > 0:
        free = [i for i in range(1, amount) if counts[i] < largest] or [i for i in range(1, amount) if counts[i] < most]
        whole, budget = sum([weights[i] for i in free]), surplus
        for i in free:
            more = min(most - counts[i], max(1, budget * weights[i] // whole), surplus)
            counts[i] = counts[i] + more
            surplus = surplus - more
    return np.array(counts)


def bell_draw(own_key, shape, deviation, limit, cuts=(), kind=jnp.bfloat16):
    values = jax.random.normal(own_key, shape, jnp.float32) * deviation
    if len(cuts) > 0:
        values = steps_of(own_key, shape, cuts, -0.22, 0.18) * values
    return jnp.clip(values, min=-limit, max=limit).astype(kind)


def setup_inputs(seed: int = 0) -> dict:
    splits = jax.random.split(jax.random.key(seed), 13)
    tokens = bell_draw(splits[0], (ROWS, SEQ, D), 1.0, 6.0, ((0, 8), (1, 4)))
    segments = draw_segments(jax.random.fold_in(splits[12], 71), 0)
    routes_keys = jax.random.split(jax.random.fold_in(splits[2], 1), N_EXPERT * ROWS * SLICE // SLICE)
    routes_turns = jax.random.permutation(jax.random.fold_in(splits[2], 3), N_EXPERT * ROWS * SLICE // SLICE)
    routes = jax.vmap(lambda own, number: shared_out(jax.random.fold_in(splits[2], 2), own, number, SLICE, EXPERTS, TOP, CAP, 1))(routes_keys, routes_turns).reshape((N_EXPERT, ROWS, SLICE, TOP))
    gate_values = jnp.clip(0.25 + 0.5 * jax.random.uniform(splits[3], (ROWS, SEQ, TOP), jnp.float32) ** steps_of(splits[3], (ROWS, SEQ, TOP), ((0, 8), (1, 4)), -0.2, 0.2), 0.25, 0.75)
    gain_one = jnp.clip(1.0 + 0.1 * jax.random.normal(splits[4], (D,), jnp.float32), 0.5, 1.5)
    gain_two = jnp.clip(1.0 + 0.1 * jax.random.normal(splits[5], (D,), jnp.float32), 0.5, 1.5)
    kv_weight = bell_draw(splits[6], (D, 2 * DH), D ** -0.5, 0.25)
    query_weight = bell_draw(splits[7], (EXPERTS, D, DH), D ** -0.5, 0.25, ((0, 4),))
    output_weight = bell_draw(splits[8], (EXPERTS, DH, D), 1.5, 9.0, ((0, 4),))
    up_weight = bell_draw(splits[9], (D, FF), D ** -0.5, 0.25)
    down_weight = bell_draw(splits[10], (FF, D), FF ** -0.5, 0.125)
    out_grad = bell_draw(splits[11], (ROWS, SEQ, D), 1.0, 6.0, ((0, 8), (1, 4)))
    return {"tokens": tokens, "segments": segments, "routes": routes, "gate_values": gate_values, "gain_one": gain_one, "gain_two": gain_two, "kv_weight": kv_weight, "query_weight": query_weight, "output_weight": output_weight, "up_weight": up_weight, "down_weight": down_weight, "out_grad": out_grad}


@jax.custom_vjp
def low(v):
    return lax.optimization_barrier(v.astype(jnp.bfloat16)).astype(jnp.float32)

@jax.custom_vjp
def low_back(v):
    return v

def low_keep(v):
    return (low(v), None)

def low_pass(kept, grad):
    return (grad,)

def back_keep(v):
    return (v, None)

def back_low(kept, grad):
    return (low(grad),)
low.defvjp(low_keep, low_pass)
low_back.defvjp(back_keep, back_low)
epsilon = 1e-06
highest_precision = lax.Precision.HIGHEST

def norm_rows(value, gain):
    return value * lax.rsqrt(lax.optimization_barrier(jnp.mean(value * value, axis=-1, keepdims=True)) + epsilon) * gain

def block_forward(params, tokens_in, segment_ids, route_ids, gate_rows):
    gain_one, gain_two, kv_weight, query_weight, output_weight, up_weight, down_weight = params
    normed = low(norm_rows(tokens_in, gain_one))
    keyval = low(low_back(jnp.einsum('rsd,dc->rsc', normed, kv_weight, precision=highest_precision)))
    keys = keyval[..., :DH]
    values = keyval[..., DH:]
    same_doc = segment_ids[:, :, None] == segment_ids[:, None, :]
    expert_range = jnp.arange(EXPERTS, dtype=jnp.int32)
    scale_factor = 1.0 / jnp.sqrt(jnp.float32(DH))
    mixed = jnp.zeros_like(tokens_in)
    for route in range(TOP):
        picked = (route_ids[..., route, None] == expert_range).astype(jnp.float32)
        chosen = low_back(normed)
        query_all = jnp.einsum('rsd,edh->rseh', chosen, query_weight, precision=highest_precision)
        query = low(low_back(lax.optimization_barrier(jnp.sum(query_all * picked[..., None], axis=2))))
        raw_scores = jnp.einsum('rqh,rkh->rqk', query, keys, precision=highest_precision) * scale_factor
        raw_scores = low_back(jnp.where(same_doc, raw_scores, -1e+30))
        attn_probs = jax.nn.softmax(raw_scores, axis=-1)
        attended = low(low_back(jnp.einsum('rqk,rkh->rqh', low(attn_probs), values, precision=highest_precision)))
        out_all = jnp.einsum('rsh,ehd->rsed', attended, output_weight, precision=highest_precision)
        branch = low(low_back(lax.optimization_barrier(jnp.sum(out_all * picked[..., None], axis=2))))
        mixed = mixed + gate_rows[..., route, None] * branch
    residual = tokens_in + mixed
    second = low(norm_rows(residual, gain_two))
    hidden = low_back(jnp.einsum('rsd,df->rsf', second, up_weight, precision=highest_precision))
    active = low(jax.nn.gelu(hidden))
    return residual + jnp.einsum('rsf,fd->rsd', active, down_weight, precision=highest_precision)

def reference(tokens, segments, routes, gate_values, gain_one, gain_two, kv_weight, query_weight, output_weight, up_weight, down_weight, out_grad):
    route_rows = jnp.transpose(routes, (1, 0, 2, 3)).reshape(ROWS, SEQ, TOP)
    params = (gain_one.astype(jnp.float32), gain_two.astype(jnp.float32), kv_weight.astype(jnp.float32), query_weight.astype(jnp.float32), output_weight.astype(jnp.float32), up_weight.astype(jnp.float32), down_weight.astype(jnp.float32))
    group_rows = 4 if ROWS % 4 == 0 else 1
    group_total = ROWS // group_rows

    def regroup(array):
        return array.reshape((group_total, group_rows) + array.shape[1:])

    def advance(totals, pieces):
        tok_piece, seg_piece, route_piece, gate_piece, cot_piece = pieces

        def forward_only(weights, inputs):
            return block_forward(weights, inputs, seg_piece, route_piece, gate_piece)
        result, pullback = jax.vjp(forward_only, params, tok_piece.astype(jnp.float32))
        weight_grads, input_grad = pullback(cot_piece.astype(jnp.float32))
        totals = jax.tree.map(lambda first, later: first + later, totals, weight_grads)
        return (totals, (result.astype(jnp.bfloat16), input_grad))
    zeros_like_params = jax.tree.map(jnp.zeros_like, params)
    totals, (outputs, input_grads) = lax.scan(advance, zeros_like_params, (regroup(tokens), regroup(segments), regroup(route_rows), regroup(gate_values), regroup(out_grad)))
    return (outputs.reshape(ROWS, SEQ, D), input_grads.reshape(ROWS, SEQ, D), totals[0], totals[1], totals[2], totals[3], totals[4], totals[5], totals[6])
```

```python
import functools
import math

import jax
import jax.numpy as jnp
from jax import lax
from jax.experimental import pallas as pl
from jax.experimental.pallas import tpu as pltpu
from jax.sharding import PartitionSpec as P

EPS = 1e-06
F32 = jnp.float32
BF = jnp.bfloat16
LOG2E = 1.4426950408889634
VMEM_LIMIT = 60 * 2**20


def nn(a, b):
    return lax.dot_general(a, b, (((1,), (0,)), ((), ())), preferred_element_type=F32)


def nt(a, b):
    return lax.dot_general(a, b, (((1,), (1,)), ((), ())), preferred_element_type=F32)


def gelu_both(x):
    c0 = math.sqrt(2.0 / math.pi)
    c1 = 0.044715 * c0
    x2 = x * x
    t = jnp.tanh(x * (c0 + c1 * x2))
    h = 0.5 + 0.5 * t
    act = x * h
    slope = h + (act - act * h) * (2.0 * c0 + (6.0 * c1) * x2)
    return act, slope


def inv_rms(x):
    return lax.rsqrt(jnp.mean(x * x, axis=-1, keepdims=True) + EPS)


def rms_back(x, gain, dy):
    inv = inv_rms(x)
    xn = x * inv
    gdy = gain * dy
    dx = inv * (gdy - xn * jnp.mean(xn * gdy, axis=-1, keepdims=True))
    return dx, dy * xn


def fold(x):
    return jnp.sum(x.reshape(x.shape[0] // 8, 8, x.shape[1]), axis=0)


def main_kernel(
    experts, rows, width, seq, fblk,
    tok_ref, cot_ref, kv_ref, seg_ref, route_ref, gate_ref, g1_ref, g2_ref,
    wst_ref, wo_ref, up_ref, dn_ref,
    out_ref, r_ref, qg_ref, kvp_ref, g2g_ref, dwo_ref, dup_ref, ddn_ref,
    cut_ref, p_ref, kvt_ref, qt_ref, att_ref, rinv_ref, gt_ref, res_ref, sec_ref,
    act_ref, hg_ref, sect_ref, cott_ref, oacc_ref,
):
    T, D = width, tok_ref.shape[1]
    FF = up_ref.shape[1]
    H = wo_ref.shape[0] // experts
    EH = experts * H
    z = lax.axis_index("expert")
    g1 = g1_ref[...]
    g2 = g2_ref[...]

    seg = seg_ref[...]
    cut_ref[0] = jnp.broadcast_to(
        jnp.sum((seg < 1).astype(F32), axis=1, keepdims=True), (rows, 128)
    ).astype(jnp.int32)
    cut_ref[1] = jnp.broadcast_to(
        jnp.sum((seg < 2).astype(F32), axis=1, keepdims=True), (rows, 128)
    ).astype(jnp.int32)

    def rows_of(r):
        return pl.ds(pl.multiple_of(r * T, T), T)

    def pick(all_t, route):
        acc = all_t[0:H]
        for e in range(1, experts):
            acc = jnp.where(route == e, all_t[e * H : (e + 1) * H], acc)
        return acc

    def spread(first, second, e0, e1):
        parts = [
            jnp.where(e0 == e, first, jnp.where(e1 == e, second, 0.0)) for e in range(experts)
        ]
        return jnp.concatenate(parts, axis=0).astype(BF)

    def attend(r, _):
        sl = rows_of(r)
        tok = tok_ref[sl, :].astype(F32)
        normed = (tok * inv_rms(tok) * g1).astype(BF)
        q_all = nt(wst_ref[0:EH, :], normed)
        e0, e1 = route_ref[r, 0:1, :], route_ref[r, 1:2, :]
        ga = (gate_ref[r, 0:1, :], gate_ref[r, 1:2, :])
        kv = kv_ref[r]
        kvt = kv.T
        kvt_ref[r] = kvt
        c1, c2 = cut_ref[0, pl.ds(r, 1), :], cut_ref[1, pl.ds(r, 1), :]
        lane = lax.broadcasted_iota(jnp.int32, (seq, 128), 1)
        key_pos = lax.broadcasted_iota(jnp.int32, (seq, 128), 0)
        key_seg = H + (key_pos >= c1).astype(jnp.int32) + (key_pos >= c2).astype(jnp.int32)
        onehot = jnp.where(lane == key_seg, 1.0, 0.0)
        kaug = jnp.where(lane < H, kv.astype(F32), onehot).astype(BF)
        pos = z * T + lax.broadcasted_iota(jnp.int32, (128 - H, T), 1)
        q_seg = (pos >= c1[:, 0:1]).astype(jnp.int32) + (pos >= c2[:, 0:1]).astype(jnp.int32)
        sid = lax.broadcasted_iota(jnp.int32, (128 - H, T), 0)
        bias = jnp.where((sid < 3) & (sid != q_seg), -1e30, 0.0).astype(BF)
        vaug = jnp.concatenate([jnp.ones((16, seq), BF), kvt[H:, :]], axis=0)
        scale = LOG2E / math.sqrt(H)
        mixes = []
        for j, route in enumerate((e0, e1)):
            qt = pick(q_all, route).astype(BF)
            qt_ref[r, j] = qt
            s = nn(kaug, jnp.concatenate([qt, bias], axis=0))
            m = jnp.max(s, axis=0, keepdims=True)
            p = jnp.exp2(s * scale - m * scale).astype(BF)
            p_ref[r, j] = p
            av = nn(vaug, p)
            rinv = 1.0 / av[0:1]
            att = av[16:] * rinv
            rinv_ref[r, j : j + 1, :] = rinv
            att_ref[r, j] = att
            mixes.append(att * ga[j])
        gt = spread(mixes[0], mixes[1], e0, e1)
        gt_ref[r] = gt
        res = tok + nn(gt.T, wo_ref[...])
        res_ref[sl, :] = res
        sec = (res * inv_rms(res) * g2).astype(BF)
        sec_ref[sl, :] = sec
        sect_ref[:, sl] = sec.T
        cott_ref[:, sl] = cot_ref[sl, :].T
        return 0

    lax.fori_loop(0, rows, attend, 0)

    tokens = rows * T
    MB = 512
    for fb in range(FF // fblk):
        fs = pl.ds(fb * fblk, fblk)

        def feed(i, _, fb=fb, fs=fs):
            sl = pl.ds(pl.multiple_of(i * MB, MB), MB)
            h = nn(sec_ref[sl, :], up_ref[:, fs])
            act, slope = gelu_both(h)
            act = act.astype(BF)
            act_ref[sl, :] = act
            hg = (nt(cot_ref[sl, :], dn_ref[fs, :]) * slope).astype(BF)
            hg_ref[sl, :] = hg
            o = nn(act, dn_ref[fs, :])
            s = nt(hg, up_ref[:, fs])
            if fb == 0:
                oacc_ref[sl, :] = res_ref[sl, :] + o
                r_ref[sl, :] = s
            else:
                oacc_ref[sl, :] += o
                r_ref[sl, :] += s
            return 0

        lax.fori_loop(0, tokens // MB, feed, 0)

        def weights(j, _, fb=fb):
            js = pl.ds(pl.multiple_of(j * 256, 256), 256)
            for q in range(fblk // 256):
                qs = pl.ds(q * 256, 256)
                os = pl.ds(fb * fblk + q * 256, 256)
                dup_ref[js, os] = nn(sect_ref[js, :], hg_ref[:, qs]).astype(BF)
                ddn_ref[js, os] = nn(cott_ref[js, :], act_ref[:, qs]).astype(BF)
            return 0

        lax.fori_loop(0, D // 256, weights, 0)

    g2g_ref[...] = jnp.zeros_like(g2g_ref)
    dwo_ref[...] = jnp.zeros_like(dwo_ref)

    def back(r, _):
        sl = rows_of(r)
        out_ref[sl, :] = oacc_ref[sl, :].astype(BF)
        dres, dgain = rms_back(res_ref[sl, :], g2, r_ref[sl, :])
        g2g_ref[...] += fold(dgain)
        rg = cot_ref[sl, :].astype(F32) + dres
        r_ref[sl, :] = rg
        rb = rg.astype(BF)
        dwo_ref[...] += nn(gt_ref[r], rb)
        ag_all = nt(wo_ref[...], rb)
        e0, e1 = route_ref[r, 0:1, :], route_ref[r, 1:2, :]
        ga = (gate_ref[r, 0:1, :], gate_ref[r, 1:2, :])
        kv = kv_ref[r]
        kt = kvt_ref[r, 0:H, :]
        zero = jnp.zeros((H, T), BF)
        kvg = None
        dqs = []
        for j, route in enumerate((e0, e1)):
            rinv = rinv_ref[r, j : j + 1, :]
            da = pick(ag_all, route) * (ga[j] * rinv)
            dd = jnp.sum(da * att_ref[r, j], axis=0, keepdims=True)
            dab = jnp.concatenate([zero, da.astype(BF)], axis=0)
            qb = jnp.concatenate([qt_ref[r, j] * (1.0 / math.sqrt(H)), zero], axis=0).astype(BF)
            p = p_ref[r, j]
            dp = nn(kv, dab)
            ds = (p.astype(F32) * (dp - dd)).astype(BF)
            part = nt(p, dab) + nt(ds, qb)
            kvg = part if kvg is None else kvg + part
            dqs.append(nn(kt, ds) * (1.0 / math.sqrt(H)))
        kvp_ref[r] = kvg.astype(BF)
        qg_ref[r] = spread(dqs[0], dqs[1], e0, e1)
        return 0

    lax.fori_loop(0, rows, back, 0)


def last_kernel(
    experts, rows, width,
    tok_ref, r_ref, qg_ref, kvg_ref, g1_ref, wst_ref,
    tg_ref, g1g_ref, dwst_ref,
):
    T = width
    g1 = g1_ref[...]
    g1g_ref[...] = jnp.zeros_like(g1g_ref)
    dwst_ref[...] = jnp.zeros_like(dwst_ref)

    def step(r, _):
        sl = pl.ds(pl.multiple_of(r * T, T), T)
        tok = tok_ref[sl, :].astype(F32)
        normed = (tok * inv_rms(tok) * g1).astype(BF)
        stack = jnp.concatenate([qg_ref[r], kvg_ref[r].T], axis=0)
        dwst_ref[...] += nn(stack, normed)
        ng = nn(stack.T, wst_ref[...])
        dtok, dgain = rms_back(tok, g1, ng)
        g1g_ref[...] += fold(dgain)
        tg_ref[sl, :] = r_ref[sl, :] + dtok
        return 0

    lax.fori_loop(0, rows, step, 0)


def on_device(
    tokens, segments, routes, gate_values, gain_one, gain_two, kv_weight,
    query_weight, output_weight, up_weight, down_weight, out_grad,
):
    rows, T, D = tokens.shape
    H = query_weight.shape[2]
    experts = lax.axis_size("expert")
    EH = experts * H
    seq = experts * T
    FF = up_weight.shape[1]
    z = lax.axis_index("expert")
    toks = rows * T
    sds = jax.ShapeDtypeStruct

    route = jnp.transpose(lax.dynamic_index_in_dim(routes, z, 0, keepdims=False), (0, 2, 1))
    gate = jnp.transpose(gate_values, (0, 2, 1))
    wq = lax.all_gather(query_weight[0].T, "expert", axis=0, tiled=True)
    wo = lax.all_gather(output_weight[0], "expert", axis=0, tiled=True)
    wst = jnp.concatenate([wq, kv_weight.T], axis=0)
    g1 = gain_one.reshape(1, D)
    g2 = gain_two.reshape(1, D)
    tok2 = tokens.reshape(toks, D)
    tok_f = tok2.astype(F32)
    normed = (tok_f * inv_rms(tok_f) * g1).astype(BF)
    kv = jnp.dot(normed, kv_weight, preferred_element_type=F32).astype(BF)
    kv_all = lax.all_gather(kv.reshape(rows, T, 2 * H), "expert", axis=1, tiled=True)

    fblk = 512
    params = pltpu.CompilerParams(vmem_limit_bytes=VMEM_LIMIT)
    out, rg, qg, kvp, g2g, dwo, dup, ddn = pl.pallas_call(
        functools.partial(main_kernel, experts, rows, T, seq, fblk),
        out_shape=(
            sds((toks, D), BF), sds((toks, D), F32), sds((rows, EH, T), BF),
            sds((rows, seq, 2 * H), BF), sds((8, D), F32), sds((EH, D), F32),
            sds((D, FF), BF), sds((D, FF), BF),
        ),
        scratch_shapes=[
            pltpu.VMEM((2, rows, 128), jnp.int32),
            pltpu.VMEM((rows, 2, seq, T), BF),
            pltpu.VMEM((rows, 2 * H, seq), BF),
            pltpu.VMEM((rows, 2, H, T), BF),
            pltpu.VMEM((rows, 2, H, T), F32),
            pltpu.VMEM((rows, 2, T), F32),
            pltpu.VMEM((rows, EH, T), BF),
            pltpu.VMEM((toks, D), F32),
            pltpu.VMEM((toks, D), BF),
            pltpu.VMEM((toks, fblk), BF),
            pltpu.VMEM((toks, fblk), BF),
            pltpu.VMEM((D, toks), BF),
            pltpu.VMEM((D, toks), BF),
            pltpu.VMEM((toks, D), F32),
        ],
        compiler_params=params,
    )(tok2, out_grad.reshape(toks, D), kv_all, segments, route, gate, g1, g2, wst, wo,
      up_weight, down_weight)

    kvg = lax.psum_scatter(kvp, "expert", scatter_dimension=1, tiled=True)
    dup_all, ddn_all = lax.psum((dup, ddn), ("group", "dp", "expert"))
    tg, g1g, dwst = pl.pallas_call(
        functools.partial(last_kernel, experts, rows, T),
        out_shape=(sds((toks, D), F32), sds((8, D), F32), sds((EH + 2 * H, D), F32)),
        compiler_params=params,
    )(tok2, rg, qg, kvg, g1, wst)

    parts = jnp.concatenate(
        [dwst[:EH].reshape(experts, H, D), dwo.reshape(experts, H, D)], axis=1
    ).astype(BF)
    mine = lax.psum_scatter(parts, "expert", scatter_dimension=0, tiled=True)
    mine = lax.psum(mine, ("group", "dp")).astype(F32)
    small = jnp.concatenate(
        [dwst[EH:], jnp.sum(g1g, axis=0)[None], jnp.sum(g2g, axis=0)[None]], axis=0
    )
    small = lax.psum(small, ("group", "dp", "expert"))
    return (
        out.reshape(tokens.shape),
        tg.reshape(tokens.shape),
        small[2 * H],
        small[2 * H + 1],
        small[: 2 * H].T,
        mine[:, :H].transpose(0, 2, 1),
        mine[:, H:],
        dup_all.astype(F32),
        ddn_all.astype(F32).T,
    )


def solution(mesh):
    rows = P(("group", "dp"), "expert", None)
    in_specs = (
        rows,
        P(("group", "dp"), None),
        P(None, ("group", "dp"), None, None),
        rows,
        P(), P(), P(),
        P("expert", None, None),
        P("expert", None, None),
        P(), P(),
        rows,
    )
    out_specs = (
        rows, rows, P(), P(), P(),
        P("expert", None, None),
        P("expert", None, None),
        P(), P(),
    )
    return jax.shard_map(
        on_device, mesh=mesh, in_specs=in_specs, out_specs=out_specs, check_vma=False
    )
```

```python
import functools
import math

import jax
import jax.numpy as jnp
from jax import lax
from jax.experimental import pallas as pl
from jax.experimental.pallas import tpu as pltpu
from jax.sharding import PartitionSpec as P

EPS = 1e-06
F32 = jnp.float32
BF = jnp.bfloat16
LOG2E = 1.4426950408889634
VMEM_LIMIT = 60 * 2**20


def nn(a, b):
    return lax.dot_general(a, b, (((1,), (0,)), ((), ())), preferred_element_type=F32)


def nt(a, b):
    return lax.dot_general(a, b, (((1,), (1,)), ((), ())), preferred_element_type=F32)


def gelu_both(x):
    c0 = math.sqrt(2.0 / math.pi)
    c1 = 0.044715 * c0
    x2 = x * x
    t = jnp.tanh(x * (c0 + c1 * x2))
    h = 0.5 + 0.5 * t
    act = x * h
    slope = h + (act - act * h) * (2.0 * c0 + (6.0 * c1) * x2)
    return act, slope


def inv_rms(x):
    return lax.rsqrt(jnp.mean(x * x, axis=-1, keepdims=True) + EPS)


def rms_back(x, gain, dy):
    inv = inv_rms(x)
    xn = x * inv
    gdy = gain * dy
    dx = inv * (gdy - xn * jnp.mean(xn * gdy, axis=-1, keepdims=True))
    return dx, dy * xn


def fold(x):
    return jnp.sum(x.reshape(x.shape[0] // 8, 8, x.shape[1]), axis=0)


def remote(src, dst, send, recv, where):
    return pltpu.make_async_remote_copy(
        src_ref=src, dst_ref=dst, send_sem=send, recv_sem=recv,
        device_id=where, device_id_type=pl.DeviceIdType.MESH,
    )


def mega_kernel(
    n, rows, T, FF, fblk,
    tok_ref, cot_hbm, seg_ref, route_ref, gate_ref, g1_ref, g2_ref,
    kvw_ref, wq_in, wo_in, up_hbm, dn_hbm,
    out_ref, tg_ref, g1g_ref, g2g_ref, dwst_ref, dwo_ref, dup_ref, ddn_ref,
    cot_ref, up_ref, dn_ref, nrm_ref, kv_ref, kvp_ref, rcv_ref, wst_ref, wo_ref,
    cut_ref, p_ref, kvt_ref, qt_ref, att_ref, rinv_ref, gt_ref, res_ref, sec_ref,
    sect_ref, cott_ref, oacc_ref, act_ref, hg_ref, qg_ref,
    load_sem, gsend, grecv, wsend, wrecv, rsend, rrecv,
):
    D = tok_ref.shape[1]
    H = wo_in.shape[0]
    EH = n * H
    KV = 2 * H
    seq = n * T
    rg = rows // 2
    half = rg * T
    z = lax.axis_index("expert")
    has_left, has_right = z > 0, z < n - 1
    left, right = {"expert": lax.rem(z + n - 1, n)}, {"expert": lax.rem(z + 1, n)}

    loads = [
        pltpu.make_async_copy(a, b, load_sem.at[i])
        for i, (a, b) in enumerate(((cot_hbm, cot_ref), (up_hbm, up_ref), (dn_hbm, dn_ref)))
    ]
    for c in loads:
        c.start()

    barrier = pltpu.get_barrier_semaphore()
    peers = 0
    for axis in ("group", "dp", "expert"):
        size = lax.axis_size(axis)
        for d in range(1, size):
            pl.semaphore_signal(
                barrier, inc=1, device_id={axis: lax.rem(lax.axis_index(axis) + d, size)},
                device_id_type=pl.DeviceIdType.MESH,
            )
            peers += 1
    pl.semaphore_wait(barrier, peers)

    def rows_of(r):
        return pl.ds(pl.multiple_of(r * T, T), T)

    def block(b, size):
        return pl.ds(pl.multiple_of(b * size, size), size)

    def kv_copy(r, b, slot, where):
        at = kv_ref.at[r, block(b, T)]
        return remote(at, at, gsend.at[r, slot], grecv.at[r, b], where)

    def w_copy(b, slot, where):
        wq_at, wo_at = wst_ref.at[block(b, H)], wo_ref.at[block(b, H)]
        return (
            remote(wq_at, wq_at, wsend.at[0, slot], wrecv.at[0, b], where),
            remote(wo_at, wo_at, wsend.at[1, slot], wrecv.at[1, b], where),
        )

    def pass_on(d, copies):
        @pl.when(z - d >= 0)
        def _():
            for c in copies(z - d, z - d, right):
                c.wait_recv()

            @pl.when(has_right)
            def _():
                for c in copies(z - d, z - d, right):
                    c.start()

        @pl.when(z + d <= n - 1)
        def _():
            for c in copies(z + d, z + d, left):
                c.wait_recv()

            @pl.when(has_left)
            def _():
                for c in copies(z + d, z + d, left):
                    c.start()

    def send_own(copies):
        @pl.when(has_right)
        def _():
            for c in copies(z, z, right):
                c.start()

        @pl.when(has_left)
        def _():
            for c in copies(z, n, left):
                c.start()

    def sent(copies):
        for b in range(n):
            goes = ((b <= z) & has_right) | ((b > z) & has_left)

            @pl.when(goes)
            def _(b=b):
                for c in copies(b, b, right):
                    c.wait_send()

        @pl.when(has_left)
        def _():
            for c in copies(z, n, left):
                c.wait_send()

    def row_copies(r):
        return lambda b, slot, where: (kv_copy(r, b, slot, where),)

    def gather_step(k):
        for d in range(1, n):
            r = k - d + 1

            @pl.when((r >= 0) & (r < rows))
            def _(r=r, d=d):
                pass_on(d, row_copies(r))

    def sum_copy(r, b, slot, where):
        return remote(
            kvp_ref.at[r, block(b, T)], rcv_ref.at[r, slot], rsend.at[r, b], rrecv.at[r, slot], where
        )

    def sum_block(r, b, slot, first):
        @pl.when(jnp.logical_not(first))
        def _():
            sum_copy(r, b, slot, right).wait_recv()
            at = block(b, T)
            kvp_ref[r, at, :] = (
                kvp_ref[r, at, :].astype(F32) + rcv_ref[r, slot].astype(F32)
            ).astype(BF)

    def sum_step(k, lo, hi):
        r1 = k - z + lo

        @pl.when((r1 >= lo) & (r1 < hi))
        def _():
            def go(b, _):
                sum_block(r1, b, b, z == 0)
                sum_copy(r1, b, jnp.where(b == z + 1, b, b), right).start()
                return 0

            lax.fori_loop(z + 1, n, go, 0)

        r2 = k - (n - 1 - z) + lo

        @pl.when((r2 >= lo) & (r2 < hi))
        def _():
            def go(b, _):
                sum_block(r2, b, b, z == n - 1)
                sum_copy(r2, b, jnp.where(b == z - 1, n, b), left).start()
                return 0

            lax.fori_loop(0, z, go, 0)

    def sum_end(r):
        @pl.when(has_left)
        def _():
            sum_block(r, z, z, False)

        @pl.when(has_right)
        def _():
            sum_block(r, z, n, False)

    def sums_sent(r):
        for b in range(n):
            @pl.when(z != b)
            def _(b=b):
                sum_copy(r, b, b, right).wait_send()

    g1 = g1_ref[...]
    g2 = g2_ref[...]
    wst_ref[block(z, H), :] = wq_in[...].astype(F32).T.astype(BF)
    wo_ref[block(z, H), :] = wo_in[...]
    send_own(w_copy)
    wst_ref[EH : EH + KV, :] = kvw_ref[...].astype(F32).T.astype(BF)

    def make_kv(r, _):
        sl = rows_of(r)
        tok = tok_ref[sl, :].astype(F32)
        normed = (tok * inv_rms(tok) * g1).astype(BF)
        nrm_ref[sl, :] = normed
        kv_ref[r, block(z, T), :] = nn(normed, kvw_ref[...]).astype(BF)
        send_own(row_copies(r))
        return 0

    lax.fori_loop(0, rows, make_kv, 0)

    seg = seg_ref[...]
    for i in range(2):
        cut_ref[i] = jnp.broadcast_to(
            jnp.sum((seg < i + 1).astype(F32), axis=1, keepdims=True), (rows, 128)
        ).astype(jnp.int32)
    for ref in (g1g_ref, g2g_ref, dwst_ref, dwo_ref):
        ref[...] = jnp.zeros_like(ref)
    for d in range(1, n):
        pass_on(d, w_copy)
        if d < n - 1:
            gather_step(d - 1)
    loads[0].wait()

    def pick(all_t, route):
        acc = all_t[0:H]
        for e in range(1, n):
            acc = jnp.where(route == e, all_t[e * H : (e + 1) * H], acc)
        return acc

    def spread(first, second, e0, e1):
        parts = [jnp.where(e0 == e, first, jnp.where(e1 == e, second, 0.0)) for e in range(n)]
        return jnp.concatenate(parts, axis=0).astype(BF)

    def attend(i, r):
        sl, gl = rows_of(r), rows_of(i)
        q_all = nt(wst_ref[0:EH, :], nrm_ref[sl, :])
        e0, e1 = route_ref[r, 0:1, :], route_ref[r, 1:2, :]
        ga = (gate_ref[r, 0:1, :], gate_ref[r, 1:2, :])
        kv = kv_ref[r]
        kvt = kv.T
        kvt_ref[i] = kvt
        c1, c2 = cut_ref[0, pl.ds(r, 1), :], cut_ref[1, pl.ds(r, 1), :]
        lane = lax.broadcasted_iota(jnp.int32, (seq, KV), 1)
        key_pos = lax.broadcasted_iota(jnp.int32, (seq, KV), 0)
        key_seg = H + (key_pos >= c1).astype(jnp.int32) + (key_pos >= c2).astype(jnp.int32)
        onehot = jnp.where(lane == key_seg, 1.0, 0.0)
        kaug = jnp.where(lane < H, kv.astype(F32), onehot).astype(BF)
        pos = z * T + lax.broadcasted_iota(jnp.int32, (KV - H, T), 1)
        q_seg = (pos >= c1[:, 0:1]).astype(jnp.int32) + (pos >= c2[:, 0:1]).astype(jnp.int32)
        sid = lax.broadcasted_iota(jnp.int32, (KV - H, T), 0)
        bias = jnp.where((sid < 3) & (sid != q_seg), -1e30, 0.0).astype(BF)
        vaug = jnp.concatenate([jnp.ones((16, seq), BF), kvt[H:, :]], axis=0)
        scale = LOG2E / math.sqrt(H)
        mixes = []
        for j, route in enumerate((e0, e1)):
            qt = pick(q_all, route).astype(BF)
            qt_ref[i, j] = qt
            s = nn(kaug, jnp.concatenate([qt, bias], axis=0))
            m = jnp.max(s, axis=0, keepdims=True)
            p = jnp.exp2(s * scale - m * scale).astype(BF)
            p_ref[i, j] = p
            av = nn(vaug, p)
            rinv = 1.0 / av[0:1]
            att = av[16:] * rinv
            rinv_ref[i, j : j + 1, :] = rinv
            att_ref[i, j] = att
            mixes.append(att * ga[j])
        gt = spread(mixes[0], mixes[1], e0, e1)
        gt_ref[i] = gt
        res = tok_ref[sl, :].astype(F32) + nn(gt.T, wo_ref[...])
        res_ref[gl, :] = res
        sec = (res * inv_rms(res) * g2).astype(BF)
        sec_ref[gl, :] = sec
        sect_ref[:, gl] = sec.T
        cott_ref[:, gl] = cot_ref[sl, :].T

    MB = min(512, half)

    def feed_forward(grp, fb):
        fs = pl.ds(fb * fblk, fblk)

        def feed(i, _):
            sl = pl.ds(pl.multiple_of(i * MB, MB), MB)
            al = pl.ds(pl.multiple_of(grp * half + i * MB, MB), MB)
            h = nn(sec_ref[sl, :], up_ref[:, fs])
            act, slope = gelu_both(h)
            act = act.astype(BF)
            act_ref[sl, :] = act
            hg = (nt(cot_ref[al, :], dn_ref[fs, :]) * slope).astype(BF)
            hg_ref[sl, :] = hg
            o = nn(act, dn_ref[fs, :])
            s = nt(hg, up_ref[:, fs])
            if fb == 0:
                oacc_ref[sl, :] = res_ref[sl, :] + o
                tg_ref[al, :] = s
            else:
                oacc_ref[sl, :] += o
                tg_ref[al, :] += s
            return 0

        lax.fori_loop(0, half // MB, feed, 0)

        def weights(j, _):
            js = pl.ds(pl.multiple_of(j * 256, 256), 256)
            for q in range(fblk // 256):
                qs = pl.ds(q * 256, 256)
                os = pl.ds(fb * fblk + q * 256, 256)
                a = nn(sect_ref[js, :], hg_ref[:, qs])
                b = nn(cott_ref[js, :], act_ref[:, qs])
                if grp > 0:
                    a = a + dup_ref[js, os].astype(F32)
                    b = b + ddn_ref[js, os].astype(F32)
                dup_ref[js, os] = a.astype(BF)
                ddn_ref[js, os] = b.astype(BF)
            return 0

        lax.fori_loop(0, D // 256, weights, 0)

    def back(i, r):
        sl, gl = rows_of(r), rows_of(i)
        out_ref[sl, :] = oacc_ref[gl, :].astype(BF)
        dres, dgain = rms_back(res_ref[gl, :], g2, tg_ref[sl, :])
        g2g_ref[...] += fold(dgain)
        rgrad = cot_ref[sl, :].astype(F32) + dres
        tg_ref[sl, :] = rgrad
        rb = rgrad.astype(BF)
        dwo_ref[...] += nn(gt_ref[i], rb)
        ag_all = nt(wo_ref[...], rb)
        e0, e1 = route_ref[r, 0:1, :], route_ref[r, 1:2, :]
        ga = (gate_ref[r, 0:1, :], gate_ref[r, 1:2, :])
        kv = kv_ref[r]
        kt = kvt_ref[i, 0:H, :]
        zero = jnp.zeros((H, T), BF)
        kvg = None
        dqs = []
        for j, route in enumerate((e0, e1)):
            rinv = rinv_ref[i, j : j + 1, :]
            da = pick(ag_all, route) * (ga[j] * rinv)
            dd = jnp.sum(da * att_ref[i, j], axis=0, keepdims=True)
            dab = jnp.concatenate([zero, da.astype(BF)], axis=0)
            qb = jnp.concatenate([qt_ref[i, j] * (1.0 / math.sqrt(H)), zero], axis=0).astype(BF)
            p = p_ref[i, j]
            dp = nn(kv, dab)
            ds = (p.astype(F32) * (dp - dd)).astype(BF)
            part = nt(p, dab) + nt(ds, qb)
            kvg = part if kvg is None else kvg + part
            dqs.append(nn(kt, ds) * (1.0 / math.sqrt(H)))
        kvp_ref[r] = kvg.astype(BF)
        qg = spread(dqs[0], dqs[1], e0, e1)
        qg_ref[r] = qg
        dwst_ref[0:EH, :] += nn(qg, nrm_ref[sl, :])

    def finish(r):
        sl = rows_of(r)
        sum_end(r)
        tok = tok_ref[sl, :].astype(F32)
        kvgt = kvp_ref[r, block(z, T), :].T
        dwst_ref[EH : EH + KV, :] += nn(kvgt, nrm_ref[sl, :])
        stack = jnp.concatenate([qg_ref[r], kvgt], axis=0)
        dtok, dgain = rms_back(tok, g1, nn(stack.T, wst_ref[...]))
        g1g_ref[...] += fold(dgain)
        tg_ref[sl, :] += dtok

    steps_left = iter(range(rg + n - 2, rows + n - 2))
    per_block = -(-(rows - rg) // (FF // fblk))
    more_sums = -(-(n - 1) // rg)

    for grp in range(2):
        lo, hi = grp * rg, (grp + 1) * rg

        def attend_row(i, _, grp=grp, lo=lo):
            if grp == 0:
                gather_step(i + n - 2)
            attend(i, lo + i)
            if grp == 1:
                for q in range(more_sums):
                    sum_step(rg + i * more_sums + q, 0, rg)
            return 0

        lax.fori_loop(0, rg, attend_row, 0)
        if grp == 0:
            loads[1].wait()
            loads[2].wait()
        for fb in range(FF // fblk):
            feed_forward(grp, fb)
            if grp == 0:
                for _ in range(per_block):
                    k = next(steps_left, None)
                    if k is not None:
                        gather_step(k)

        def back_row(i, _, lo=lo, hi=hi):
            back(i, lo + i)
            sum_step(i, lo, hi)
            return 0

        lax.fori_loop(0, rg, back_row, 0)

    def finish_first(i, _):
        finish(i)
        for q in range(more_sums):
            sum_step(rg + i * more_sums + q, rg, rows)
        return 0

    lax.fori_loop(0, rg, finish_first, 0)

    def finish_second(i, _):
        finish(rg + i)
        return 0

    lax.fori_loop(0, rg, finish_second, 0)

    sent(w_copy)

    def all_sent(r, _):
        sent(row_copies(r))
        sums_sent(r)
        return 0

    lax.fori_loop(0, rows, all_sent, 0)


def on_device(
    tokens, segments, routes, gate_values, gain_one, gain_two, kv_weight,
    query_weight, output_weight, up_weight, down_weight, out_grad,
):
    rows, T, D = tokens.shape
    H = query_weight.shape[2]
    n = lax.axis_size("expert")
    EH = n * H
    KV = 2 * H
    seq = n * T
    FF = up_weight.shape[1]
    z = lax.axis_index("expert")
    toks = rows * T
    rg = rows // 2
    half = rg * T
    fblk = 512
    sds = jax.ShapeDtypeStruct
    vmem = pltpu.VMEM
    dma = pltpu.SemaphoreType.DMA

    route = jnp.transpose(lax.dynamic_index_in_dim(routes, z, 0, keepdims=False), (0, 2, 1))
    gate = jnp.transpose(gate_values, (0, 2, 1))
    whole = pl.BlockSpec(memory_space=pltpu.VMEM)
    hbm = pl.BlockSpec(memory_space=pl.ANY)
    out, tg, g1g, g2g, dwst, dwo, dup, ddn = pl.pallas_call(
        functools.partial(mega_kernel, n, rows, T, FF, fblk),
        out_shape=(
            sds((toks, D), BF), sds((toks, D), F32), sds((8, D), F32), sds((8, D), F32),
            sds((EH + KV, D), F32), sds((EH, D), F32), sds((D, FF), BF), sds((D, FF), BF),
        ),
        in_specs=[whole, hbm] + [whole] * 8 + [hbm, hbm],
        out_specs=[whole] * 8,
        scratch_shapes=[
            vmem((toks, D), BF),
            vmem((D, FF), BF),
            vmem((FF, D), BF),
            vmem((toks, D), BF),
            vmem((rows, seq, KV), BF),
            vmem((rows, seq, KV), BF),
            vmem((rows, n + 1, T, KV), BF),
            vmem((EH + KV, D), BF),
            vmem((EH, D), BF),
            vmem((2, rows, 128), jnp.int32),
            vmem((rg, 2, seq, T), BF),
            vmem((rg, KV, seq), BF),
            vmem((rg, 2, H, T), BF),
            vmem((rg, 2, H, T), F32),
            vmem((rg, 2, T), F32),
            vmem((rg, EH, T), BF),
            vmem((half, D), F32),
            vmem((half, D), BF),
            vmem((D, half), BF),
            vmem((D, half), BF),
            vmem((half, D), F32),
            vmem((half, fblk), BF),
            vmem((half, fblk), BF),
            vmem((rows, EH, T), BF),
            dma((3,)),
            dma((rows, n + 1)),
            dma((rows, n)),
            dma((2, n + 1)),
            dma((2, n)),
            dma((rows, n)),
            dma((rows, n + 1)),
        ],
        compiler_params=pltpu.CompilerParams(
            vmem_limit_bytes=VMEM_LIMIT, collective_id=0, has_side_effects=True
        ),
    )(
        tokens.reshape(toks, D), out_grad.reshape(toks, D), segments, route, gate,
        gain_one.reshape(1, D), gain_two.reshape(1, D), kv_weight, query_weight[0],
        output_weight[0], up_weight, down_weight,
    )
    dup_all, ddn_all = lax.psum((dup, ddn), ("group", "dp", "expert"))
    parts = jnp.concatenate(
        [dwst[:EH].reshape(n, H, D), dwo.reshape(n, H, D)], axis=1
    ).astype(BF)
    mine = lax.psum_scatter(parts, "expert", scatter_dimension=0, tiled=True)
    mine = lax.psum(mine, ("group", "dp")).astype(F32)
    small = jnp.concatenate(
        [dwst[EH:], jnp.sum(g1g, axis=0)[None], jnp.sum(g2g, axis=0)[None]], axis=0
    )
    small = lax.psum(small, ("group", "dp", "expert"))
    return (
        out.reshape(tokens.shape),
        tg.reshape(tokens.shape),
        small[KV],
        small[KV + 1],
        small[:KV].T,
        mine[:, :H].transpose(0, 2, 1),
        mine[:, H:],
        dup_all.astype(F32),
        ddn_all.astype(F32).T,
    )


def solution(mesh):
    rows = P(("group", "dp"), "expert", None)
    in_specs = (
        rows,
        P(("group", "dp"), None),
        P(None, ("group", "dp"), None, None),
        rows,
        P(), P(), P(),
        P("expert", None, None),
        P("expert", None, None),
        P(), P(),
        rows,
    )
    out_specs = (
        rows, rows, P(), P(), P(),
        P("expert", None, None),
        P("expert", None, None),
        P(), P(),
    )
    return jax.shard_map(
        on_device, mesh=mesh, in_specs=in_specs, out_specs=out_specs, check_vma=False
    )
```

```python
import functools
import math

import jax
import jax.numpy as jnp
from jax import lax
from jax.experimental import pallas as pl
from jax.experimental.pallas import tpu as pltpu
from jax.sharding import PartitionSpec as P

EPS = 1e-06
F32 = jnp.float32
BF = jnp.bfloat16
LOG2E = 1.4426950408889634
VMEM_LIMIT = 60 * 2**20


def nn(a, b):
    return lax.dot_general(a, b, (((1,), (0,)), ((), ())), preferred_element_type=F32)


def nt(a, b):
    return lax.dot_general(a, b, (((1,), (1,)), ((), ())), preferred_element_type=F32)


def gelu_both(x):
    c0 = math.sqrt(2.0 / math.pi)
    c1 = 0.044715 * c0
    x2 = x * x
    t = jnp.tanh(x * (c0 + c1 * x2))
    h = 0.5 + 0.5 * t
    act = x * h
    slope = h + (act - act * h) * (2.0 * c0 + (6.0 * c1) * x2)
    return act, slope


def inv_rms(x):
    return lax.rsqrt(jnp.mean(x * x, axis=-1, keepdims=True) + EPS)


def rms_back(x, gain, dy):
    inv = inv_rms(x)
    xn = x * inv
    gdy = gain * dy
    dx = inv * (gdy - xn * jnp.mean(xn * gdy, axis=-1, keepdims=True))
    return dx, dy * xn


def fold(x):
    return jnp.sum(x.reshape(x.shape[0] // 8, 8, x.shape[1]), axis=0)


def remote(src, dst, send, recv, where):
    return pltpu.make_async_remote_copy(
        src_ref=src, dst_ref=dst, send_sem=send, recv_sem=recv,
        device_id=where, device_id_type=pl.DeviceIdType.MESH,
    )


def mega_kernel(
    n, rows, T, FF, fblk,
    tok_ref, cot_hbm, seg_ref, route_ref, gate_ref, g1_ref, g2_ref,
    kvw_ref, wq_in, wo_in, up_hbm, dn_hbm,
    out_hbm, tg_hbm, dup_hbm, ddn_hbm, gain_ref, kvw_out, wq_out, wo_out,
    g2g_ref, dwst_ref, dwo_ref, w_ref, we_ref, wk_ref, rr_ref, rre_ref, rrk_ref,
    ga_ref, gae_ref, gak_ref, ddt_ref, tg_ref, ost_ref,
    cot_ref, up_ref, dn_ref, nrm_ref, kv_ref, kvp_ref, rcv_ref, wst_ref, wo_ref,
    cut_ref, p_ref, kvt_ref, qt_ref, att_ref, rinv_ref, gt_ref, res_ref, sec_ref,
    sect_ref, cott_ref, oacc_ref, act_ref, hg_ref, qg_ref,
    load_sem, gsend, grecv, wsend, wrecv, rsend, rrecv, csend, crecv, out_sem,
    ost_sem, tg_sem,
):
    D = tok_ref.shape[1]
    H = wo_in.shape[0]
    EH = n * H
    KV = 2 * H
    seq = n * T
    rg = rows // 2
    half = rg * T
    z = lax.axis_index("expert")
    has_left, has_right = z > 0, z < n - 1
    left, right = {"expert": lax.rem(z + n - 1, n)}, {"expert": lax.rem(z + 1, n)}

    loads = [
        pltpu.make_async_copy(a, b, load_sem.at[i])
        for i, (a, b) in enumerate(((cot_hbm, cot_ref), (up_hbm, up_ref), (dn_hbm, dn_ref)))
    ]
    for c in loads:
        c.start()

    barrier = pltpu.get_barrier_semaphore()
    peers = 0
    for axis in ("group", "dp", "expert"):
        size = lax.axis_size(axis)
        for d in range(1, size):
            pl.semaphore_signal(
                barrier, inc=1, device_id={axis: lax.rem(lax.axis_index(axis) + d, size)},
                device_id_type=pl.DeviceIdType.MESH,
            )
            peers += 1
    pl.semaphore_wait(barrier, peers)

    def rows_of(r):
        return pl.ds(pl.multiple_of(r * T, T), T)

    def block(b, size):
        return pl.ds(pl.multiple_of(b * size, size), size)

    def kv_copy(r, b, slot, where):
        at = kv_ref.at[r, block(b, T)]
        return remote(at, at, gsend.at[r, slot], grecv.at[r, b], where)

    def w_copy(b, slot, where):
        wq_at, wo_at = wst_ref.at[block(b, H)], wo_ref.at[block(b, H)]
        return (
            remote(wq_at, wq_at, wsend.at[0, slot], wrecv.at[0, b], where),
            remote(wo_at, wo_at, wsend.at[1, slot], wrecv.at[1, b], where),
        )

    def pass_on(d, copies):
        @pl.when(z - d >= 0)
        def _():
            for c in copies(z - d, z - d, right):
                c.wait_recv()

            @pl.when(has_right)
            def _():
                for c in copies(z - d, z - d, right):
                    c.start()

        @pl.when(z + d <= n - 1)
        def _():
            for c in copies(z + d, z + d, left):
                c.wait_recv()

            @pl.when(has_left)
            def _():
                for c in copies(z + d, z + d, left):
                    c.start()

    def send_own(copies):
        @pl.when(has_right)
        def _():
            for c in copies(z, z, right):
                c.start()

        @pl.when(has_left)
        def _():
            for c in copies(z, n, left):
                c.start()

    def sent(copies):
        for b in range(n):
            goes = ((b <= z) & has_right) | ((b > z) & has_left)

            @pl.when(goes)
            def _(b=b):
                for c in copies(b, b, right):
                    c.wait_send()

        @pl.when(has_left)
        def _():
            for c in copies(z, n, left):
                c.wait_send()

    def row_copies(r):
        return lambda b, slot, where: (kv_copy(r, b, slot, where),)

    def gather_step(k):
        for d in range(1, n):
            r = k - d + 1

            @pl.when((r >= 0) & (r < rows))
            def _(r=r, d=d):
                pass_on(d, row_copies(r))

    def sum_copy(r, b, slot, where):
        return remote(
            kvp_ref.at[r, block(b, T)], rcv_ref.at[r, slot], rsend.at[r, b], rrecv.at[r, slot], where
        )

    def sum_block(r, b, slot, first):
        @pl.when(jnp.logical_not(first))
        def _():
            sum_copy(r, b, slot, right).wait_recv()
            at = block(b, T)
            kvp_ref[r, at, :] = (
                kvp_ref[r, at, :].astype(F32) + rcv_ref[r, slot].astype(F32)
            ).astype(BF)

    def sum_step(k, lo, hi):
        r1 = k - z + lo

        @pl.when((r1 >= lo) & (r1 < hi))
        def _():
            def go(b, _):
                sum_block(r1, b, b, z == 0)
                sum_copy(r1, b, jnp.where(b == z + 1, b, b), right).start()
                return 0

            lax.fori_loop(z + 1, n, go, 0)

        r2 = k - (n - 1 - z) + lo

        @pl.when((r2 >= lo) & (r2 < hi))
        def _():
            def go(b, _):
                sum_block(r2, b, b, z == n - 1)
                sum_copy(r2, b, jnp.where(b == z - 1, n, b), left).start()
                return 0

            lax.fori_loop(0, z, go, 0)

    def sum_end(r):
        @pl.when(has_left)
        def _():
            sum_block(r, z, z, False)

        @pl.when(has_right)
        def _():
            sum_block(r, z, n, False)

    def sums_sent(r):
        for b in range(n):
            @pl.when(z != b)
            def _(b=b):
                sum_copy(r, b, b, right).wait_send()

    bits = {
        axis: [(axis, b) for b in range((lax.axis_size(axis) - 1).bit_length())]
        for axis in ("dp", "group", "expert")
    }
    straight = bits["dp"] + bits["group"] + bits["expert"]
    turned = bits["dp"] + bits["group"][::-1] + bits["expert"]

    def bit_of(stage):
        axis, b = stage
        return lax.rem(lax.axis_index(axis) // 2**b, 2)

    def partner_of(stage):
        axis, b = stage
        return {axis: lax.axis_index(axis) + (1 - 2 * bit_of(stage)) * 2**b}

    def chain(number, w, rr, ga, order, collect, done):
        total, deep = w.shape[0], len(order)
        kept = ga.shape[0]

        def start_of(s, size):
            off = 0
            for k in range(s):
                off = off + bit_of(order[k]) * (size >> (k + 1))
            return off

        def part(ref, off, size):
            return ref.at[pl.ds(pl.multiple_of(off, 16), size)]

        def reduce_copy(s):
            size = total >> (s + 1)
            off = start_of(s, total) + (1 - bit_of(order[s])) * size
            return remote(
                part(w, off, size), part(rr, total - 2 * size, size),
                csend.at[number, s], crecv.at[number, s], partner_of(order[s]),
            )

        def collect_copy(s):
            size = kept >> (s + 1)
            at = part(ga, start_of(s + 1, kept), size)
            return remote(
                at, at, csend.at[number, deep + s], crecv.at[number, deep + s], partner_of(order[s])
            )

        def advance(u):
            if 0 < u <= deep:
                s = u - 1
                size = total >> u
                reduce_copy(s).wait_recv()
                mine = pl.ds(pl.multiple_of(start_of(u, total), 16), size)
                added = w[mine, :].astype(F32) + rr[pl.ds(total - 2 * size, size), :].astype(F32)
                if u < deep:
                    w[mine, :] = added.astype(BF)
                else:
                    at = pl.ds(pl.multiple_of(start_of(collect, kept), 16), size)
                    ga[at, :] = added.astype(BF)
            if u < deep:
                reduce_copy(u).start()
            if deep < u <= deep + collect:
                collect_copy(collect - (u - deep)).wait_recv()
            if deep <= u < deep + collect:
                collect_copy(collect - 1 - (u - deep)).start()
            if u == deep + collect:
                done()

        def sent_all():
            for s in range(deep):
                reduce_copy(s).wait_send()
            for s in range(collect):
                collect_copy(s).wait_send()

        return advance, deep + collect, sent_all

    g1 = g1_ref[...]
    g2 = g2_ref[...]
    wst_ref[block(z, H), :] = wq_in[...].astype(F32).T.astype(BF)
    wo_ref[block(z, H), :] = wo_in[...]
    send_own(w_copy)
    wst_ref[EH : EH + KV, :] = kvw_ref[...].astype(F32).T.astype(BF)

    def make_kv(r, _):
        sl = rows_of(r)
        tok = tok_ref[sl, :].astype(F32)
        normed = (tok * inv_rms(tok) * g1).astype(BF)
        nrm_ref[sl, :] = normed
        kv_ref[r, block(z, T), :] = nn(normed, kvw_ref[...]).astype(BF)
        send_own(row_copies(r))
        return 0

    lax.fori_loop(0, rows, make_kv, 0)

    seg = seg_ref[...]
    for i in range(2):
        cut_ref[i] = jnp.broadcast_to(
            jnp.sum((seg < i + 1).astype(F32), axis=1, keepdims=True), (rows, 128)
        ).astype(jnp.int32)
    for ref in (g2g_ref, dwst_ref, dwo_ref, wk_ref):
        ref[...] = jnp.zeros_like(ref)
    for d in range(1, n):
        pass_on(d, w_copy)
        if d < n - 1:
            gather_step(d - 1)
    loads[0].wait()

    def pick(all_t, route):
        acc = all_t[0:H]
        for e in range(1, n):
            acc = jnp.where(route == e, all_t[e * H : (e + 1) * H], acc)
        return acc

    def spread(first, second, e0, e1):
        parts = [jnp.where(e0 == e, first, jnp.where(e1 == e, second, 0.0)) for e in range(n)]
        return jnp.concatenate(parts, axis=0).astype(BF)

    def attend(i, r):
        sl, gl = rows_of(r), rows_of(i)
        q_all = nt(wst_ref[0:EH, :], nrm_ref[sl, :])
        e0, e1 = route_ref[r, 0:1, :], route_ref[r, 1:2, :]
        ga = (gate_ref[r, 0:1, :], gate_ref[r, 1:2, :])
        kv = kv_ref[r]
        kvt = kv.T
        kvt_ref[i] = kvt
        c1, c2 = cut_ref[0, pl.ds(r, 1), :], cut_ref[1, pl.ds(r, 1), :]
        lane = lax.broadcasted_iota(jnp.int32, (seq, KV), 1)
        key_pos = lax.broadcasted_iota(jnp.int32, (seq, KV), 0)
        key_seg = H + (key_pos >= c1).astype(jnp.int32) + (key_pos >= c2).astype(jnp.int32)
        onehot = jnp.where(lane == key_seg, 1.0, 0.0)
        kaug = jnp.where(lane < H, kv.astype(F32), onehot).astype(BF)
        pos = z * T + lax.broadcasted_iota(jnp.int32, (KV - H, T), 1)
        q_seg = (pos >= c1[:, 0:1]).astype(jnp.int32) + (pos >= c2[:, 0:1]).astype(jnp.int32)
        sid = lax.broadcasted_iota(jnp.int32, (KV - H, T), 0)
        bias = jnp.where((sid < 3) & (sid != q_seg), -1e30, 0.0).astype(BF)
        vaug = jnp.concatenate([jnp.ones((16, seq), BF), kvt[H:, :]], axis=0)
        scale = LOG2E / math.sqrt(H)
        mixes = []
        for j, route in enumerate((e0, e1)):
            qt = pick(q_all, route).astype(BF)
            qt_ref[i, j] = qt
            s = nn(kaug, jnp.concatenate([qt, bias], axis=0))
            m = jnp.max(s, axis=0, keepdims=True)
            p = jnp.exp2(s * scale - m * scale).astype(BF)
            p_ref[i, j] = p
            av = nn(vaug, p)
            rinv = 1.0 / av[0:1]
            att = av[16:] * rinv
            rinv_ref[i, j : j + 1, :] = rinv
            att_ref[i, j] = att
            mixes.append(att * ga[j])
        gt = spread(mixes[0], mixes[1], e0, e1)
        gt_ref[i] = gt
        res = tok_ref[sl, :].astype(F32) + nn(gt.T, wo_ref[...])
        res_ref[gl, :] = res
        sec = (res * inv_rms(res) * g2).astype(BF)
        sec_ref[gl, :] = sec
        sect_ref[:, gl] = sec.T
        cott_ref[:, gl] = cot_ref[sl, :].T

    MB = min(512, half)

    def feed_forward(grp, fb):
        fs = pl.ds(fb * fblk, fblk)

        def feed(i, _):
            sl = pl.ds(pl.multiple_of(i * MB, MB), MB)
            al = pl.ds(pl.multiple_of(grp * half + i * MB, MB), MB)
            h = nn(sec_ref[sl, :], up_ref[:, fs])
            act, slope = gelu_both(h)
            act = act.astype(BF)
            act_ref[sl, :] = act
            hg = (nt(cot_ref[al, :], dn_ref[fs, :]) * slope).astype(BF)
            hg_ref[sl, :] = hg
            o = nn(act, dn_ref[fs, :])
            s = nt(hg, up_ref[:, fs])
            if fb == 0:
                oacc_ref[sl, :] = res_ref[sl, :] + o
                tg_ref[al, :] = s
            else:
                oacc_ref[sl, :] += o
                tg_ref[al, :] += s
            return 0

        lax.fori_loop(0, half // MB, feed, 0)
        if grp == 1:
            tick()

        def weights(j, _):
            js = pl.ds(pl.multiple_of(j * 256, 256), 256)
            for q in range(fblk // 256):
                qs = pl.ds(q * 256, 256)
                a = nn(sect_ref[js, :], hg_ref[:, qs])
                b = nn(cott_ref[js, :], act_ref[:, qs])
                for t in range(2):
                    at = pl.ds(pl.multiple_of((2 * q + t) * D + j * 256, 256), 256)
                    for k, v in ((2 * fb, a), (2 * fb + 1, b)):
                        v = v[:, t * 128 : (t + 1) * 128]
                        if grp > 0:
                            v = v + w_ref[k, at, :].astype(F32)
                        w_ref[k, at, :] = v.astype(BF)
            return 0

        lax.fori_loop(0, D // 256, weights, 0)
        if grp == 1:
            tick()

    def out_copy(r):
        slot = lax.rem(r, 2)
        return pltpu.make_async_copy(ost_ref.at[slot], out_hbm.at[rows_of(r)], ost_sem.at[slot])

    def grad_copy(r):
        return pltpu.make_async_copy(tg_ref.at[rows_of(r)], tg_hbm.at[rows_of(r)], tg_sem.at[r])

    def back(i, r):
        sl, gl = rows_of(r), rows_of(i)
        @pl.when(r >= 2)
        def _():
            out_copy(r - 2).wait()

        ost_ref[lax.rem(r, 2)] = oacc_ref[gl, :].astype(BF)
        out_copy(r).start()
        dres, dgain = rms_back(res_ref[gl, :], g2, tg_ref[sl, :])
        g2g_ref[...] += fold(dgain)
        rgrad = cot_ref[sl, :].astype(F32) + dres
        tg_ref[sl, :] = rgrad
        rb = rgrad.astype(BF)
        dwo_ref[...] += nn(gt_ref[i], rb)
        ag_all = nt(wo_ref[...], rb)
        e0, e1 = route_ref[r, 0:1, :], route_ref[r, 1:2, :]
        ga = (gate_ref[r, 0:1, :], gate_ref[r, 1:2, :])
        kv = kv_ref[r]
        kt = kvt_ref[i, 0:H, :]
        zero = jnp.zeros((H, T), BF)
        kvg = None
        dqs = []
        for j, route in enumerate((e0, e1)):
            rinv = rinv_ref[i, j : j + 1, :]
            da = pick(ag_all, route) * (ga[j] * rinv)
            dd = jnp.sum(da * att_ref[i, j], axis=0, keepdims=True)
            dab = jnp.concatenate([zero, da.astype(BF)], axis=0)
            qb = jnp.concatenate([qt_ref[i, j] * (1.0 / math.sqrt(H)), zero], axis=0).astype(BF)
            p = p_ref[i, j]
            dp = nn(kv, dab)
            ds = (p.astype(F32) * (dp - dd)).astype(BF)
            part = nt(p, dab) + nt(ds, qb)
            kvg = part if kvg is None else kvg + part
            dqs.append(nn(kt, ds) * (1.0 / math.sqrt(H)))
        kvp_ref[r] = kvg.astype(BF)
        qg = spread(dqs[0], dqs[1], e0, e1)
        qg_ref[r] = qg
        dwst_ref[0:EH, :] += nn(qg, nrm_ref[sl, :])

    def key_part(r):
        sum_end(r)
        dwst_ref[EH : EH + KV, :] += nn(kvp_ref[r, block(z, T), :].T, nrm_ref[rows_of(r), :])

    def token_part(r):
        sl = rows_of(r)
        tok = tok_ref[sl, :].astype(F32)
        stack = jnp.concatenate([qg_ref[r], kvp_ref[r, block(z, T), :].T], axis=0)
        dtok, _ = rms_back(tok, g1, nn(stack.T, wst_ref[...]))
        tg_ref[sl, :] += dtok
        grad_copy(r).start()

    blocks = FF // fblk
    deep = len(straight)
    outer = len(bits["dp"]) + len(bits["group"])
    pieces = (2 * H // 16) * (D // 128)
    each = pieces >> outer

    def place(p, e):
        turned_e = sum(((e >> k) & 1) << (len(bits["expert"]) - 1 - k) for k in range(len(bits["expert"])))
        return ((p // each * n + turned_e) * each + p % each) * 16

    def put_experts():
        for ref, base in ((dwst_ref, 0), (dwo_ref, H)):
            for e in range(n):
                for g in range(H // 16):
                    tile = ref[e * H + g * 16 : e * H + (g + 1) * 16, :].astype(BF)
                    for q in range(D // 128):
                        at = place((base // 16 + g) * (D // 128) + q, e)
                        we_ref[at : at + 16, :] = tile[:, q * 128 : (q + 1) * 128]

    def experts_done():
        def tile(base, q):
            rows_at = [((base // 16 + g) * (D // 128) + q) * 16 for g in range(H // 16)]
            return jnp.concatenate([gae_ref[a : a + 16, :] for a in rows_at], axis=0).astype(F32)

        for q in range(D // 128):
            wq_out[q * 128 : (q + 1) * 128, :] = tile(0, q).T
            wo_out[:, q * 128 : (q + 1) * 128] = tile(H, q)

    tall = wk_ref.shape[0] // (D // 128)

    def put_keys():
        summed = jnp.sum(wst_ref[...].astype(F32) * dwst_ref[...], axis=0, keepdims=True) / g1
        second_gain = jnp.sum(g2g_ref[...], axis=0, keepdims=True)
        gains = jnp.concatenate([summed, second_gain, jnp.zeros((14, D), F32)], axis=0).astype(BF)
        keys = dwst_ref[EH : EH + KV, :].astype(BF)
        for q in range(D // 128):
            wk_ref[q * tall : q * tall + KV, :] = keys[:, q * 128 : (q + 1) * 128]
            wk_ref[q * tall + KV : q * tall + KV + 16, :] = gains[:, q * 128 : (q + 1) * 128]

    def keys_done():
        for q in range(D // 128):
            lanes = slice(q * 128, (q + 1) * 128)
            kvw_out[lanes, :] = gak_ref[q * tall : q * tall + KV, :].astype(F32).T
            gain_ref[:, lanes] = gak_ref[q * tall + KV : q * tall + KV + 16, :].astype(F32)

    def up_done(fb):
        def go():
            for q in range(fblk // 128):
                pltpu.make_async_copy(
                    ga_ref.at[2 * fb, q * D : (q + 1) * D],
                    dup_hbm.at[:, fb * fblk + q * 128 : fb * fblk + (q + 1) * 128],
                    out_sem.at[fb, q],
                ).start()

        return go

    def up_waits():
        for fb in range(blocks):
            for q in range(fblk // 128):
                pltpu.make_async_copy(
                    ga_ref.at[2 * fb, q * D : (q + 1) * D],
                    dup_hbm.at[:, fb * fblk + q * 128 : fb * fblk + (q + 1) * 128],
                    out_sem.at[fb, q],
                ).wait()

    def down_copy(fb):
        return pltpu.make_async_copy(
            ddt_ref.at[fb % 2], ddn_hbm.at[fb * fblk : (fb + 1) * fblk], out_sem.at[fb, fblk // 128]
        )

    def down_done(fb):
        def go():
            if fb >= 2:
                down_copy(fb - 2).wait()
            for q in range(fblk // 128):
                ddt_ref[fb % 2, q * 128 : (q + 1) * 128, :] = (
                    ga_ref[2 * fb + 1, q * D : (q + 1) * D, :].T
                )
            down_copy(fb).start()

        return go

    chains = []
    for fb in range(blocks):
        chains.append(
            [
                chain(2 * fb, w_ref.at[2 * fb], rr_ref.at[2 * fb], ga_ref.at[2 * fb],
                      straight, deep, up_done(fb)),
                chain(2 * fb + 1, w_ref.at[2 * fb + 1], rr_ref.at[2 * fb + 1],
                      ga_ref.at[2 * fb + 1], turned, deep, down_done(fb)),
            ]
        )
    chains.append([chain(2 * blocks, we_ref, rre_ref, gae_ref, straight, outer, experts_done)])
    chains.append([chain(2 * blocks + 1, wk_ref, rrk_ref, gak_ref, straight, deep, keys_done)])
    at_step = [None] * len(chains)

    def begin(c):
        at_step[c] = 0
        for advance, _, _ in chains[c]:
            advance(0)

    def tick():
        for c, parts in enumerate(chains):
            if at_step[c] is not None and at_step[c] < parts[0][1]:
                at_step[c] += 1
                for advance, _, _ in parts:
                    advance(at_step[c])

    def ticks(i, count):
        for k in range(count):
            @pl.when(i == k)
            def _():
                tick()

    steps_left = iter(range(rg + n - 2, rows + n - 2))
    per_block = -(-(rows - rg) // (FF // fblk))
    more_sums = -(-(n - 1) // rg)

    for grp in range(2):
        lo, hi = grp * rg, (grp + 1) * rg

        def attend_row(i, _, grp=grp, lo=lo):
            if grp == 0:
                gather_step(i + n - 2)
            attend(i, lo + i)
            if grp == 1:
                for q in range(more_sums):
                    sum_step(rg + i * more_sums + q, 0, rg)
            return 0

        lax.fori_loop(0, rg, attend_row, 0)
        if grp == 0:
            loads[1].wait()
            loads[2].wait()
        for fb in range(blocks):
            feed_forward(grp, fb)
            if grp == 0:
                for _ in range(per_block):
                    k = next(steps_left, None)
                    if k is not None:
                        gather_step(k)
            else:
                begin(fb)

        def back_row(i, _, lo=lo, hi=hi, grp=grp):
            back(i, lo + i)
            sum_step(i, lo, hi)
            if grp == 1:
                ticks(i, rg)
            return 0

        lax.fori_loop(0, rg, back_row, 0)

    put_experts()
    begin(blocks)

    def finish_first(i, _):
        key_part(i)
        token_part(i)
        for q in range(more_sums):
            sum_step(rg + i * more_sums + q, rg, rows)
        ticks(i, rg)
        return 0

    lax.fori_loop(0, rg, finish_first, 0)

    def finish_keys(i, _):
        key_part(rg + i)
        return 0

    lax.fori_loop(0, rg, finish_keys, 0)
    put_keys()
    tick()
    begin(blocks + 1)

    def finish_second(i, _):
        token_part(rg + i)
        ticks(i, rg)
        return 0

    lax.fori_loop(0, rg, finish_second, 0)
    while any(at_step[c] < chains[c][0][1] for c in range(len(chains))):
        tick()
    for parts in chains:
        for _, _, sent_all in parts:
            sent_all()
    up_waits()
    for fb in range(max(0, blocks - 2), blocks):
        down_copy(fb).wait()

    out_copy(rows - 2).wait()
    out_copy(rows - 1).wait()
    sent(w_copy)

    def all_sent(r, _):
        sent(row_copies(r))
        sums_sent(r)
        grad_copy(r).wait()
        return 0

    lax.fori_loop(0, rows, all_sent, 0)


def on_device(
    tokens, segments, routes, gate_values, gain_one, gain_two, kv_weight,
    query_weight, output_weight, up_weight, down_weight, out_grad,
):
    rows, T, D = tokens.shape
    H = query_weight.shape[2]
    n = lax.axis_size("expert")
    EH = n * H
    KV = 2 * H
    seq = n * T
    FF = up_weight.shape[1]
    z = lax.axis_index("expert")
    toks = rows * T
    rg = rows // 2
    half = rg * T
    devices = n * lax.axis_size("group") * lax.axis_size("dp")
    fblk = 512 * max(1, devices // 128)
    tall = fblk * D // 128
    tall_e = n * 2 * H * D // 128
    tall_k = 2 * KV * D // 128
    tall_k = max(tall_k, 16 * devices)
    blocks = FF // fblk
    steps = (devices - 1).bit_length()
    sds = jax.ShapeDtypeStruct
    vmem = pltpu.VMEM
    dma = pltpu.SemaphoreType.DMA

    route = jnp.transpose(lax.dynamic_index_in_dim(routes, z, 0, keepdims=False), (0, 2, 1))
    gate = jnp.transpose(gate_values, (0, 2, 1))
    whole = pl.BlockSpec(memory_space=pltpu.VMEM)
    hbm = pl.BlockSpec(memory_space=pl.ANY)
    out, tg, dup, ddn, gains, kvw_grad, wq_grad, wo_grad = pl.pallas_call(
        functools.partial(mega_kernel, n, rows, T, FF, fblk),
        out_shape=(
            sds((toks, D), BF), sds((toks, D), F32), sds((D, FF), BF), sds((FF, D), BF),
            sds((16, D), F32), sds((D, KV), F32), sds((D, H), F32), sds((H, D), F32),
        ),
        in_specs=[whole, hbm] + [whole] * 8 + [hbm, hbm],
        out_specs=[hbm] * 4 + [whole] * 4,
        scratch_shapes=[
            vmem((8, D), F32),
            vmem((EH + KV, D), F32),
            vmem((EH, D), F32),
            vmem((2 * blocks, tall, 128), BF),
            vmem((tall_e, 128), BF),
            vmem((tall_k, 128), BF),
            vmem((2 * blocks, tall, 128), BF),
            vmem((tall_e, 128), BF),
            vmem((tall_k, 128), BF),
            vmem((2 * blocks, tall, 128), BF),
            vmem((tall_e // n, 128), BF),
            vmem((tall_k, 128), BF),
            vmem((2, fblk, D), BF),
            vmem((toks, D), F32),
            vmem((2, T, D), BF),
            vmem((toks, D), BF),
            vmem((D, FF), BF),
            vmem((FF, D), BF),
            vmem((toks, D), BF),
            vmem((rows, seq, KV), BF),
            vmem((rows, seq, KV), BF),
            vmem((rows, n + 1, T, KV), BF),
            vmem((EH + KV, D), BF),
            vmem((EH, D), BF),
            vmem((2, rows, 128), jnp.int32),
            vmem((rg, 2, seq, T), BF),
            vmem((rg, KV, seq), BF),
            vmem((rg, 2, H, T), BF),
            vmem((rg, 2, H, T), F32),
            vmem((rg, 2, T), F32),
            vmem((rg, EH, T), BF),
            vmem((half, D), F32),
            vmem((half, D), BF),
            vmem((D, half), BF),
            vmem((D, half), BF),
            vmem((half, D), F32),
            vmem((half, fblk), BF),
            vmem((half, fblk), BF),
            vmem((rows, EH, T), BF),
            dma((3,)),
            dma((rows, n + 1)),
            dma((rows, n)),
            dma((2, n + 1)),
            dma((2, n)),
            dma((rows, n)),
            dma((rows, n + 1)),
            dma((2 * blocks + 2, 2 * steps)),
            dma((2 * blocks + 2, 2 * steps)),
            dma((blocks, fblk // 128 + 1)),
            dma((2,)),
            dma((rows,)),
        ],
        compiler_params=pltpu.CompilerParams(
            vmem_limit_bytes=VMEM_LIMIT, collective_id=0, has_side_effects=True
        ),
    )(
        tokens.reshape(toks, D), out_grad.reshape(toks, D), segments, route, gate,
        gain_one.reshape(1, D), gain_two.reshape(1, D), kv_weight, query_weight[0],
        output_weight[0], up_weight, down_weight,
    )
    return (
        out.reshape(tokens.shape),
        tg.reshape(tokens.shape),
        gains[0],
        gains[1],
        kvw_grad,
        wq_grad[None],
        wo_grad[None],
        dup.astype(F32),
        ddn.astype(F32),
    )


def solution(mesh):
    rows = P(("group", "dp"), "expert", None)
    in_specs = (
        rows,
        P(("group", "dp"), None),
        P(None, ("group", "dp"), None, None),
        rows,
        P(), P(), P(),
        P("expert", None, None),
        P("expert", None, None),
        P(), P(),
        rows,
    )
    out_specs = (
        rows, rows, P(), P(), P(),
        P("expert", None, None),
        P("expert", None, None),
        P(), P(),
    )
    return jax.shard_map(
        on_device, mesh=mesh, in_specs=in_specs, out_specs=out_specs, check_vma=False
    )
```

```python
import functools
import math

import jax
import jax.numpy as jnp
from jax import lax
from jax.experimental import pallas as pl
from jax.experimental.pallas import tpu as pltpu
from jax.sharding import PartitionSpec as P

EPS = 1e-06
F32 = jnp.float32
BF = jnp.bfloat16
LOG2E = 1.4426950408889634
VMEM_LIMIT = 66_000_000


def nn(a, b):
    return lax.dot_general(a, b, (((1,), (0,)), ((), ())), preferred_element_type=F32)


def nt(a, b):
    return lax.dot_general(a, b, (((1,), (1,)), ((), ())), preferred_element_type=F32)


def gelu_both(x):
    c0 = math.sqrt(2.0 / math.pi)
    c1 = 0.044715 * c0
    x2 = x * x
    t = jnp.tanh(x * (c0 + c1 * x2))
    h = 0.5 + 0.5 * t
    act = x * h
    slope = h + (act - act * h) * (2.0 * c0 + (6.0 * c1) * x2)
    return act, slope


def inv_rms(x):
    return lax.rsqrt(jnp.mean(x * x, axis=-1, keepdims=True) + EPS)


def rms_back(x, gain, dy):
    inv = inv_rms(x)
    xn = x * inv
    gdy = gain * dy
    dx = inv * (gdy - xn * jnp.mean(xn * gdy, axis=-1, keepdims=True))
    return dx, dy * xn


def fold(x):
    return jnp.sum(x.reshape(x.shape[0] // 8, 8, x.shape[1]), axis=0)


def remote(src, dst, send, recv, where):
    return pltpu.make_async_remote_copy(
        src_ref=src, dst_ref=dst, send_sem=send, recv_sem=recv,
        device_id=where, device_id_type=pl.DeviceIdType.MESH,
    )


def mega_kernel(
    n, rows, T, FF, fblk,
    tok_ref, cot_hbm, seg_ref, route_ref, gate_ref, g1_ref, g2_ref,
    kvw_ref, wq_in, wo_in, up_hbm, dn_hbm,
    out_hbm, tg_hbm, dup_hbm, ddn_hbm, gain_ref, kvw_out, wq_out, wo_out,
    g2g_ref, dwst_ref, dwo_ref, w_ref, we_ref, wk_ref, rr_ref, rre_ref, rrk_ref,
    ga_ref, gae_ref, gak_ref, own_ref, tg_ref, ost_ref,
    cot_ref, up_ref, dn_ref, nrm_ref, kv_ref, kvp_ref, rcv_ref, wst_ref, wo_ref,
    cut_ref, p_ref, qt_ref, att_ref, rinv_ref, gt_ref, res_ref, sec_ref,
    sect_ref, cott_ref, oacc_ref, act_ref, hg_ref, qg_ref,
    load_sem, gsend, grecv, rsend, rrecv, csend, crecv, up_sem, down_sem,
    ost_sem, tg_sem,
):
    D = tok_ref.shape[1]
    H = wo_in.shape[0]
    EH = n * H
    KV = 2 * H
    seq = n * T
    groups = (rows // 4, rows // 4, rows // 2)
    z = lax.axis_index("expert")
    has_left, has_right = z > 0, z < n - 1
    left, right = {"expert": lax.rem(z + n - 1, n)}, {"expert": lax.rem(z + 1, n)}

    loads = [
        pltpu.make_async_copy(a, b, load_sem.at[i])
        for i, (a, b) in enumerate(((cot_hbm, cot_ref), (up_hbm, up_ref), (dn_hbm, dn_ref)))
    ]
    for c in loads:
        c.start()

    barrier = pltpu.get_barrier_semaphore()
    peers = 0
    for axis in ("group", "dp", "expert"):
        size = lax.axis_size(axis)
        for d in range(1, size):
            pl.semaphore_signal(
                barrier, inc=1, device_id={axis: lax.rem(lax.axis_index(axis) + d, size)},
                device_id_type=pl.DeviceIdType.MESH,
            )
            peers += 1
    pl.semaphore_wait(barrier, peers)

    def rows_of(r):
        return pl.ds(pl.multiple_of(r * T, T), T)

    def block(b, size):
        return pl.ds(pl.multiple_of(b * size, size), size)

    def kv_copy(r, b, slot, where):
        at = kv_ref.at[r, block(b, T)]
        return remote(at, at, gsend.at[r, slot], grecv.at[r, b], where)

    def pass_on(d, copies):
        @pl.when(z - d >= 0)
        def _():
            for c in copies(z - d, z - d, right):
                c.wait_recv()

            @pl.when(has_right)
            def _():
                for c in copies(z - d, z - d, right):
                    c.start()

        @pl.when(z + d <= n - 1)
        def _():
            for c in copies(z + d, z + d, left):
                c.wait_recv()

            @pl.when(has_left)
            def _():
                for c in copies(z + d, z + d, left):
                    c.start()

    def send_own(copies):
        @pl.when(has_right)
        def _():
            for c in copies(z, z, right):
                c.start()

        @pl.when(has_left)
        def _():
            for c in copies(z, n, left):
                c.start()

    def sent(copies):
        for b in range(n):
            goes = ((b <= z) & has_right) | ((b > z) & has_left)

            @pl.when(goes)
            def _(b=b):
                for c in copies(b, b, right):
                    c.wait_send()

        @pl.when(has_left)
        def _():
            for c in copies(z, n, left):
                c.wait_send()

    def row_copies(r):
        return lambda b, slot, where: (kv_copy(r, b, slot, where),)

    def gather_step(k):
        @pl.when(k + 1 < rows)
        def _():
            send_own(row_copies(k + 1))

        for d in range(1, n):
            r = k - d + 1

            @pl.when((r >= 0) & (r < rows))
            def _(r=r, d=d):
                pass_on(d, row_copies(r))

    def sum_copy(r, b, slot, where):
        return remote(
            kvp_ref.at[r, block(b, T)], rcv_ref.at[r, slot], rsend.at[r, b], rrecv.at[r, slot], where
        )

    def sum_block(r, b, slot, first):
        @pl.when(jnp.logical_not(first))
        def _():
            sum_copy(r, b, slot, right).wait_recv()
            at = block(b, T)
            kvp_ref[r, at, :] = (
                kvp_ref[r, at, :].astype(F32) + rcv_ref[r, slot].astype(F32)
            ).astype(BF)

    def sum_step(k, lo, hi, lag):
        r1 = k - lag * z + lo

        @pl.when((r1 >= lo) & (r1 < hi))
        def _():
            def go(c, _):
                b = n - 1 - c
                sum_block(r1, b, b, z == 0)
                sum_copy(r1, b, b, right).start()
                return 0

            lax.fori_loop(0, n - 1 - z, go, 0)

        r2 = k - lag * (n - 1 - z) + lo

        @pl.when((r2 >= lo) & (r2 < hi))
        def _():
            def go(b, _):
                sum_block(r2, b, b, z == n - 1)
                sum_copy(r2, b, jnp.where(b == z - 1, n, b), left).start()
                return 0

            lax.fori_loop(0, z, go, 0)

    def sum_end(r):
        @pl.when(has_left)
        def _():
            sum_block(r, z, z, False)

        @pl.when(has_right)
        def _():
            sum_block(r, z, n, False)

    def straight_copy(r, b, source):
        return remote(
            kvp_ref.at[r, block(b, T)], rcv_ref.at[r, source], rsend.at[r, b],
            rrecv.at[r, source], {"expert": b},
        )

    def send_straight(r):
        for d in range(1, n):
            straight_copy(r, lax.rem(z + d, n), z).start()

    def end_straight(r):
        at = block(z, T)
        total = kvp_ref[r, at, :].astype(F32)
        for d in range(1, n):
            source = lax.rem(z + d, n)
            straight_copy(r, source, source).wait_recv()
            total = total + rcv_ref[r, source].astype(F32)
        kvp_ref[r, at, :] = total.astype(BF)

    def sums_sent(r):
        for b in range(n):
            @pl.when(z != b)
            def _(b=b):
                sum_copy(r, b, b, right).wait_send()

    def pair(axis, b, wait):
        return (axis, 2**b, 2, wait)

    def line(axis, wait):
        return (axis, 1, lax.axis_size(axis), wait)

    def pairs(axis, waits):
        count = (lax.axis_size(axis) - 1).bit_length()
        return [pair(axis, b, waits[min(b, len(waits) - 1)]) for b in range(count)]

    def digit_of(stage):
        axis, stride, radix, _ = stage
        return lax.rem(lax.axis_index(axis) // stride, radix)

    def peer_of(stage, d):
        axis, stride, radix, _ = stage
        digit = digit_of(stage)
        other = lax.rem(digit + d, radix)
        return other, {axis: lax.axis_index(axis) + (other - digit) * stride}

    def chain(number, w, rr, ga, stages, collect, done):
        deep = len(stages)
        total = w.shape[0] if w is not None else ga.shape[0]
        kept = ga.shape[0]
        sem_at = [0]
        for stage in stages:
            sem_at.append(sem_at[-1] + stage[2] - 1)

        def size_of(s, size):
            for k in range(s):
                size = size // stages[k][2]
            return size

        def start_of(s, size):
            off = 0
            for k in range(s):
                size = size // stages[k][2]
                off = off + digit_of(stages[k]) * size
            return off

        def part(ref, off, size):
            return ref.at[pl.ds(pl.multiple_of(off, 16), size)]

        def slot(s, d):
            return total - size_of(s, total) + (d - 1) * size_of(s + 1, total)

        def reduce_copies(s):
            size = size_of(s + 1, total)
            for d in range(1, stages[s][2]):
                other, where = peer_of(stages[s], d)
                yield remote(
                    part(w, start_of(s, total) + other * size, size), part(rr, slot(s, d), size),
                    csend.at[number, sem_at[s] + d - 1], crecv.at[number, sem_at[s] + d - 1], where,
                )

        def collect_copies(s):
            at = part(ga, start_of(s + 1, kept), size_of(s + 1, kept))
            for d in range(1, stages[s][2]):
                _, where = peer_of(stages[s], d)
                k = sem_at[deep] + sem_at[s] + d - 1
                yield remote(at, at, csend.at[number, k], crecv.at[number, k], where)

        def own_part():
            return pl.ds(pl.multiple_of(start_of(collect, kept), 16), size_of(collect, kept))

        def advance(u, only_send=False):
            if 0 < u <= deep and not only_send:
                s = u - 1
                size = size_of(u, total)
                for c in reduce_copies(s):
                    c.wait_recv()
                mine = pl.ds(pl.multiple_of(start_of(u, total), 16), size)
                added = w[mine, :].astype(F32)
                for d in range(1, stages[s][2]):
                    added = added + rr[pl.ds(slot(s, d), size), :].astype(F32)
                if u < deep:
                    w[mine, :] = added.astype(BF)
                else:
                    ga[own_part(), :] = added.astype(BF)
            if u < deep:
                for c in reduce_copies(u):
                    c.start()
            if deep < u <= deep + collect:
                for c in collect_copies(collect - (u - deep)):
                    c.wait_recv()
            if deep <= u < deep + collect:
                for c in collect_copies(collect - 1 - (u - deep)):
                    c.start()
            if u == deep + collect:
                done()

        def sent_all(reduced=True):
            for s in range(deep if reduced else 0):
                for c in reduce_copies(s):
                    c.wait_send()
            for s in range(collect):
                for c in collect_copies(s):
                    c.wait_send()

        waits = [stage[3] for stage in stages] + [stage[3] for stage in stages[:collect][::-1]] + [0]
        return advance, waits, sent_all, own_part

    core = pairs("dp", (1, 3))
    straight = core + pairs("group", (3, 2)) + [line("expert", 4)]
    turned = core + pairs("group", (2, 3))[::-1] + [line("expert", 4)]
    short = core + [line("group", 3), line("expert", 3)]
    pieces = (2 * H // 16) * (D // 128)
    each = pieces // (lax.axis_size("dp") * lax.axis_size("group"))

    def place(p, e):
        return ((p // each * n + e) * each + p % each) * 16

    g1 = g1_ref[...]
    g2 = g2_ref[...]
    for src, base in ((wq_in, 0), (wo_in, H // 16)):
        for g in range(H // 16):
            for q in range(D // 128):
                at = ((base + g) * (D // 128) + q) * 16
                own_ref[at : at + 16, :] = src[g * 16 : (g + 1) * 16, q * 128 : (q + 1) * 128]
    collect_weights, _, weights_sent, weights_part = chain(
        0, None, None, we_ref, short, len(short), lambda: None
    )
    shard = sum(digit_of(stage) * 2 ** (len(core) - 1 - k) for k, stage in enumerate(core))
    shard = shard * lax.axis_size("group") + lax.axis_index("group")
    we_ref[weights_part(), :] = own_ref[pl.ds(pl.multiple_of(shard * each * 16, 16), each * 16), :]
    collect_weights(len(short), True)
    wst_ref[EH : EH + KV, :] = kvw_ref[...].astype(F32).T.astype(BF)

    def make_kv(r, _):
        sl = rows_of(r)
        tok = tok_ref[sl, :].astype(F32)
        normed = (tok * inv_rms(tok) * g1).astype(BF)
        nrm_ref[sl, :] = normed
        kv_ref[r, block(z, T), :] = nn(normed, kvw_ref[...]).astype(BF)
        return 0

    make_kv(0, 0)
    send_own(row_copies(0))
    lax.fori_loop(1, rows, make_kv, 0)

    seg = seg_ref[...]
    for i in range(2):
        cut_ref[i] = jnp.broadcast_to(
            jnp.sum((seg < i + 1).astype(F32), axis=1, keepdims=True), (rows, 128)
        ).astype(jnp.int32)
    for ref in (g2g_ref, dwst_ref, dwo_ref, wk_ref):
        ref[...] = jnp.zeros_like(ref)
    for k in range(max(n - 2, len(short))):
        if k < n - 2:
            gather_step(k)
        if k < len(short):
            collect_weights(len(short) + k + 1)
    for e in range(n):
        for base, ref in ((0, wst_ref), (H // 16, wo_ref)):
            for g in range(H // 16):
                for q in range(D // 128):
                    at = place((base + g) * (D // 128) + q, e)
                    ref[e * H + g * 16 : e * H + (g + 1) * 16, q * 128 : (q + 1) * 128] = (
                        we_ref[at : at + 16, :]
                    )
    loads[0].wait()

    def pick(all_t, route):
        acc = all_t[0:H]
        for e in range(1, n):
            acc = jnp.where(route == e, all_t[e * H : (e + 1) * H], acc)
        return acc

    def spread(first, second, e0, e1):
        parts = [jnp.where(e0 == e, first, jnp.where(e1 == e, second, 0.0)) for e in range(n)]
        return jnp.concatenate(parts, axis=0).astype(BF)

    def attend(i, r):
        sl, gl = rows_of(r), rows_of(i)
        q_all = nt(wst_ref[0:EH, :], nrm_ref[sl, :])
        e0, e1 = route_ref[z, r, 0:1, :], route_ref[z, r, 1:2, :]
        ga = (gate_ref[r, 0:1, :], gate_ref[r, 1:2, :])
        kv = kv_ref[r]
        kvt = kv.T
        c1, c2 = cut_ref[0, pl.ds(r, 1), :], cut_ref[1, pl.ds(r, 1), :]
        lane = lax.broadcasted_iota(jnp.int32, (seq, KV), 1)
        key_pos = lax.broadcasted_iota(jnp.int32, (seq, KV), 0)
        key_seg = H + (key_pos >= c1).astype(jnp.int32) + (key_pos >= c2).astype(jnp.int32)
        onehot = jnp.where(lane == key_seg, 1.0, 0.0)
        kaug = jnp.where(lane < H, kv.astype(F32), onehot).astype(BF)
        pos = z * T + lax.broadcasted_iota(jnp.int32, (KV - H, T), 1)
        q_seg = (pos >= c1[:, 0:1]).astype(jnp.int32) + (pos >= c2[:, 0:1]).astype(jnp.int32)
        sid = lax.broadcasted_iota(jnp.int32, (KV - H, T), 0)
        bias = jnp.where((sid < 3) & (sid != q_seg), -1e30, 0.0).astype(BF)
        vaug = jnp.concatenate([jnp.ones((16, seq), BF), kvt[H:, :]], axis=0)
        scale = LOG2E / math.sqrt(H)
        mixes = []
        for j, route in enumerate((e0, e1)):
            qt = pick(q_all, route).astype(BF)
            qt_ref[i, j] = qt
            s = nn(kaug, jnp.concatenate([qt, bias], axis=0))
            m = jnp.max(s, axis=0, keepdims=True)
            p = jnp.exp2(s * scale - m * scale).astype(BF)
            p_ref[i, j] = p
            av = nn(vaug, p)
            rinv = 1.0 / av[0:1]
            att = av[16:] * rinv
            rinv_ref[i, j : j + 1, :] = rinv
            att_ref[i, j] = att.astype(BF)
            mixes.append(att * ga[j])
        gt = spread(mixes[0], mixes[1], e0, e1)
        gt_ref[i] = gt
        res = tok_ref[sl, :].astype(F32) + nn(gt.T, wo_ref[...])
        res_ref[gl, :] = res
        sec = (res * inv_rms(res) * g2).astype(BF)
        sec_ref[gl, :] = sec
        sect_ref[:, gl] = sec.T
        cott_ref[:, gl] = cot_ref[sl, :].T

    def feed_forward(grp, fb):
        half = groups[grp] * T
        base = sum(groups[:grp]) * T
        MB = min(512, half)
        fs = pl.ds(fb * fblk, fblk)

        def feed(i, _):
            sl = pl.ds(pl.multiple_of(i * MB, MB), MB)
            al = pl.ds(pl.multiple_of(base + i * MB, T), MB)
            h = nn(sec_ref[sl, :], up_ref[:, fs])
            act, slope = gelu_both(h)
            act = act.astype(BF)
            act_ref[sl, :] = act
            hg = (nt(cot_ref[al, :], dn_ref[fs, :]) * slope).astype(BF)
            hg_ref[sl, :] = hg
            o = nn(act, dn_ref[fs, :])
            s = nt(hg, up_ref[:, fs])
            if fb == 0:
                oacc_ref[sl, :] = res_ref[sl, :] + o
                tg_ref[al, :] = s
            else:
                oacc_ref[sl, :] += o
                tg_ref[al, :] += s
            sites(i, half // MB)
            return 0

        lax.fori_loop(0, half // MB, feed, 0)

        a = nn(sect_ref[:, 0:half], hg_ref[0:half, :])
        b = nn(cott_ref[:, 0:half], act_ref[0:half, :])
        for t in range(fblk // 128):
            at = slice(t * D, (t + 1) * D)
            for k, v in ((2 * fb, a), (2 * fb + 1, b)):
                v = v[:, t * 128 : (t + 1) * 128]
                if grp > 0:
                    v = v + w_ref[k, at, :].astype(F32)
                w_ref[k, at, :] = v.astype(BF)
        site()

    def out_copy(r):
        slot = lax.rem(r, 2)
        return pltpu.make_async_copy(ost_ref.at[slot], out_hbm.at[rows_of(r)], ost_sem.at[slot])

    def grad_copy(r):
        return pltpu.make_async_copy(tg_ref.at[rows_of(r)], tg_hbm.at[rows_of(r)], tg_sem.at[r])

    def back(i, r):
        sl, gl = rows_of(r), rows_of(i)
        @pl.when(r >= 2)
        def _():
            out_copy(r - 2).wait()

        ost_ref[lax.rem(r, 2)] = oacc_ref[gl, :].astype(BF)
        out_copy(r).start()
        dres, dgain = rms_back(res_ref[gl, :], g2, tg_ref[sl, :])
        g2g_ref[...] += fold(dgain)
        rgrad = cot_ref[sl, :].astype(F32) + dres
        tg_ref[sl, :] = rgrad
        rb = rgrad.astype(BF)
        dwo_ref[...] += nn(gt_ref[i], rb)
        ag_all = nt(wo_ref[...], rb)
        e0, e1 = route_ref[z, r, 0:1, :], route_ref[z, r, 1:2, :]
        ga = (gate_ref[r, 0:1, :], gate_ref[r, 1:2, :])
        kv = kv_ref[r]
        kt = kv.T[0:H, :]
        zero = jnp.zeros((H, T), BF)
        kvg = None
        dqs = []
        for j, route in enumerate((e0, e1)):
            rinv = rinv_ref[i, j : j + 1, :]
            da = pick(ag_all, route) * (ga[j] * rinv)
            dd = jnp.sum(da * att_ref[i, j].astype(F32), axis=0, keepdims=True)
            dab = jnp.concatenate([zero, da.astype(BF)], axis=0)
            qb = jnp.concatenate([qt_ref[i, j] * (1.0 / math.sqrt(H)), zero], axis=0).astype(BF)
            p = p_ref[i, j]
            dp = nn(kv, dab)
            ds = (p.astype(F32) * (dp - dd)).astype(BF)
            part = nt(p, dab) + nt(ds, qb)
            kvg = part if kvg is None else kvg + part
            dqs.append(nn(kt, ds) * (1.0 / math.sqrt(H)))
        kvp_ref[r] = kvg.astype(BF)
        qg = spread(dqs[0], dqs[1], e0, e1)
        qg_ref[r] = qg
        dwst_ref[0:EH, :] += nn(qg, nrm_ref[sl, :])

    def key_part(r, direct=False):
        if direct:
            end_straight(r)
        else:
            sum_end(r)
        dwst_ref[EH : EH + KV, :] += nn(kvp_ref[r, block(z, T), :].T, nrm_ref[rows_of(r), :])

    def token_part(r):
        sl = rows_of(r)
        tok = tok_ref[sl, :].astype(F32)
        stack = jnp.concatenate([qg_ref[r], kvp_ref[r, block(z, T), :].T], axis=0)
        dtok, _ = rms_back(tok, g1, nn(stack.T, wst_ref[...]))
        tg_ref[sl, :] += dtok
        grad_copy(r).start()

    blocks = FF // fblk

    def put_experts():
        for ref, base in ((dwst_ref, 0), (dwo_ref, H)):
            for e in range(n):
                for g in range(H // 16):
                    tile = ref[e * H + g * 16 : e * H + (g + 1) * 16, :].astype(BF)
                    for q in range(D // 128):
                        at = place((base // 16 + g) * (D // 128) + q, e)
                        we_ref[at : at + 16, :] = tile[:, q * 128 : (q + 1) * 128]

    def experts_done():
        def tile(base, q):
            rows_at = [((base // 16 + g) * (D // 128) + q) * 16 for g in range(H // 16)]
            return jnp.concatenate([gae_ref[a : a + 16, :] for a in rows_at], axis=0).astype(F32)

        for q in range(D // 128):
            wq_out[:, q * 128 : (q + 1) * 128] = tile(0, q)
            wo_out[:, q * 128 : (q + 1) * 128] = tile(H, q)

    tall = wk_ref.shape[0] // (D // 128)

    def put_keys():
        summed = jnp.sum(wst_ref[...].astype(F32) * dwst_ref[...], axis=0, keepdims=True) / g1
        second_gain = jnp.sum(g2g_ref[...], axis=0, keepdims=True)
        gains = jnp.concatenate([summed, second_gain, jnp.zeros((14, D), F32)], axis=0).astype(BF)
        keys = dwst_ref[EH : EH + KV, :].astype(BF)
        for q in range(D // 128):
            wk_ref[q * tall : q * tall + KV, :] = keys[:, q * 128 : (q + 1) * 128]
            wk_ref[q * tall + KV : q * tall + KV + 16, :] = gains[:, q * 128 : (q + 1) * 128]

    def keys_done():
        for q in range(D // 128):
            lanes = slice(q * 128, (q + 1) * 128)
            kvw_out[lanes, :] = gak_ref[q * tall : q * tall + KV, :].astype(F32).T
            gain_ref[:, lanes] = gak_ref[q * tall + KV : q * tall + KV + 16, :].astype(F32)

    tiles = fblk // 128

    def up_copies(fb):
        for q in range(tiles):
            at = fb * fblk + q * 128
            yield pltpu.make_async_copy(
                ga_ref.at[2 * fb, q * D : (q + 1) * D], dup_hbm.at[:, at : at + 128], up_sem.at[fb, q]
            )

    def down_copy(fb):
        at = pl.ds(fb * fblk, fblk)
        return pltpu.make_async_copy(dn_ref.at[at], ddn_hbm.at[at], down_sem.at[fb])

    def up_done(fb):
        def go():
            for c in up_copies(fb):
                c.start()

        return go

    def down_done(fb):
        def go():
            for q in range(tiles):
                at = fb * fblk + q * 128
                dn_ref[at : at + 128, :] = ga_ref[2 * fb + 1, q * D : (q + 1) * D, :].T
            down_copy(fb).start()

        return go

    chains = []
    for fb in range(blocks):
        chains.append(
            [
                chain(2 * fb + 1, w_ref.at[2 * fb], rr_ref.at[2 * fb], ga_ref.at[2 * fb],
                      straight, len(straight), up_done(fb)),
                chain(2 * fb + 2, w_ref.at[2 * fb + 1], rr_ref.at[2 * fb + 1],
                      ga_ref.at[2 * fb + 1], turned, len(turned), down_done(fb)),
            ]
        )
    chains.append(
        [chain(2 * blocks + 1, we_ref, rre_ref, gae_ref, short, len(short) - 1, experts_done)]
    )
    chains.append([chain(2 * blocks + 2, wk_ref, rrk_ref, gak_ref, short, len(short), keys_done)])
    at_step = [None] * len(chains)
    count_down = [0] * len(chains)
    gathers, sums, pace = [], [], [0]

    def begin(c):
        at_step[c] = 0
        count_down[c] = chains[c][0][1][0]
        for one in chains[c]:
            one[0](0)

    def under_way(c):
        return at_step[c] is not None and at_step[c] < len(chains[c][0][1]) - 1

    def tick(weight):
        for c in range(len(chains)):
            if under_way(c):
                count_down[c] -= weight
                if count_down[c] <= 0:
                    at_step[c] += 1
                    count_down[c] = chains[c][0][1][at_step[c]]
                    for one in chains[c]:
                        one[0](at_step[c])

    def site(weight=1, adds=1):
        pace[0] += weight
        if gathers and pace[0] >= 4:
            pace[0] = 0
            gather_step(gathers.pop(0))
        for _ in range(adds):
            if sums:
                sum_step(*sums.pop(0))
        tick(weight)

    def sites(i, count, weight=1, adds=1):
        for k in range(count):
            @pl.when(i == k)
            def _():
                site(weight, adds)

    gathers += range(groups[0] + n - 2, rows + n - 2)

    for grp, rg in enumerate(groups):
        lo = sum(groups[:grp])
        hi = lo + rg

        while gathers and grp > 0 and gathers[0] <= hi + n - 3:
            gather_step(gathers.pop(0))

        def attend_row(i, _, grp=grp, lo=lo, rg=rg):
            if grp == 0:
                gather_step(i + n - 2)
            attend(i, lo + i)
            if grp > 0:
                sites(i, rg)
            return 0

        lax.fori_loop(0, rg, attend_row, 0)
        if grp == 0:
            loads[1].wait()
            loads[2].wait()
        for fb in range(blocks):
            feed_forward(grp, fb)
            if grp == len(groups) - 1:
                begin(fb)

        while sums:
            sum_step(*sums.pop(0))
        final = grp == len(groups) - 1
        top = hi - rg // 2 if final else hi
        lag = 2 if final else 4

        def back_row(i, _, lo=lo, rg=rg, top=top, lag=lag, final=final):
            back(i, lo + i)
            sum_step(i, lo, top, lag)
            if final:
                @pl.when(lo + i >= top)
                def _():
                    send_straight(lo + i)

            sites(i, rg, 2)
            return 0

        lax.fori_loop(0, rg, back_row, 0)
        sums += [(k, lo, top, lag) for k in range(rg, top - lo + lag * (n - 1))]

    weights_sent(False)
    put_experts()
    begin(blocks)
    early = rows - groups[-1]

    adds = -(-len(sums) // early)

    def finish_first(i, _):
        key_part(i)
        token_part(i)
        sites(i, early, 1, adds)
        return 0

    lax.fori_loop(0, early, finish_first, 0)

    def finish_keys(r, _):
        key_part(r)
        return 0

    def finish_straight(r, _):
        key_part(r, True)
        return 0

    lax.fori_loop(early, top, finish_keys, 0)
    lax.fori_loop(top, rows, finish_straight, 0)
    put_keys()
    begin(blocks + 1)
    site()

    def finish_second(i, _):
        token_part(early + i)
        sites(i, rows - early)
        return 0

    lax.fori_loop(0, rows - early, finish_second, 0)
    while any(under_way(c) for c in range(len(chains))):
        tick(1)
    for parts in chains:
        for one in parts:
            one[2]()
    for fb in range(blocks):
        for c in up_copies(fb):
            c.wait()
        down_copy(fb).wait()

    out_copy(rows - 2).wait()
    out_copy(rows - 1).wait()
    def all_sent(r, _):
        sent(row_copies(r))
        sums_sent(r)
        grad_copy(r).wait()
        return 0

    lax.fori_loop(0, rows, all_sent, 0)


def on_device(
    tokens, segments, routes, gate_values, gain_one, gain_two, kv_weight,
    query_weight, output_weight, up_weight, down_weight, out_grad,
):
    rows, T, D = tokens.shape
    H = query_weight.shape[2]
    n = lax.axis_size("expert")
    EH = n * H
    KV = 2 * H
    seq = n * T
    FF = up_weight.shape[1]
    toks = rows * T
    rg = rows // 2
    half = rg * T
    devices = n * lax.axis_size("group") * lax.axis_size("dp")
    fblk = 512 * max(1, devices // 128)
    tall = fblk * D // 128
    tall_e = n * 2 * H * D // 128
    tall_k = 2 * KV * D // 128
    tall_k = max(tall_k, 16 * devices)
    blocks = FF // fblk
    steps = (devices // n - 1).bit_length() + lax.axis_size("group") + n
    sds = jax.ShapeDtypeStruct
    vmem = pltpu.VMEM
    dma = pltpu.SemaphoreType.DMA

    route = jnp.transpose(routes, (0, 1, 3, 2))
    gate = jnp.transpose(gate_values, (0, 2, 1))
    whole = pl.BlockSpec(memory_space=pltpu.VMEM)
    hbm = pl.BlockSpec(memory_space=pl.ANY)
    out, tg, dup, ddn, gains, kvw_grad, wq_grad, wo_grad = pl.pallas_call(
        functools.partial(mega_kernel, n, rows, T, FF, fblk),
        out_shape=(
            sds((toks, D), BF), sds((toks, D), F32), sds((D, FF), BF), sds((FF, D), BF),
            sds((16, D), F32), sds((D, KV), F32), sds((H, D), F32), sds((H, D), F32),
        ),
        in_specs=[whole, hbm] + [whole] * 8 + [hbm, hbm],
        out_specs=[hbm] * 4 + [whole] * 4,
        scratch_shapes=[
            vmem((8, D), F32),
            vmem((EH + KV, D), F32),
            vmem((EH, D), F32),
            vmem((2 * blocks, tall, 128), BF),
            vmem((tall_e, 128), BF),
            vmem((tall_k, 128), BF),
            vmem((2 * blocks, tall, 128), BF),
            vmem((tall_e, 128), BF),
            vmem((tall_k, 128), BF),
            vmem((2 * blocks, tall, 128), BF),
            vmem((tall_e // n, 128), BF),
            vmem((tall_k, 128), BF),
            vmem((tall_e // n, 128), BF),
            vmem((toks, D), F32),
            vmem((2, T, D), BF),
            vmem((toks, D), BF),
            vmem((D, FF), BF),
            vmem((FF, D), BF),
            vmem((toks, D), BF),
            vmem((rows, seq, KV), BF),
            vmem((rows, seq, KV), BF),
            vmem((rows, n + 1, T, KV), BF),
            vmem((EH + KV, D), BF),
            vmem((EH, D), BF),
            vmem((2, rows, 128), jnp.int32),
            vmem((rg, 2, seq, T), BF),
            vmem((rg, 2, H, T), BF),
            vmem((rg, 2, H, T), BF),
            vmem((rg, 2, T), F32),
            vmem((rg, EH, T), BF),
            vmem((half, D), F32),
            vmem((half, D), BF),
            vmem((D, half), BF),
            vmem((D, half), BF),
            vmem((half, D), F32),
            vmem((half, fblk), BF),
            vmem((half, fblk), BF),
            vmem((rows, EH, T), BF),
            dma((3,)),
            dma((rows, n + 1)),
            dma((rows, n)),
            dma((rows, n)),
            dma((rows, n + 1)),
            dma((2 * blocks + 3, 2 * steps)),
            dma((2 * blocks + 3, 2 * steps)),
            dma((blocks, fblk // 128)),
            dma((blocks,)),
            dma((2,)),
            dma((rows,)),
        ],
        compiler_params=pltpu.CompilerParams(
            vmem_limit_bytes=VMEM_LIMIT, collective_id=0, has_side_effects=True
        ),
    )(
        tokens.reshape(toks, D), out_grad.reshape(toks, D), segments, route, gate,
        gain_one.reshape(1, D), gain_two.reshape(1, D), kv_weight, query_weight[0].T,
        output_weight[0], up_weight, down_weight,
    )
    return (
        out.reshape(tokens.shape),
        tg.reshape(tokens.shape),
        gains[0],
        gains[1],
        kvw_grad,
        wq_grad.T[None],
        wo_grad[None],
        dup.astype(F32),
        ddn.astype(F32),
    )


def solution(mesh):
    rows = P(("group", "dp"), "expert", None)
    in_specs = (
        rows,
        P(("group", "dp"), None),
        P(None, ("group", "dp"), None, None),
        rows,
        P(), P(), P(),
        P("expert", None, None),
        P("expert", None, None),
        P(), P(),
        rows,
    )
    out_specs = (
        rows, rows, P(), P(), P(),
        P("expert", None, None),
        P("expert", None, None),
        P(), P(),
    )
    return jax.shard_map(
        on_device, mesh=mesh, in_specs=in_specs, out_specs=out_specs, check_vma=False
    )
```

```python
import functools
import math

import jax
import jax.numpy as jnp
from jax import lax
from jax.experimental import pallas as pl
from jax.experimental.pallas import tpu as pltpu
from jax.sharding import PartitionSpec as P

EPS = 1e-06
F32 = jnp.float32
BF = jnp.bfloat16
LOG2E = 1.4426950408889634
VMEM_LIMIT = 66_000_000


def nn(a, b):
    return lax.dot_general(a, b, (((1,), (0,)), ((), ())), preferred_element_type=F32)


def nt(a, b):
    return lax.dot_general(a, b, (((1,), (1,)), ((), ())), preferred_element_type=F32)


def gelu_both(x):
    c0 = math.sqrt(2.0 / math.pi)
    c1 = 0.044715 * c0
    x2 = x * x
    t = jnp.tanh(x * (c0 + c1 * x2))
    h = 0.5 + 0.5 * t
    act = x * h
    slope = h + (act - act * h) * (2.0 * c0 + (6.0 * c1) * x2)
    return act, slope


def inv_rms(x):
    return lax.rsqrt(jnp.mean(x * x, axis=-1, keepdims=True) + EPS)


def rms_back(x, gain, dy):
    inv = inv_rms(x)
    xn = x * inv
    gdy = gain * dy
    dx = inv * (gdy - xn * jnp.mean(xn * gdy, axis=-1, keepdims=True))
    return dx, dy * xn


def fold(x):
    return jnp.sum(x.reshape(x.shape[0] // 8, 8, x.shape[1]), axis=0)


def remote(src, dst, send, recv, where):
    return pltpu.make_async_remote_copy(
        src_ref=src, dst_ref=dst, send_sem=send, recv_sem=recv,
        device_id=where, device_id_type=pl.DeviceIdType.MESH,
    )


def mega_kernel(
    n, rows, T, FF, fblk,
    tok_ref, cot_hbm, seg_ref, route_ref, gate_ref, g1_ref, g2_ref,
    kvw_ref, wq_in, wo_in, up_hbm, dn_hbm,
    out_hbm, tg_hbm, dup_hbm, ddn_hbm, gain_ref, kvw_out, wq_out, wo_out,
    g2g_ref, dwst_ref, dwo_ref, w_ref, we_ref, wk_ref, rr_ref, rre_ref, rrk_ref,
    ga_ref, gae_ref, gak_ref, own_ref, tg_ref, ost_ref,
    cot_ref, up_ref, dn_ref, nrm_ref, kv_ref, kvp_ref, rcv_ref, wst_ref, wo_ref,
    cut_ref, p_ref, qt_ref, att_ref, rinv_ref, gt_ref, res_ref, sec_ref,
    sect_ref, cott_ref, oacc_ref, act_ref, hg_ref, qg_ref,
    load_sem, gsend, grecv, rsend, rrecv, csend, crecv, done_sem,
    ost_sem, tg_sem,
):
    D = tok_ref.shape[1]
    H = wo_in.shape[0]
    EH = n * H
    KV = 2 * H
    seq = n * T
    groups = (rows // 4, rows // 4, rows // 2)
    z = lax.axis_index("expert")
    has_left, has_right = z > 0, z < n - 1
    left, right = {"expert": lax.rem(z + n - 1, n)}, {"expert": lax.rem(z + 1, n)}

    loads = [
        pltpu.make_async_copy(a, b, load_sem.at[i])
        for i, (a, b) in enumerate(((cot_hbm, cot_ref), (up_hbm, up_ref), (dn_hbm, dn_ref)))
    ]
    for c in loads:
        c.start()

    barrier = pltpu.get_barrier_semaphore()
    peers = 0
    for axis in ("group", "dp", "expert"):
        size = lax.axis_size(axis)
        for d in range(1, size):
            pl.semaphore_signal(
                barrier, inc=1, device_id={axis: lax.rem(lax.axis_index(axis) + d, size)},
                device_id_type=pl.DeviceIdType.MESH,
            )
            peers += 1
    pl.semaphore_wait(barrier, peers)

    def rows_of(r):
        return pl.ds(pl.multiple_of(r * T, T), T)

    def block(b, size):
        return pl.ds(pl.multiple_of(b * size, size), size)

    def kv_copy(r, b, slot, where):
        at = kv_ref.at[r, block(b, T)]
        return remote(at, at, gsend.at[r, slot], grecv.at[r, b], where)

    def pass_on(d, copies):
        @pl.when(z - d >= 0)
        def _():
            for c in copies(z - d, z - d, right):
                c.wait_recv()

            @pl.when(has_right)
            def _():
                for c in copies(z - d, z - d, right):
                    c.start()

        @pl.when(z + d <= n - 1)
        def _():
            for c in copies(z + d, z + d, left):
                c.wait_recv()

            @pl.when(has_left)
            def _():
                for c in copies(z + d, z + d, left):
                    c.start()

    def send_own(copies):
        @pl.when(has_right)
        def _():
            for c in copies(z, z, right):
                c.start()

        @pl.when(has_left)
        def _():
            for c in copies(z, n, left):
                c.start()

    def sent(copies):
        for b in range(n):
            goes = ((b <= z) & has_right) | ((b > z) & has_left)

            @pl.when(goes)
            def _(b=b):
                for c in copies(b, b, right):
                    c.wait_send()

        @pl.when(has_left)
        def _():
            for c in copies(z, n, left):
                c.wait_send()

    def row_copies(r):
        return lambda b, slot, where: (kv_copy(r, b, slot, where),)

    def gather_step(k):
        @pl.when(k + 1 < rows)
        def _():
            send_own(row_copies(k + 1))

        for d in range(1, n):
            r = k - d + 1

            @pl.when((r >= 0) & (r < rows))
            def _(r=r, d=d):
                pass_on(d, row_copies(r))

    def sum_copy(r, b, slot, where):
        return remote(
            kvp_ref.at[r, block(b, T)], rcv_ref.at[r, slot], rsend.at[r, b], rrecv.at[r, slot], where
        )

    def sum_block(r, b, slot, first):
        @pl.when(jnp.logical_not(first))
        def _():
            sum_copy(r, b, slot, right).wait_recv()
            at = block(b, T)
            kvp_ref[r, at, :] = (
                kvp_ref[r, at, :].astype(F32) + rcv_ref[r, slot].astype(F32)
            ).astype(BF)

    def sum_step(k, lo, hi, lag):
        r1 = k - lag * z + lo

        @pl.when((r1 >= lo) & (r1 < hi))
        def _():
            def go(c, _):
                b = n - 1 - c
                sum_block(r1, b, b, z == 0)
                sum_copy(r1, b, b, right).start()
                return 0

            lax.fori_loop(0, n - 1 - z, go, 0)

        r2 = k - lag * (n - 1 - z) + lo

        @pl.when((r2 >= lo) & (r2 < hi))
        def _():
            def go(b, _):
                sum_block(r2, b, b, z == n - 1)
                sum_copy(r2, b, jnp.where(b == z - 1, n, b), left).start()
                return 0

            lax.fori_loop(0, z, go, 0)

    def sum_end(r):
        @pl.when(has_left)
        def _():
            sum_block(r, z, z, False)

        @pl.when(has_right)
        def _():
            sum_block(r, z, n, False)

    def straight_copy(r, b, source):
        return remote(
            kvp_ref.at[r, block(b, T)], rcv_ref.at[r, source], rsend.at[r, b],
            rrecv.at[r, source], {"expert": b},
        )

    def send_straight(r):
        for d in range(1, n):
            straight_copy(r, lax.rem(z + d, n), z).start()

    def end_straight(r):
        at = block(z, T)
        total = kvp_ref[r, at, :].astype(F32)
        for d in range(1, n):
            source = lax.rem(z + d, n)
            straight_copy(r, source, source).wait_recv()
            total = total + rcv_ref[r, source].astype(F32)
        kvp_ref[r, at, :] = total.astype(BF)

    def sums_sent(r):
        for b in range(n):
            @pl.when(z != b)
            def _(b=b):
                sum_copy(r, b, b, right).wait_send()

    def pair(axis, b, wait):
        return (axis, 2**b, 2, wait)

    def line(axis, wait):
        return (axis, 1, lax.axis_size(axis), wait)

    def pairs(axis, waits):
        count = (lax.axis_size(axis) - 1).bit_length()
        return [pair(axis, b, waits[min(b, len(waits) - 1)]) for b in range(count)]

    def digit_of(stage):
        axis, stride, radix, _ = stage
        return lax.rem(lax.axis_index(axis) // stride, radix)

    def peer_of(stage, d):
        axis, stride, radix, _ = stage
        digit = digit_of(stage)
        other = lax.rem(digit + d, radix)
        return other, {axis: lax.axis_index(axis) + (other - digit) * stride}

    def chain(number, w, rr, ga, stages, collect, done):
        deep = len(stages)
        total = w.shape[0] if w is not None else ga.shape[0]
        kept = ga.shape[0]
        sem_at = [0]
        for stage in stages:
            sem_at.append(sem_at[-1] + stage[2] - 1)

        def size_of(s, size):
            for k in range(s):
                size = size // stages[k][2]
            return size

        def start_of(s, size):
            off = 0
            for k in range(s):
                size = size // stages[k][2]
                off = off + digit_of(stages[k]) * size
            return off

        def part(ref, off, size):
            return ref.at[pl.ds(pl.multiple_of(off, 16), size)]

        def slot(s, d):
            return total - size_of(s, total) + (d - 1) * size_of(s + 1, total)

        def reduce_copies(s):
            size = size_of(s + 1, total)
            for d in range(1, stages[s][2]):
                other, where = peer_of(stages[s], d)
                yield remote(
                    part(w, start_of(s, total) + other * size, size), part(rr, slot(s, d), size),
                    csend.at[number, sem_at[s] + d - 1], crecv.at[number, sem_at[s] + d - 1], where,
                )

        def collect_copies(s):
            at = part(ga, start_of(s + 1, kept), size_of(s + 1, kept))
            for d in range(1, stages[s][2]):
                _, where = peer_of(stages[s], d)
                k = sem_at[deep] + sem_at[s] + d - 1
                yield remote(at, at, csend.at[number, k], crecv.at[number, k], where)

        def own_part():
            return pl.ds(pl.multiple_of(start_of(collect, kept), 16), size_of(collect, kept))

        def advance(u, only_send=False):
            if 0 < u <= deep and not only_send:
                s = u - 1
                size = size_of(u, total)
                for c in reduce_copies(s):
                    c.wait_recv()
                mine = pl.ds(pl.multiple_of(start_of(u, total), 16), size)
                added = w[mine, :].astype(F32)
                for d in range(1, stages[s][2]):
                    added = added + rr[pl.ds(slot(s, d), size), :].astype(F32)
                if u < deep:
                    w[mine, :] = added.astype(BF)
                else:
                    ga[own_part(), :] = added.astype(BF)
            if u < deep:
                for c in reduce_copies(u):
                    c.start()
            if deep < u <= deep + collect:
                for c in collect_copies(collect - (u - deep)):
                    c.wait_recv()
            if deep <= u < deep + collect:
                for c in collect_copies(collect - 1 - (u - deep)):
                    c.start()
            if u == deep + collect:
                done()

        def sent_all(reduced=True):
            for s in range(deep if reduced else 0):
                for c in reduce_copies(s):
                    c.wait_send()
            for s in range(collect):
                for c in collect_copies(s):
                    c.wait_send()

        waits = [stage[3] for stage in stages] + [stage[3] for stage in stages[:collect][::-1]] + [0]
        return advance, waits, sent_all, own_part

    core = pairs("dp", (1, 3))
    straight = core + pairs("group", (3, 2)) + pairs("expert", (2, 3))
    turned = core + pairs("group", (2, 3))[::-1] + pairs("expert", (2, 3))
    short = core + [line("group", 3), line("expert", 3)]
    pieces = (2 * H // 16) * (D // 128)
    each = pieces // (lax.axis_size("dp") * lax.axis_size("group"))

    def place(p, e):
        return ((p // each * n + e) * each + p % each) * 16

    g1 = g1_ref[...]
    g2 = g2_ref[...]
    for src, base in ((wq_in, 0), (wo_in, H // 16)):
        for g in range(H // 16):
            for q in range(D // 128):
                at = ((base + g) * (D // 128) + q) * 16
                own_ref[at : at + 16, :] = src[g * 16 : (g + 1) * 16, q * 128 : (q + 1) * 128]
    collect_weights, _, weights_sent, weights_part = chain(
        0, None, None, we_ref, short, len(short), lambda: None
    )
    shard = sum(digit_of(stage) * 2 ** (len(core) - 1 - k) for k, stage in enumerate(core))
    shard = shard * lax.axis_size("group") + lax.axis_index("group")
    we_ref[weights_part(), :] = own_ref[pl.ds(pl.multiple_of(shard * each * 16, 16), each * 16), :]
    collect_weights(len(short), True)
    wst_ref[EH : EH + KV, :] = kvw_ref[...].astype(F32).T.astype(BF)

    def make_kv(r, _):
        sl = rows_of(r)
        tok = tok_ref[sl, :].astype(F32)
        normed = (tok * inv_rms(tok) * g1).astype(BF)
        nrm_ref[sl, :] = normed
        kv_ref[r, block(z, T), :] = nn(normed, kvw_ref[...]).astype(BF)
        return 0

    make_kv(0, 0)
    send_own(row_copies(0))
    lax.fori_loop(1, rows, make_kv, 0)

    seg = seg_ref[...]
    for i in range(2):
        cut_ref[i] = jnp.broadcast_to(
            jnp.sum((seg < i + 1).astype(F32), axis=1, keepdims=True), (rows, 128)
        ).astype(jnp.int32)
    for ref in (g2g_ref, dwst_ref, dwo_ref, wk_ref):
        ref[...] = jnp.zeros_like(ref)
    for k in range(max(n - 2, len(short))):
        if k < n - 2:
            gather_step(k)
        if k < len(short):
            collect_weights(len(short) + k + 1)
    for e in range(n):
        for base, ref in ((0, wst_ref), (H // 16, wo_ref)):
            for g in range(H // 16):
                for q in range(D // 128):
                    at = place((base + g) * (D // 128) + q, e)
                    ref[e * H + g * 16 : e * H + (g + 1) * 16, q * 128 : (q + 1) * 128] = (
                        we_ref[at : at + 16, :]
                    )
    loads[0].wait()

    def pick(all_t, route):
        acc = all_t[0:H]
        for e in range(1, n):
            acc = jnp.where(route == e, all_t[e * H : (e + 1) * H], acc)
        return acc

    def spread(first, second, e0, e1):
        parts = [jnp.where(e0 == e, first, jnp.where(e1 == e, second, 0.0)) for e in range(n)]
        return jnp.concatenate(parts, axis=0).astype(BF)

    def attend(i, r):
        sl, gl = rows_of(r), rows_of(i)
        q_all = nt(wst_ref[0:EH, :], nrm_ref[sl, :])
        e0, e1 = route_ref[z, r, 0:1, :], route_ref[z, r, 1:2, :]
        ga = (gate_ref[r, 0:1, :], gate_ref[r, 1:2, :])
        kv = kv_ref[r]
        kvt = kv.T
        c1, c2 = cut_ref[0, pl.ds(r, 1), :], cut_ref[1, pl.ds(r, 1), :]
        lane = lax.broadcasted_iota(jnp.int32, (seq, KV), 1)
        key_pos = lax.broadcasted_iota(jnp.int32, (seq, KV), 0)
        key_seg = H + (key_pos >= c1).astype(jnp.int32) + (key_pos >= c2).astype(jnp.int32)
        onehot = jnp.where(lane == key_seg, 1.0, 0.0)
        kaug = jnp.where(lane < H, kv.astype(F32), onehot).astype(BF)
        pos = z * T + lax.broadcasted_iota(jnp.int32, (KV - H, T), 1)
        q_seg = (pos >= c1[:, 0:1]).astype(jnp.int32) + (pos >= c2[:, 0:1]).astype(jnp.int32)
        sid = lax.broadcasted_iota(jnp.int32, (KV - H, T), 0)
        bias = jnp.where((sid < 3) & (sid != q_seg), -1e30, 0.0).astype(BF)
        vaug = jnp.concatenate([jnp.ones((16, seq), BF), kvt[H:, :]], axis=0)
        scale = LOG2E / math.sqrt(H)
        mixes = []
        for j, route in enumerate((e0, e1)):
            qt = pick(q_all, route).astype(BF)
            qt_ref[i, j] = qt
            s = nn(kaug, jnp.concatenate([qt, bias], axis=0))
            m = jnp.max(s, axis=0, keepdims=True)
            p = jnp.exp2(s * scale - m * scale).astype(BF)
            p_ref[i, j] = p
            av = nn(vaug, p)
            rinv = 1.0 / av[0:1]
            att = av[16:] * rinv
            rinv_ref[i, j : j + 1, :] = rinv
            att_ref[i, j] = att.astype(BF)
            mixes.append(att * ga[j])
        gt = spread(mixes[0], mixes[1], e0, e1)
        gt_ref[i] = gt
        res = tok_ref[sl, :].astype(F32) + nn(gt.T, wo_ref[...])
        res_ref[gl, :] = res
        sec = (res * inv_rms(res) * g2).astype(BF)
        sec_ref[gl, :] = sec
        sect_ref[:, gl] = sec.T
        cott_ref[:, gl] = cot_ref[sl, :].T

    def feed_forward(grp, fb):
        half = groups[grp] * T
        base = sum(groups[:grp]) * T
        MB = min(512, half)
        fs = pl.ds(fb * fblk, fblk)

        def feed(i, _):
            sl = pl.ds(pl.multiple_of(i * MB, MB), MB)
            al = pl.ds(pl.multiple_of(base + i * MB, T), MB)
            h = nn(sec_ref[sl, :], up_ref[:, fs])
            act, slope = gelu_both(h)
            act = act.astype(BF)
            act_ref[sl, :] = act
            hg = (nt(cot_ref[al, :], dn_ref[fs, :]) * slope).astype(BF)
            hg_ref[sl, :] = hg
            o = nn(act, dn_ref[fs, :])
            s = nt(hg, up_ref[:, fs])
            if fb == 0:
                oacc_ref[sl, :] = res_ref[sl, :] + o
                tg_ref[al, :] = s
            else:
                oacc_ref[sl, :] += o
                tg_ref[al, :] += s
            sites(i, half // MB)
            return 0

        lax.fori_loop(0, half // MB, feed, 0)

        a = nn(sect_ref[:, 0:half], hg_ref[0:half, :])
        b = nn(cott_ref[:, 0:half], act_ref[0:half, :])
        for t in range(fblk // 128):
            at = slice(t * D, (t + 1) * D)
            for k, v in ((2 * fb, a), (2 * fb + 1, b)):
                v = v[:, t * 128 : (t + 1) * 128]
                if grp > 0:
                    v = v + w_ref[k, at, :].astype(F32)
                w_ref[k, at, :] = v.astype(BF)
        site()

    def out_copy(r):
        slot = lax.rem(r, 2)
        return pltpu.make_async_copy(ost_ref.at[slot], out_hbm.at[rows_of(r)], ost_sem.at[slot])

    def grad_copy(r):
        return pltpu.make_async_copy(tg_ref.at[rows_of(r)], tg_hbm.at[rows_of(r)], tg_sem.at[r])

    def back(i, r):
        sl, gl = rows_of(r), rows_of(i)
        @pl.when(r >= 2)
        def _():
            out_copy(r - 2).wait()

        ost_ref[lax.rem(r, 2)] = oacc_ref[gl, :].astype(BF)
        out_copy(r).start()
        dres, dgain = rms_back(res_ref[gl, :], g2, tg_ref[sl, :])
        g2g_ref[...] += fold(dgain)
        rgrad = cot_ref[sl, :].astype(F32) + dres
        tg_ref[sl, :] = rgrad
        rb = rgrad.astype(BF)
        dwo_ref[...] += nn(gt_ref[i], rb)
        ag_all = nt(wo_ref[...], rb)
        e0, e1 = route_ref[z, r, 0:1, :], route_ref[z, r, 1:2, :]
        ga = (gate_ref[r, 0:1, :], gate_ref[r, 1:2, :])
        kv = kv_ref[r]
        kt = kv.T[0:H, :]
        zero = jnp.zeros((H, T), BF)
        kvg = None
        dqs = []
        for j, route in enumerate((e0, e1)):
            rinv = rinv_ref[i, j : j + 1, :]
            da = pick(ag_all, route) * (ga[j] * rinv)
            dd = jnp.sum(da * att_ref[i, j].astype(F32), axis=0, keepdims=True)
            dab = jnp.concatenate([zero, da.astype(BF)], axis=0)
            qb = jnp.concatenate([qt_ref[i, j] * (1.0 / math.sqrt(H)), zero], axis=0).astype(BF)
            p = p_ref[i, j]
            dp = nn(kv, dab)
            ds = (p.astype(F32) * (dp - dd)).astype(BF)
            part = nt(p, dab) + nt(ds, qb)
            kvg = part if kvg is None else kvg + part
            dqs.append(nn(kt, ds) * (1.0 / math.sqrt(H)))
        kvp_ref[r] = kvg.astype(BF)
        qg = spread(dqs[0], dqs[1], e0, e1)
        qg_ref[r] = qg
        dwst_ref[0:EH, :] += nn(qg, nrm_ref[sl, :])

    def key_part(r, direct=False):
        if direct:
            end_straight(r)
        else:
            sum_end(r)
        dwst_ref[EH : EH + KV, :] += nn(kvp_ref[r, block(z, T), :].T, nrm_ref[rows_of(r), :])

    def token_part(r):
        sl = rows_of(r)
        tok = tok_ref[sl, :].astype(F32)
        stack = jnp.concatenate([qg_ref[r], kvp_ref[r, block(z, T), :].T], axis=0)
        dtok, _ = rms_back(tok, g1, nn(stack.T, wst_ref[...]))
        tg_ref[sl, :] += dtok
        grad_copy(r).start()

    blocks = FF // fblk

    def put_experts():
        for ref, base in ((dwst_ref, 0), (dwo_ref, H)):
            for e in range(n):
                for g in range(H // 16):
                    tile = ref[e * H + g * 16 : e * H + (g + 1) * 16, :].astype(BF)
                    for q in range(D // 128):
                        at = place((base // 16 + g) * (D // 128) + q, e)
                        we_ref[at : at + 16, :] = tile[:, q * 128 : (q + 1) * 128]

    def experts_done():
        def tile(base, q):
            rows_at = [((base // 16 + g) * (D // 128) + q) * 16 for g in range(H // 16)]
            return jnp.concatenate([gae_ref[a : a + 16, :] for a in rows_at], axis=0).astype(F32)

        for q in range(D // 128):
            wq_out[:, q * 128 : (q + 1) * 128] = tile(0, q)
            wo_out[:, q * 128 : (q + 1) * 128] = tile(H, q)

    tall = wk_ref.shape[0] // (D // 128)

    def put_keys():
        summed = jnp.sum(wst_ref[...].astype(F32) * dwst_ref[...], axis=0, keepdims=True) / g1
        second_gain = jnp.sum(g2g_ref[...], axis=0, keepdims=True)
        gains = jnp.concatenate([summed, second_gain, jnp.zeros((14, D), F32)], axis=0).astype(BF)
        keys = dwst_ref[EH : EH + KV, :].astype(BF)
        for q in range(D // 128):
            wk_ref[q * tall : q * tall + KV, :] = keys[:, q * 128 : (q + 1) * 128]
            wk_ref[q * tall + KV : q * tall + KV + 16, :] = gains[:, q * 128 : (q + 1) * 128]

    def keys_done():
        for q in range(D // 128):
            lanes = slice(q * 128, (q + 1) * 128)
            kvw_out[lanes, :] = gak_ref[q * tall : q * tall + KV, :].astype(F32).T
            gain_ref[:, lanes] = gak_ref[q * tall + KV : q * tall + KV + 16, :].astype(F32)

    def result_copy(k):
        to = ddn_hbm if k % 2 else dup_hbm
        return pltpu.make_async_copy(ga_ref.at[k], to.at[k // 2], done_sem.at[k])

    chains = []
    for fb in range(blocks):
        chains.append(
            [
                chain(2 * fb + 1, w_ref.at[2 * fb], rr_ref.at[2 * fb], ga_ref.at[2 * fb],
                      straight, len(straight), result_copy(2 * fb).start),
                chain(2 * fb + 2, w_ref.at[2 * fb + 1], rr_ref.at[2 * fb + 1],
                      ga_ref.at[2 * fb + 1], turned, len(turned), result_copy(2 * fb + 1).start),
            ]
        )
    chains.append(
        [chain(2 * blocks + 1, we_ref, rre_ref, gae_ref, short, len(short) - 1, experts_done)]
    )
    chains.append([chain(2 * blocks + 2, wk_ref, rrk_ref, gak_ref, short, len(short), keys_done)])
    at_step = [None] * len(chains)
    count_down = [0] * len(chains)
    gathers, sums, pace = [], [], [0]

    def begin(c):
        at_step[c] = 0
        count_down[c] = chains[c][0][1][0]
        for one in chains[c]:
            one[0](0)

    def under_way(c):
        return at_step[c] is not None and at_step[c] < len(chains[c][0][1]) - 1

    def tick(weight):
        for c in range(len(chains)):
            if under_way(c):
                count_down[c] -= weight
                if count_down[c] <= 0:
                    at_step[c] += 1
                    count_down[c] = chains[c][0][1][at_step[c]]
                    for one in chains[c]:
                        one[0](at_step[c])

    def site(weight=1, adds=1):
        pace[0] += weight
        if gathers and pace[0] >= 4:
            pace[0] = 0
            gather_step(gathers.pop(0))
        for _ in range(adds):
            if sums:
                sum_step(*sums.pop(0))
        tick(weight)

    def sites(i, count, weight=1, adds=1):
        for k in range(count):
            @pl.when(i == k)
            def _():
                site(weight, adds)

    gathers += range(groups[0] + n - 2, rows + n - 2)

    for grp, rg in enumerate(groups):
        lo = sum(groups[:grp])
        hi = lo + rg

        while gathers and grp > 0 and gathers[0] <= hi + n - 3:
            gather_step(gathers.pop(0))

        def attend_row(i, _, grp=grp, lo=lo, rg=rg):
            if grp == 0:
                gather_step(i + n - 2)
            attend(i, lo + i)
            if grp > 0:
                sites(i, rg)
            return 0

        lax.fori_loop(0, rg, attend_row, 0)
        if grp == 0:
            loads[1].wait()
            loads[2].wait()
        for fb in range(blocks):
            feed_forward(grp, fb)
            if grp == len(groups) - 1:
                begin(fb)

        while sums:
            sum_step(*sums.pop(0))
        final = grp == len(groups) - 1
        top = hi - 1 if final else hi
        lag = 2 if final else 4

        def back_row(i, _, lo=lo, rg=rg, top=top, lag=lag, final=final):
            back(i, lo + i)
            sum_step(i, lo, top, lag)
            if final:
                @pl.when(lo + i >= top)
                def _():
                    send_straight(lo + i)

            sites(i, rg, 2)
            return 0

        lax.fori_loop(0, rg, back_row, 0)
        sums += [(k, lo, top, lag) for k in range(rg, top - lo + lag * (n - 1))]

    weights_sent(False)
    put_experts()
    begin(blocks)
    early = rows - groups[-1]

    adds = -(-len(sums) // early)

    def finish_first(i, _):
        key_part(i)
        token_part(i)
        sites(i, early, 1, adds)
        return 0

    lax.fori_loop(0, early, finish_first, 0)

    def finish_keys(r, _):
        key_part(r)
        return 0

    def finish_straight(r, _):
        key_part(r, True)
        return 0

    lax.fori_loop(early, top, finish_keys, 0)
    lax.fori_loop(top, rows, finish_straight, 0)
    put_keys()
    begin(blocks + 1)
    site()

    def finish_second(i, _):
        token_part(early + i)
        sites(i, rows - early)
        return 0

    lax.fori_loop(0, rows - early, finish_second, 0)
    out_copy(rows - 2).wait()
    out_copy(rows - 1).wait()
    def all_sent(r, _):
        sent(row_copies(r))
        sums_sent(r)
        return 0

    lax.fori_loop(0, rows, all_sent, 0)
    while any(under_way(c) for c in range(len(chains))):
        tick(1)

    def grads_out(r, _):
        grad_copy(r).wait()
        return 0

    lax.fori_loop(0, rows, grads_out, 0)
    for parts in chains:
        for one in parts:
            one[2]()
    for k in range(2 * blocks):
        result_copy(k).wait()


def lay_kernel(
    up_ref, dn_ref, tg_ref, o_ref, gain_ref, kvw_ref, wq_ref, wo_ref,
    dup_ref, ddn_ref, tgo_ref, oo_ref, g1_ref, g2_ref, kvwo_ref, wqo_ref, woo_ref,
):
    for t in range(up_ref.shape[0]):
        lanes = slice(t * 128, (t + 1) * 128)
        dup_ref[:, lanes] = up_ref[t].astype(F32)
        ddn_ref[lanes, :] = dn_ref[t].T.astype(F32)
    tgo_ref[...] = tg_ref[...]
    oo_ref[...] = o_ref[...]

    @pl.when(pl.program_id(0) == 0)
    def _():
        g1_ref[...] = gain_ref[0:1, :]
        g2_ref[...] = gain_ref[1:2, :]
        kvwo_ref[...] = kvw_ref[...]
        wqo_ref[...] = wq_ref[...]
        woo_ref[...] = wo_ref[...]


def on_device(
    tokens, segments, routes, gate_values, gain_one, gain_two, kv_weight,
    query_weight, output_weight, up_weight, down_weight, out_grad,
):
    rows, T, D = tokens.shape
    H = query_weight.shape[2]
    n = lax.axis_size("expert")
    EH = n * H
    KV = 2 * H
    seq = n * T
    FF = up_weight.shape[1]
    toks = rows * T
    rg = rows // 2
    half = rg * T
    devices = n * lax.axis_size("group") * lax.axis_size("dp")
    fblk = 512 * max(1, devices // 128)
    tall = fblk * D // 128
    tall_e = n * 2 * H * D // 128
    tall_k = 2 * KV * D // 128
    tall_k = max(tall_k, 16 * devices)
    blocks = FF // fblk
    steps = (devices // n - 1).bit_length() + lax.axis_size("group") + n
    sds = jax.ShapeDtypeStruct
    vmem = pltpu.VMEM
    dma = pltpu.SemaphoreType.DMA

    route = jnp.transpose(routes, (0, 1, 3, 2))
    gate = jnp.transpose(gate_values, (0, 2, 1))
    whole = pl.BlockSpec(memory_space=pltpu.VMEM)
    hbm = pl.BlockSpec(memory_space=pl.ANY)
    out, tg, dup, ddn, gains, kvw_grad, wq_grad, wo_grad = pl.pallas_call(
        functools.partial(mega_kernel, n, rows, T, FF, fblk),
        out_shape=(
            sds((toks, D), BF), sds((toks, D), F32), sds((blocks, tall, 128), BF), sds((blocks, tall, 128), BF),
            sds((16, D), F32), sds((D, KV), F32), sds((H, D), F32), sds((H, D), F32),
        ),
        in_specs=[whole, hbm] + [whole] * 8 + [hbm, hbm],
        out_specs=[hbm] * 4 + [whole] * 4,
        scratch_shapes=[
            vmem((8, D), F32),
            vmem((EH + KV, D), F32),
            vmem((EH, D), F32),
            vmem((2 * blocks, tall, 128), BF),
            vmem((tall_e, 128), BF),
            vmem((tall_k, 128), BF),
            vmem((2 * blocks, tall, 128), BF),
            vmem((tall_e, 128), BF),
            vmem((tall_k, 128), BF),
            vmem((2 * blocks, tall, 128), BF),
            vmem((tall_e // n, 128), BF),
            vmem((tall_k, 128), BF),
            vmem((tall_e // n, 128), BF),
            vmem((toks, D), F32),
            vmem((2, T, D), BF),
            vmem((toks, D), BF),
            vmem((D, FF), BF),
            vmem((FF, D), BF),
            vmem((toks, D), BF),
            vmem((rows, seq, KV), BF),
            vmem((rows, seq, KV), BF),
            vmem((rows, n + 1, T, KV), BF),
            vmem((EH + KV, D), BF),
            vmem((EH, D), BF),
            vmem((2, rows, 128), jnp.int32),
            vmem((rg, 2, seq, T), BF),
            vmem((rg, 2, H, T), BF),
            vmem((rg, 2, H, T), BF),
            vmem((rg, 2, T), F32),
            vmem((rg, EH, T), BF),
            vmem((half, D), F32),
            vmem((half, D), BF),
            vmem((D, half), BF),
            vmem((D, half), BF),
            vmem((half, D), F32),
            vmem((half, fblk), BF),
            vmem((half, fblk), BF),
            vmem((rows, EH, T), BF),
            dma((3,)),
            dma((rows, n + 1)),
            dma((rows, n)),
            dma((rows, n)),
            dma((rows, n + 1)),
            dma((2 * blocks + 3, 2 * steps)),
            dma((2 * blocks + 3, 2 * steps)),
            dma((2 * blocks,)),
            dma((2,)),
            dma((rows,)),
        ],
        compiler_params=pltpu.CompilerParams(
            vmem_limit_bytes=VMEM_LIMIT, collective_id=0, has_side_effects=True
        ),
    )(
        tokens.reshape(toks, D), out_grad.reshape(toks, D), segments, route, gate,
        gain_one.reshape(1, D), gain_two.reshape(1, D), kv_weight, query_weight[0].T,
        output_weight[0], up_weight, down_weight,
    )
    parts = 2
    tiles = FF // 128
    step = tiles // parts
    bt = toks // parts
    row_block = pl.BlockSpec((bt, D), lambda i: (i, 0))
    tile_block = pl.BlockSpec((step, D, 128), lambda i: (i, 0, 0))

    def full(a):
        return pl.BlockSpec(a.shape, lambda i: (0, 0))

    gain = sds((1, D), F32)
    small = (gain, gain, kvw_grad, wq_grad, wo_grad)
    dup, ddn, tg, out, gain_one_grad, gain_two_grad, kvw_grad, wq_grad, wo_grad = pl.pallas_call(
        lay_kernel,
        grid=(parts,),
        out_shape=(
            sds((D, FF), F32), sds((FF, D), F32), sds((toks, D), F32), sds((toks, D), BF),
        ) + tuple(sds(a.shape, F32) for a in small),
        in_specs=[tile_block, tile_block, row_block, row_block, full(gains)]
        + [full(a) for a in small[2:]],
        out_specs=[
            pl.BlockSpec((D, step * 128), lambda i: (0, i)),
            pl.BlockSpec((step * 128, D), lambda i: (i, 0)),
            row_block, row_block,
        ] + [full(a) for a in small],
        compiler_params=pltpu.CompilerParams(vmem_limit_bytes=VMEM_LIMIT),
    )(
        dup.reshape(tiles, D, 128), ddn.reshape(tiles, D, 128), tg, out, gains,
        kvw_grad, wq_grad, wo_grad,
    )
    return (
        out.reshape(tokens.shape),
        tg.reshape(tokens.shape),
        gain_one_grad.reshape(D),
        gain_two_grad.reshape(D),
        kvw_grad,
        wq_grad.T[None],
        wo_grad[None],
        dup,
        ddn,
    )


def solution(mesh):
    rows = P(("group", "dp"), "expert", None)
    in_specs = (
        rows,
        P(("group", "dp"), None),
        P(None, ("group", "dp"), None, None),
        rows,
        P(), P(), P(),
        P("expert", None, None),
        P("expert", None, None),
        P(), P(),
        rows,
    )
    out_specs = (
        rows, rows, P(), P(), P(),
        P("expert", None, None),
        P("expert", None, None),
        P(), P(),
    )
    return jax.shard_map(
        on_device, mesh=mesh, in_specs=in_specs, out_specs=out_specs, check_vma=False
    )
```

```python
import functools
import math

import jax
import jax.numpy as jnp
from jax import lax
from jax.experimental import pallas as pl
from jax.experimental.pallas import tpu as pltpu
from jax.sharding import PartitionSpec as P

EPS = 1e-06
F32 = jnp.float32
BF = jnp.bfloat16
LOG2E = 1.4426950408889634
VMEM_LIMIT = 66_000_000


def nn(a, b):
    return lax.dot_general(a, b, (((1,), (0,)), ((), ())), preferred_element_type=F32)


def nt(a, b):
    return lax.dot_general(a, b, (((1,), (1,)), ((), ())), preferred_element_type=F32)


def gelu_both(x):
    c0 = math.sqrt(2.0 / math.pi)
    c1 = 0.044715 * c0
    x2 = x * x
    t = jnp.tanh(x * (c0 + c1 * x2))
    h = 0.5 + 0.5 * t
    act = x * h
    slope = h + (act - act * h) * (2.0 * c0 + (6.0 * c1) * x2)
    return act, slope


def inv_rms(x):
    return lax.rsqrt(jnp.mean(x * x, axis=-1, keepdims=True) + EPS)


def rms_back(x, gain, dy):
    inv = inv_rms(x)
    xn = x * inv
    gdy = gain * dy
    dx = inv * (gdy - xn * jnp.mean(xn * gdy, axis=-1, keepdims=True))
    return dx, dy * xn


def fold(x):
    return jnp.sum(x.reshape(x.shape[0] // 8, 8, x.shape[1]), axis=0)


def remote(src, dst, send, recv, where):
    return pltpu.make_async_remote_copy(
        src_ref=src, dst_ref=dst, send_sem=send, recv_sem=recv,
        device_id=where, device_id_type=pl.DeviceIdType.MESH,
    )


def mega_kernel(
    n, rows, T, FF, fblk,
    tok_ref, cot_hbm, seg_ref, route_ref, gate_ref, g1_ref, g2_ref,
    kvw_ref, wq_in, wo_in, up_hbm, dn_hbm,
    out_hbm, tg_hbm, dup_hbm, ddn_hbm, gain_ref, kvw_out, wq_out, wo_out,
    g2g_ref, dwst_ref, dwo_ref, w_ref, we_ref, wk_ref, rr_ref, rre_ref, rrk_ref,
    ga_ref, gae_ref, gak_ref, own_ref, tg_ref, ost_ref,
    cot_ref, up_ref, dn_ref, nrm_ref, kv_ref, kvp_ref, rcv_ref, wst_ref, wo_ref,
    cut_ref, p_ref, qt_ref, att_ref, rinv_ref, gt_ref, res_ref, sec_ref,
    sect_ref, cott_ref, oacc_ref, act_ref, hg_ref, qg_ref,
    load_sem, gsend, grecv, rsend, rrecv, csend, crecv, done_sem,
    ost_sem, tg_sem,
):
    D = tok_ref.shape[1]
    H = wo_in.shape[0]
    EH = n * H
    KV = 2 * H
    seq = n * T
    groups = (rows // 4, rows // 4, rows // 2)
    z = lax.axis_index("expert")
    has_left, has_right = z > 0, z < n - 1
    left, right = {"expert": lax.rem(z + n - 1, n)}, {"expert": lax.rem(z + 1, n)}

    loads = [
        pltpu.make_async_copy(a, b, load_sem.at[i])
        for i, (a, b) in enumerate(((cot_hbm, cot_ref), (up_hbm, up_ref), (dn_hbm, dn_ref)))
    ]
    for c in loads:
        c.start()

    barrier = pltpu.get_barrier_semaphore()
    peers = 0
    for axis in ("group", "dp", "expert"):
        size = lax.axis_size(axis)
        for d in range(1, size):
            pl.semaphore_signal(
                barrier, inc=1, device_id={axis: lax.rem(lax.axis_index(axis) + d, size)},
                device_id_type=pl.DeviceIdType.MESH,
            )
            peers += 1
    pl.semaphore_wait(barrier, peers)

    def rows_of(r):
        return pl.ds(pl.multiple_of(r * T, T), T)

    def block(b, size):
        return pl.ds(pl.multiple_of(b * size, size), size)

    def kv_copy(r, b, slot, where):
        at = kv_ref.at[r, block(b, T)]
        return remote(at, at, gsend.at[r, slot], grecv.at[r, b], where)

    def pass_on(d, copies):
        @pl.when(z - d >= 0)
        def _():
            for c in copies(z - d, z - d, right):
                c.wait_recv()

            @pl.when(has_right)
            def _():
                for c in copies(z - d, z - d, right):
                    c.start()

        @pl.when(z + d <= n - 1)
        def _():
            for c in copies(z + d, z + d, left):
                c.wait_recv()

            @pl.when(has_left)
            def _():
                for c in copies(z + d, z + d, left):
                    c.start()

    def send_own(copies):
        @pl.when(has_right)
        def _():
            for c in copies(z, z, right):
                c.start()

        @pl.when(has_left)
        def _():
            for c in copies(z, n, left):
                c.start()

    def sent(copies):
        for b in range(n):
            goes = ((b <= z) & has_right) | ((b > z) & has_left)

            @pl.when(goes)
            def _(b=b):
                for c in copies(b, b, right):
                    c.wait_send()

        @pl.when(has_left)
        def _():
            for c in copies(z, n, left):
                c.wait_send()

    def row_copies(r):
        return lambda b, slot, where: (kv_copy(r, b, slot, where),)

    def gather_step(k):
        @pl.when(k + 1 < rows)
        def _():
            send_own(row_copies(k + 1))

        for d in range(1, n):
            r = k - d + 1

            @pl.when((r >= 0) & (r < rows))
            def _(r=r, d=d):
                pass_on(d, row_copies(r))

    def sum_copy(r, b, slot, where):
        return remote(
            kvp_ref.at[r, block(b, T)], rcv_ref.at[r, slot], rsend.at[r, b], rrecv.at[r, slot], where
        )

    def sum_block(r, b, slot, first):
        @pl.when(jnp.logical_not(first))
        def _():
            sum_copy(r, b, slot, right).wait_recv()
            at = block(b, T)
            kvp_ref[r, at, :] = (
                kvp_ref[r, at, :].astype(F32) + rcv_ref[r, slot].astype(F32)
            ).astype(BF)

    def sum_step(k, lo, hi, lag):
        r1 = k - lag * z + lo

        @pl.when((r1 >= lo) & (r1 < hi))
        def _():
            def go(c, _):
                b = n - 1 - c
                sum_block(r1, b, b, z == 0)
                sum_copy(r1, b, b, right).start()
                return 0

            lax.fori_loop(0, n - 1 - z, go, 0)

        r2 = k - lag * (n - 1 - z) + lo

        @pl.when((r2 >= lo) & (r2 < hi))
        def _():
            def go(b, _):
                sum_block(r2, b, b, z == n - 1)
                sum_copy(r2, b, jnp.where(b == z - 1, n, b), left).start()
                return 0

            lax.fori_loop(0, z, go, 0)

    def sum_end(r):
        @pl.when(has_left)
        def _():
            sum_block(r, z, z, False)

        @pl.when(has_right)
        def _():
            sum_block(r, z, n, False)

    def straight_copy(r, b, source):
        return remote(
            kvp_ref.at[r, block(b, T)], rcv_ref.at[r, source], rsend.at[r, b],
            rrecv.at[r, source], {"expert": b},
        )

    def send_straight(r):
        for d in range(1, n):
            straight_copy(r, lax.rem(z + d, n), z).start()

    def end_straight(r):
        at = block(z, T)
        total = kvp_ref[r, at, :].astype(F32)
        for d in range(1, n):
            source = lax.rem(z + d, n)
            straight_copy(r, source, source).wait_recv()
            total = total + rcv_ref[r, source].astype(F32)
        kvp_ref[r, at, :] = total.astype(BF)

    def sums_sent(r):
        for b in range(n):
            @pl.when(z != b)
            def _(b=b):
                sum_copy(r, b, b, right).wait_send()

    def pair(axis, b, wait):
        return (axis, 2**b, 2, wait)

    def line(axis, wait):
        return (axis, 1, lax.axis_size(axis), wait)

    def pairs(axis, waits):
        count = (lax.axis_size(axis) - 1).bit_length()
        return [pair(axis, b, waits[min(b, len(waits) - 1)]) for b in range(count)]

    def digit_of(stage):
        axis, stride, radix, _ = stage
        return lax.rem(lax.axis_index(axis) // stride, radix)

    def peer_of(stage, d):
        axis, stride, radix, _ = stage
        digit = digit_of(stage)
        other = lax.rem(digit + d, radix)
        return other, {axis: lax.axis_index(axis) + (other - digit) * stride}

    def chain(number, w, rr, ga, stages, collect, done):
        deep = len(stages)
        total = w.shape[0] if w is not None else ga.shape[0]
        kept = ga.shape[0]
        sem_at = [0]
        for stage in stages:
            sem_at.append(sem_at[-1] + stage[2] - 1)

        def size_of(s, size):
            for k in range(s):
                size = size // stages[k][2]
            return size

        def start_of(s, size):
            off = 0
            for k in range(s):
                size = size // stages[k][2]
                off = off + digit_of(stages[k]) * size
            return off

        def part(ref, off, size):
            return ref.at[pl.ds(pl.multiple_of(off, 16), size)]

        def slot(s, d):
            return total - size_of(s, total) + (d - 1) * size_of(s + 1, total)

        def reduce_copies(s):
            size = size_of(s + 1, total)
            for d in range(1, stages[s][2]):
                other, where = peer_of(stages[s], d)
                yield remote(
                    part(w, start_of(s, total) + other * size, size), part(rr, slot(s, d), size),
                    csend.at[number, sem_at[s] + d - 1], crecv.at[number, sem_at[s] + d - 1], where,
                )

        def collect_copies(s):
            at = part(ga, start_of(s + 1, kept), size_of(s + 1, kept))
            for d in range(1, stages[s][2]):
                _, where = peer_of(stages[s], d)
                k = sem_at[deep] + sem_at[s] + d - 1
                yield remote(at, at, csend.at[number, k], crecv.at[number, k], where)

        def own_part():
            return pl.ds(pl.multiple_of(start_of(collect, kept), 16), size_of(collect, kept))

        def advance(u, only_send=False):
            if 0 < u <= deep and not only_send:
                s = u - 1
                size = size_of(u, total)
                for c in reduce_copies(s):
                    c.wait_recv()
                mine = pl.ds(pl.multiple_of(start_of(u, total), 16), size)
                added = w[mine, :].astype(F32)
                for d in range(1, stages[s][2]):
                    added = added + rr[pl.ds(slot(s, d), size), :].astype(F32)
                if u < deep:
                    w[mine, :] = added.astype(BF)
                else:
                    ga[own_part(), :] = added.astype(BF)
            if u < deep:
                for c in reduce_copies(u):
                    c.start()
            if deep < u <= deep + collect:
                for c in collect_copies(collect - (u - deep)):
                    c.wait_recv()
            if deep <= u < deep + collect:
                for c in collect_copies(collect - 1 - (u - deep)):
                    c.start()
            if u == deep + collect:
                done()

        def sent_all(reduced=True):
            for s in range(deep if reduced else 0):
                for c in reduce_copies(s):
                    c.wait_send()
            for s in range(collect):
                for c in collect_copies(s):
                    c.wait_send()

        waits = [stage[3] for stage in stages] + [stage[3] for stage in stages[:collect][::-1]] + [0]
        return advance, waits, sent_all, own_part

    core = pairs("dp", (1, 3))
    straight = core + pairs("group", (3, 2)) + pairs("expert", (2, 3))
    turned = core + pairs("group", (2, 3))[::-1] + pairs("expert", (2, 3))
    short = core + [line("group", 3), line("expert", 3)]
    pieces = (2 * H // 16) * (D // 128)
    each = pieces // (lax.axis_size("dp") * lax.axis_size("group"))

    def place(p, e):
        return ((p // each * n + e) * each + p % each) * 16

    g1 = g1_ref[...]
    g2 = g2_ref[...]
    for src, base in ((wq_in, 0), (wo_in, H // 16)):
        for g in range(H // 16):
            for q in range(D // 128):
                at = ((base + g) * (D // 128) + q) * 16
                own_ref[at : at + 16, :] = src[g * 16 : (g + 1) * 16, q * 128 : (q + 1) * 128]
    collect_weights, _, weights_sent, weights_part = chain(
        0, None, None, we_ref, short, len(short), lambda: None
    )
    shard = sum(digit_of(stage) * 2 ** (len(core) - 1 - k) for k, stage in enumerate(core))
    shard = shard * lax.axis_size("group") + lax.axis_index("group")
    we_ref[weights_part(), :] = own_ref[pl.ds(pl.multiple_of(shard * each * 16, 16), each * 16), :]
    collect_weights(len(short), True)
    wst_ref[EH : EH + KV, :] = kvw_ref[...].astype(F32).T.astype(BF)

    def make_kv(r, _):
        sl = rows_of(r)
        tok = tok_ref[sl, :].astype(F32)
        normed = (tok * inv_rms(tok) * g1).astype(BF)
        nrm_ref[sl, :] = normed
        kv_ref[r, block(z, T), :] = nn(normed, kvw_ref[...]).astype(BF)
        return 0

    make_kv(0, 0)
    send_own(row_copies(0))
    lax.fori_loop(1, rows, make_kv, 0)

    seg = seg_ref[...]
    for i in range(2):
        cut_ref[i] = jnp.broadcast_to(
            jnp.sum((seg < i + 1).astype(F32), axis=1, keepdims=True), (rows, 128)
        ).astype(jnp.int32)
    for ref in (g2g_ref, dwst_ref, dwo_ref, wk_ref):
        ref[...] = jnp.zeros_like(ref)
    for k in range(max(n - 2, len(short))):
        if k < n - 2:
            gather_step(k)
        if k < len(short):
            collect_weights(len(short) + k + 1)
    for e in range(n):
        for base, ref in ((0, wst_ref), (H // 16, wo_ref)):
            for g in range(H // 16):
                for q in range(D // 128):
                    at = place((base + g) * (D // 128) + q, e)
                    ref[e * H + g * 16 : e * H + (g + 1) * 16, q * 128 : (q + 1) * 128] = (
                        we_ref[at : at + 16, :]
                    )
    loads[0].wait()

    def pick(all_t, route):
        acc = all_t[0:H]
        for e in range(1, n):
            acc = jnp.where(route == e, all_t[e * H : (e + 1) * H], acc)
        return acc

    def spread(first, second, e0, e1):
        parts = [jnp.where(e0 == e, first, jnp.where(e1 == e, second, 0.0)) for e in range(n)]
        return jnp.concatenate(parts, axis=0).astype(BF)

    def attend(i, r):
        sl, gl = rows_of(r), rows_of(i)
        q_all = nt(wst_ref[0:EH, :], nrm_ref[sl, :])
        e0, e1 = route_ref[z, r, 0:1, :], route_ref[z, r, 1:2, :]
        ga = (gate_ref[r, 0:1, :], gate_ref[r, 1:2, :])
        kv = kv_ref[r]
        kvt = kv.T
        c1, c2 = cut_ref[0, pl.ds(r, 1), :], cut_ref[1, pl.ds(r, 1), :]
        lane = lax.broadcasted_iota(jnp.int32, (seq, KV), 1)
        key_pos = lax.broadcasted_iota(jnp.int32, (seq, KV), 0)
        key_seg = H + (key_pos >= c1).astype(jnp.int32) + (key_pos >= c2).astype(jnp.int32)
        onehot = jnp.where(lane == key_seg, 1.0, 0.0)
        kaug = jnp.where(lane < H, kv.astype(F32), onehot).astype(BF)
        pos = z * T + lax.broadcasted_iota(jnp.int32, (KV - H, T), 1)
        q_seg = (pos >= c1[:, 0:1]).astype(jnp.int32) + (pos >= c2[:, 0:1]).astype(jnp.int32)
        sid = lax.broadcasted_iota(jnp.int32, (KV - H, T), 0)
        bias = jnp.where((sid < 3) & (sid != q_seg), -1e30, 0.0).astype(BF)
        vaug = jnp.concatenate([jnp.ones((16, seq), BF), kvt[H:, :]], axis=0)
        scale = LOG2E / math.sqrt(H)
        mixes = []
        for j, route in enumerate((e0, e1)):
            qt = pick(q_all, route).astype(BF)
            qt_ref[i, j] = qt
            s = nn(kaug, jnp.concatenate([qt, bias], axis=0))
            m = jnp.max(s, axis=0, keepdims=True)
            p = jnp.exp2(s * scale - m * scale).astype(BF)
            p_ref[i, j] = p
            av = nn(vaug, p)
            rinv = 1.0 / av[0:1]
            att = av[16:] * rinv
            rinv_ref[i, j : j + 1, :] = rinv
            att_ref[i, j] = att.astype(BF)
            mixes.append(att * ga[j])
        gt = spread(mixes[0], mixes[1], e0, e1)
        gt_ref[i] = gt
        res = tok_ref[sl, :].astype(F32) + nn(gt.T, wo_ref[...])
        res_ref[gl, :] = res
        sec = (res * inv_rms(res) * g2).astype(BF)
        sec_ref[gl, :] = sec
        sect_ref[:, gl] = sec.T
        cott_ref[:, gl] = cot_ref[sl, :].T

    def feed_forward(grp, fb):
        half = groups[grp] * T
        base = sum(groups[:grp]) * T
        MB = min(512, half)
        fs = pl.ds(fb * fblk, fblk)

        def feed(i, _):
            sl = pl.ds(pl.multiple_of(i * MB, MB), MB)
            al = pl.ds(pl.multiple_of(base + i * MB, T), MB)
            h = nn(sec_ref[sl, :], up_ref[:, fs])
            act, slope = gelu_both(h)
            act = act.astype(BF)
            act_ref[sl, :] = act
            hg = (nt(cot_ref[al, :], dn_ref[fs, :]) * slope).astype(BF)
            hg_ref[sl, :] = hg
            o = nn(act, dn_ref[fs, :])
            s = nt(hg, up_ref[:, fs])
            if fb == 0:
                oacc_ref[sl, :] = res_ref[sl, :] + o
                tg_ref[al, :] = s
            else:
                oacc_ref[sl, :] += o
                tg_ref[al, :] += s
            sites(i, half // MB)
            return 0

        lax.fori_loop(0, half // MB, feed, 0)

        a = nn(sect_ref[:, 0:half], hg_ref[0:half, :])
        b = nn(cott_ref[:, 0:half], act_ref[0:half, :])
        for t in range(fblk // 128):
            at = slice(t * D, (t + 1) * D)
            for k, v in ((2 * fb, a), (2 * fb + 1, b)):
                v = v[:, t * 128 : (t + 1) * 128]
                if grp > 0:
                    v = v + w_ref[k, at, :].astype(F32)
                w_ref[k, at, :] = v.astype(BF)
        site()

    def out_copy(r):
        slot = lax.rem(r, 2)
        return pltpu.make_async_copy(ost_ref.at[slot], out_hbm.at[rows_of(r)], ost_sem.at[slot])

    def grad_copy(r):
        return pltpu.make_async_copy(tg_ref.at[rows_of(r)], tg_hbm.at[rows_of(r)], tg_sem.at[r])

    def back(i, r):
        sl, gl = rows_of(r), rows_of(i)
        @pl.when(r >= 2)
        def _():
            out_copy(r - 2).wait()

        ost_ref[lax.rem(r, 2)] = oacc_ref[gl, :].astype(BF)
        out_copy(r).start()
        dres, dgain = rms_back(res_ref[gl, :], g2, tg_ref[sl, :])
        g2g_ref[...] += fold(dgain)
        rgrad = cot_ref[sl, :].astype(F32) + dres
        tg_ref[sl, :] = rgrad
        rb = rgrad.astype(BF)
        dwo_ref[...] += nn(gt_ref[i], rb)
        ag_all = nt(wo_ref[...], rb)
        e0, e1 = route_ref[z, r, 0:1, :], route_ref[z, r, 1:2, :]
        ga = (gate_ref[r, 0:1, :], gate_ref[r, 1:2, :])
        kv = kv_ref[r]
        kt = kv.T[0:H, :]
        zero = jnp.zeros((H, T), BF)
        kvg = None
        dqs = []
        for j, route in enumerate((e0, e1)):
            rinv = rinv_ref[i, j : j + 1, :]
            da = pick(ag_all, route) * (ga[j] * rinv)
            dd = jnp.sum(da * att_ref[i, j].astype(F32), axis=0, keepdims=True)
            dab = jnp.concatenate([zero, da.astype(BF)], axis=0)
            qb = jnp.concatenate([qt_ref[i, j] * (1.0 / math.sqrt(H)), zero], axis=0).astype(BF)
            p = p_ref[i, j]
            dp = nn(kv, dab)
            ds = (p.astype(F32) * (dp - dd)).astype(BF)
            part = nt(p, dab) + nt(ds, qb)
            kvg = part if kvg is None else kvg + part
            dqs.append(nn(kt, ds) * (1.0 / math.sqrt(H)))
        kvp_ref[r] = kvg.astype(BF)
        qg = spread(dqs[0], dqs[1], e0, e1)
        qg_ref[r] = qg
        dwst_ref[0:EH, :] += nn(qg, nrm_ref[sl, :])

    def key_part(r, direct=False):
        if direct:
            end_straight(r)
        else:
            sum_end(r)
        dwst_ref[EH : EH + KV, :] += nn(kvp_ref[r, block(z, T), :].T, nrm_ref[rows_of(r), :])

    def token_part(r):
        sl = rows_of(r)
        tok = tok_ref[sl, :].astype(F32)
        stack = jnp.concatenate([qg_ref[r], kvp_ref[r, block(z, T), :].T], axis=0)
        dtok, _ = rms_back(tok, g1, nn(stack.T, wst_ref[...]))
        tg_ref[sl, :] += dtok
        grad_copy(r).start()

    blocks = FF // fblk

    def put_experts():
        for ref, base in ((dwst_ref, 0), (dwo_ref, H)):
            for e in range(n):
                for g in range(H // 16):
                    tile = ref[e * H + g * 16 : e * H + (g + 1) * 16, :].astype(BF)
                    for q in range(D // 128):
                        at = place((base // 16 + g) * (D // 128) + q, e)
                        we_ref[at : at + 16, :] = tile[:, q * 128 : (q + 1) * 128]

    def experts_done():
        def tile(base, q):
            rows_at = [((base // 16 + g) * (D // 128) + q) * 16 for g in range(H // 16)]
            return jnp.concatenate([gae_ref[a : a + 16, :] for a in rows_at], axis=0).astype(F32)

        for q in range(D // 128):
            wq_out[:, q * 128 : (q + 1) * 128] = tile(0, q)
            wo_out[:, q * 128 : (q + 1) * 128] = tile(H, q)

    tall = wk_ref.shape[0] // (D // 128)

    def put_keys():
        summed = jnp.sum(wst_ref[...].astype(F32) * dwst_ref[...], axis=0, keepdims=True) / g1
        second_gain = jnp.sum(g2g_ref[...], axis=0, keepdims=True)
        gains = jnp.concatenate([summed, second_gain, jnp.zeros((14, D), F32)], axis=0).astype(BF)
        keys = dwst_ref[EH : EH + KV, :].astype(BF)
        for q in range(D // 128):
            wk_ref[q * tall : q * tall + KV, :] = keys[:, q * 128 : (q + 1) * 128]
            wk_ref[q * tall + KV : q * tall + KV + 16, :] = gains[:, q * 128 : (q + 1) * 128]

    def keys_done():
        for q in range(D // 128):
            lanes = slice(q * 128, (q + 1) * 128)
            kvw_out[lanes, :] = gak_ref[q * tall : q * tall + KV, :].astype(F32).T
            gain_ref[:, lanes] = gak_ref[q * tall + KV : q * tall + KV + 16, :].astype(F32)

    def result_copy(k):
        to = ddn_hbm if k % 2 else dup_hbm
        return pltpu.make_async_copy(ga_ref.at[k], to.at[k // 2], done_sem.at[k])

    chains = []
    for fb in range(blocks):
        chains.append(
            [
                chain(2 * fb + 1, w_ref.at[2 * fb], rr_ref.at[2 * fb], ga_ref.at[2 * fb],
                      straight, len(straight), result_copy(2 * fb).start),
                chain(2 * fb + 2, w_ref.at[2 * fb + 1], rr_ref.at[2 * fb + 1],
                      ga_ref.at[2 * fb + 1], turned, len(turned), result_copy(2 * fb + 1).start),
            ]
        )
    chains.append(
        [chain(2 * blocks + 1, we_ref, rre_ref, gae_ref, short, len(short) - 1, experts_done)]
    )
    chains.append([chain(2 * blocks + 2, wk_ref, rrk_ref, gak_ref, short, len(short), keys_done)])
    at_step = [None] * len(chains)
    count_down = [0] * len(chains)
    gathers, sums, pace = [], [], [0]

    def begin(c):
        at_step[c] = 0
        count_down[c] = chains[c][0][1][0]
        for one in chains[c]:
            one[0](0)

    def under_way(c):
        return at_step[c] is not None and at_step[c] < len(chains[c][0][1]) - 1

    def tick(weight):
        for c in range(len(chains)):
            if under_way(c):
                count_down[c] -= weight
                if count_down[c] <= 0:
                    at_step[c] += 1
                    count_down[c] = chains[c][0][1][at_step[c]]
                    for one in chains[c]:
                        one[0](at_step[c])

    def site(weight=1, adds=1):
        pace[0] += weight
        if gathers and pace[0] >= 4:
            pace[0] = 0
            gather_step(gathers.pop(0))
        for _ in range(adds):
            if sums:
                sum_step(*sums.pop(0))
        tick(weight)

    def sites(i, count, weight=1, adds=1):
        for k in range(count):
            @pl.when(i == k)
            def _():
                site(weight, adds)

    gathers += range(groups[0] + n - 2, rows + n - 2)

    for grp, rg in enumerate(groups):
        lo = sum(groups[:grp])
        hi = lo + rg

        while gathers and grp > 0 and gathers[0] <= hi + n - 3:
            gather_step(gathers.pop(0))

        def attend_row(i, _, grp=grp, lo=lo, rg=rg):
            if grp == 0:
                gather_step(i + n - 2)
            attend(i, lo + i)
            if grp > 0:
                sites(i, rg)
            return 0

        lax.fori_loop(0, rg, attend_row, 0)
        if grp == 0:
            loads[1].wait()
            loads[2].wait()
        for fb in range(blocks):
            feed_forward(grp, fb)
            if grp == len(groups) - 1:
                begin(fb)

        while sums:
            sum_step(*sums.pop(0))
        final = grp == len(groups) - 1
        top = hi - rg // 2 if final else hi
        lag = 2 if final else 4

        def back_row(i, _, lo=lo, rg=rg, top=top, lag=lag, final=final):
            back(i, lo + i)
            sum_step(i, lo, top, lag)
            if final:
                @pl.when(lo + i >= top)
                def _():
                    send_straight(lo + i)

            sites(i, rg, 2)
            return 0

        lax.fori_loop(0, rg, back_row, 0)
        sums += [(k, lo, top, lag) for k in range(rg, top - lo + lag * (n - 1))]

    weights_sent(False)
    put_experts()
    begin(blocks)
    early = rows - groups[-1]

    adds = -(-len(sums) // early)

    def finish_first(i, _):
        key_part(i)
        token_part(i)
        sites(i, early, 1, adds)
        return 0

    lax.fori_loop(0, early, finish_first, 0)

    def finish_keys(r, _):
        key_part(r)
        return 0

    def finish_straight(r, _):
        key_part(r, True)
        return 0

    lax.fori_loop(early, top, finish_keys, 0)
    lax.fori_loop(top, rows, finish_straight, 0)
    put_keys()
    begin(blocks + 1)
    site()

    def finish_second(i, _):
        token_part(early + i)
        sites(i, rows - early)
        return 0

    lax.fori_loop(0, rows - early, finish_second, 0)
    out_copy(rows - 2).wait()
    out_copy(rows - 1).wait()
    def all_sent(r, _):
        sent(row_copies(r))
        sums_sent(r)
        return 0

    lax.fori_loop(0, rows, all_sent, 0)
    while any(under_way(c) for c in range(len(chains))):
        tick(1)

    def grads_out(r, _):
        grad_copy(r).wait()
        return 0

    lax.fori_loop(0, rows, grads_out, 0)
    for parts in chains:
        for one in parts:
            one[2]()
    for k in range(2 * blocks):
        result_copy(k).wait()


def lay_kernel(
    up_ref, dn_ref, tg_ref, o_ref, gain_ref, kvw_ref, wq_ref, wo_ref,
    dup_ref, ddn_ref, tgo_ref, oo_ref, g1_ref, g2_ref, kvwo_ref, wqo_ref, woo_ref,
):
    for t in range(up_ref.shape[0]):
        lanes = slice(t * 128, (t + 1) * 128)
        dup_ref[:, lanes] = up_ref[t].astype(F32)
        ddn_ref[lanes, :] = dn_ref[t].T.astype(F32)
    tgo_ref[...] = tg_ref[...]
    oo_ref[...] = o_ref[...]

    @pl.when(pl.program_id(0) == 0)
    def _():
        g1_ref[...] = gain_ref[0:1, :]
        g2_ref[...] = gain_ref[1:2, :]
        kvwo_ref[...] = kvw_ref[...]
        wqo_ref[...] = wq_ref[...]
        woo_ref[...] = wo_ref[...]


def on_device(
    tokens, segments, routes, gate_values, gain_one, gain_two, kv_weight,
    query_weight, output_weight, up_weight, down_weight, out_grad,
):
    rows, T, D = tokens.shape
    H = query_weight.shape[2]
    n = lax.axis_size("expert")
    EH = n * H
    KV = 2 * H
    seq = n * T
    FF = up_weight.shape[1]
    toks = rows * T
    rg = rows // 2
    half = rg * T
    devices = n * lax.axis_size("group") * lax.axis_size("dp")
    fblk = 512 * max(1, devices // 128)
    tall = fblk * D // 128
    tall_e = n * 2 * H * D // 128
    tall_k = 2 * KV * D // 128
    tall_k = max(tall_k, 16 * devices)
    blocks = FF // fblk
    steps = (devices // n - 1).bit_length() + lax.axis_size("group") + n
    sds = jax.ShapeDtypeStruct
    vmem = pltpu.VMEM
    dma = pltpu.SemaphoreType.DMA

    route = jnp.transpose(routes, (0, 1, 3, 2))
    gate = jnp.transpose(gate_values, (0, 2, 1))
    whole = pl.BlockSpec(memory_space=pltpu.VMEM)
    hbm = pl.BlockSpec(memory_space=pl.ANY)
    out, tg, dup, ddn, gains, kvw_grad, wq_grad, wo_grad = pl.pallas_call(
        functools.partial(mega_kernel, n, rows, T, FF, fblk),
        out_shape=(
            sds((toks, D), BF), sds((toks, D), F32), sds((blocks, tall, 128), BF), sds((blocks, tall, 128), BF),
            sds((16, D), F32), sds((D, KV), F32), sds((H, D), F32), sds((H, D), F32),
        ),
        in_specs=[whole, hbm] + [whole] * 8 + [hbm, hbm],
        out_specs=[hbm] * 4 + [whole] * 4,
        scratch_shapes=[
            vmem((8, D), F32),
            vmem((EH + KV, D), F32),
            vmem((EH, D), F32),
            vmem((2 * blocks, tall, 128), BF),
            vmem((tall_e, 128), BF),
            vmem((tall_k, 128), BF),
            vmem((2 * blocks, tall, 128), BF),
            vmem((tall_e, 128), BF),
            vmem((tall_k, 128), BF),
            vmem((2 * blocks, tall, 128), BF),
            vmem((tall_e // n, 128), BF),
            vmem((tall_k, 128), BF),
            vmem((tall_e // n, 128), BF),
            vmem((toks, D), F32),
            vmem((2, T, D), BF),
            vmem((toks, D), BF),
            vmem((D, FF), BF),
            vmem((FF, D), BF),
            vmem((toks, D), BF),
            vmem((rows, seq, KV), BF),
            vmem((rows, seq, KV), BF),
            vmem((rows, n + 1, T, KV), BF),
            vmem((EH + KV, D), BF),
            vmem((EH, D), BF),
            vmem((2, rows, 128), jnp.int32),
            vmem((rg, 2, seq, T), BF),
            vmem((rg, 2, H, T), BF),
            vmem((rg, 2, H, T), BF),
            vmem((rg, 2, T), F32),
            vmem((rg, EH, T), BF),
            vmem((half, D), F32),
            vmem((half, D), BF),
            vmem((D, half), BF),
            vmem((D, half), BF),
            vmem((half, D), F32),
            vmem((half, fblk), BF),
            vmem((half, fblk), BF),
            vmem((rows, EH, T), BF),
            dma((3,)),
            dma((rows, n + 1)),
            dma((rows, n)),
            dma((rows, n)),
            dma((rows, n + 1)),
            dma((2 * blocks + 3, 2 * steps)),
            dma((2 * blocks + 3, 2 * steps)),
            dma((2 * blocks,)),
            dma((2,)),
            dma((rows,)),
        ],
        compiler_params=pltpu.CompilerParams(
            vmem_limit_bytes=VMEM_LIMIT, collective_id=0, has_side_effects=True
        ),
    )(
        tokens.reshape(toks, D), out_grad.reshape(toks, D), segments, route, gate,
        gain_one.reshape(1, D), gain_two.reshape(1, D), kv_weight, query_weight[0].T,
        output_weight[0], up_weight, down_weight,
    )
    parts = 2
    tiles = FF // 128
    step = tiles // parts
    bt = toks // parts
    row_block = pl.BlockSpec((bt, D), lambda i: (i, 0))
    tile_block = pl.BlockSpec((step, D, 128), lambda i: (i, 0, 0))

    def full(a):
        return pl.BlockSpec(a.shape, lambda i: (0, 0))

    gain = sds((1, D), F32)
    small = (gain, gain, kvw_grad, wq_grad, wo_grad)
    dup, ddn, tg, out, gain_one_grad, gain_two_grad, kvw_grad, wq_grad, wo_grad = pl.pallas_call(
        lay_kernel,
        grid=(parts,),
        out_shape=(
            sds((D, FF), F32), sds((FF, D), F32), sds((toks, D), F32), sds((toks, D), BF),
        ) + tuple(sds(a.shape, F32) for a in small),
        in_specs=[tile_block, tile_block, row_block, row_block, full(gains)]
        + [full(a) for a in small[2:]],
        out_specs=[
            pl.BlockSpec((D, step * 128), lambda i: (0, i)),
            pl.BlockSpec((step * 128, D), lambda i: (i, 0)),
            row_block, row_block,
        ] + [full(a) for a in small],
        compiler_params=pltpu.CompilerParams(vmem_limit_bytes=VMEM_LIMIT),
    )(
        dup.reshape(tiles, D, 128), ddn.reshape(tiles, D, 128), tg, out, gains,
        kvw_grad, wq_grad, wo_grad,
    )
    return (
        out.reshape(tokens.shape),
        tg.reshape(tokens.shape),
        gain_one_grad.reshape(D),
        gain_two_grad.reshape(D),
        kvw_grad,
        wq_grad.T[None],
        wo_grad[None],
        dup,
        ddn,
    )


def solution(mesh):
    rows = P(("group", "dp"), "expert", None)
    in_specs = (
        rows,
        P(("group", "dp"), None),
        P(None, ("group", "dp"), None, None),
        rows,
        P(), P(), P(),
        P("expert", None, None),
        P("expert", None, None),
        P(), P(),
        rows,
    )
    out_specs = (
        rows, rows, P(), P(), P(),
        P("expert", None, None),
        P("expert", None, None),
        P(), P(),
    )
    return jax.shard_map(
        on_device, mesh=mesh, in_specs=in_specs, out_specs=out_specs, check_vma=False
    )
```

```python
import functools
import math

import jax
import jax.numpy as jnp
from jax import lax
from jax.experimental import pallas as pl
from jax.experimental.pallas import tpu as pltpu
from jax.sharding import PartitionSpec as P

EPS = 1e-06
F32 = jnp.float32
BF = jnp.bfloat16
LOG2E = 1.4426950408889634
VMEM_LIMIT = 66_000_000


def nn(a, b):
    return lax.dot_general(a, b, (((1,), (0,)), ((), ())), preferred_element_type=F32)


def nt(a, b):
    return lax.dot_general(a, b, (((1,), (1,)), ((), ())), preferred_element_type=F32)


def gelu_both(x):
    c0 = math.sqrt(2.0 / math.pi)
    c1 = 0.044715 * c0
    x2 = x * x
    t = jnp.tanh(x * (c0 + c1 * x2))
    h = 0.5 + 0.5 * t
    act = x * h
    slope = h + (act - act * h) * (2.0 * c0 + (6.0 * c1) * x2)
    return act, slope


def inv_rms(x):
    return lax.rsqrt(jnp.mean(x * x, axis=-1, keepdims=True) + EPS)


def rms_back(x, gain, dy):
    inv = inv_rms(x)
    xn = x * inv
    gdy = gain * dy
    dx = inv * (gdy - xn * jnp.mean(xn * gdy, axis=-1, keepdims=True))
    return dx, dy * xn


def fold(x):
    return jnp.sum(x.reshape(x.shape[0] // 8, 8, x.shape[1]), axis=0)


def remote(src, dst, send, recv, where):
    return pltpu.make_async_remote_copy(
        src_ref=src, dst_ref=dst, send_sem=send, recv_sem=recv,
        device_id=where, device_id_type=pl.DeviceIdType.MESH,
    )


def mega_kernel(
    n, rows, T, FF, fblk,
    tok_ref, cot_hbm, seg_ref, route_ref, gate_ref, g1_ref, g2_ref,
    kvw_ref, wq_in, wo_in, up_hbm, dn_hbm,
    out_hbm, tg_hbm, dup_hbm, ddn_hbm, gain_ref, kvw_out, wq_out, wo_out,
    g2g_ref, dwst_ref, dwo_ref, w_ref, we_ref, wk_ref, rr_ref, rre_ref, rrk_ref,
    ga_ref, gae_ref, gak_ref, own_ref, tg_ref, ost_ref,
    cot_ref, up_ref, dn_ref, nrm_ref, kv_ref, kvp_ref, rcv_ref, wst_ref, wo_ref,
    cut_ref, p_ref, qt_ref, att_ref, rinv_ref, gt_ref, res_ref, sec_ref,
    sect_ref, cott_ref, oacc_ref, act_ref, hg_ref, qg_ref,
    load_sem, gsend, grecv, rsend, rrecv, csend, crecv, done_sem,
    ost_sem, tg_sem,
):
    D = tok_ref.shape[1]
    H = wo_in.shape[0]
    EH = n * H
    KV = 2 * H
    seq = n * T
    groups = (rows // 4, rows // 4, rows // 2)
    z = lax.axis_index("expert")
    has_left, has_right = z > 0, z < n - 1
    left, right = {"expert": lax.rem(z + n - 1, n)}, {"expert": lax.rem(z + 1, n)}

    loads = [
        pltpu.make_async_copy(a, b, load_sem.at[i])
        for i, (a, b) in enumerate(((cot_hbm, cot_ref), (up_hbm, up_ref), (dn_hbm, dn_ref)))
    ]
    for c in loads:
        c.start()

    barrier = pltpu.get_barrier_semaphore()
    peers = 0
    for axis in ("group", "dp", "expert"):
        size = lax.axis_size(axis)
        for d in range(1, size):
            pl.semaphore_signal(
                barrier, inc=1, device_id={axis: lax.rem(lax.axis_index(axis) + d, size)},
                device_id_type=pl.DeviceIdType.MESH,
            )
            peers += 1
    pl.semaphore_wait(barrier, peers)

    def rows_of(r):
        return pl.ds(pl.multiple_of(r * T, T), T)

    def block(b, size):
        return pl.ds(pl.multiple_of(b * size, size), size)

    def kv_copy(r, b, slot, where):
        at = kv_ref.at[r, block(b, T)]
        return remote(at, at, gsend.at[r, slot], grecv.at[r, b], where)

    def pass_on(d, copies):
        @pl.when(z - d >= 0)
        def _():
            for c in copies(z - d, z - d, right):
                c.wait_recv()

            @pl.when(has_right)
            def _():
                for c in copies(z - d, z - d, right):
                    c.start()

        @pl.when(z + d <= n - 1)
        def _():
            for c in copies(z + d, z + d, left):
                c.wait_recv()

            @pl.when(has_left)
            def _():
                for c in copies(z + d, z + d, left):
                    c.start()

    def send_own(copies):
        @pl.when(has_right)
        def _():
            for c in copies(z, z, right):
                c.start()

        @pl.when(has_left)
        def _():
            for c in copies(z, n, left):
                c.start()

    def sent(copies):
        for b in range(n):
            goes = ((b <= z) & has_right) | ((b > z) & has_left)

            @pl.when(goes)
            def _(b=b):
                for c in copies(b, b, right):
                    c.wait_send()

        @pl.when(has_left)
        def _():
            for c in copies(z, n, left):
                c.wait_send()

    def row_copies(r):
        return lambda b, slot, where: (kv_copy(r, b, slot, where),)

    def gather_step(k):
        @pl.when(k + 1 < rows)
        def _():
            send_own(row_copies(k + 1))

        for d in range(1, n):
            r = k - d + 1

            @pl.when((r >= 0) & (r < rows))
            def _(r=r, d=d):
                pass_on(d, row_copies(r))

    def sum_copy(r, b, slot, where):
        return remote(
            kvp_ref.at[r, block(b, T)], rcv_ref.at[r, slot], rsend.at[r, b], rrecv.at[r, slot], where
        )

    def sum_block(r, b, slot, first):
        @pl.when(jnp.logical_not(first))
        def _():
            sum_copy(r, b, slot, right).wait_recv()
            at = block(b, T)
            kvp_ref[r, at, :] = (
                kvp_ref[r, at, :].astype(F32) + rcv_ref[r, slot].astype(F32)
            ).astype(BF)

    def sum_step(k, lo, hi, lag):
        r1 = k - lag * z + lo

        @pl.when((r1 >= lo) & (r1 < hi))
        def _():
            def go(c, _):
                b = n - 1 - c
                sum_block(r1, b, b, z == 0)
                sum_copy(r1, b, b, right).start()
                return 0

            lax.fori_loop(0, n - 1 - z, go, 0)

        r2 = k - lag * (n - 1 - z) + lo

        @pl.when((r2 >= lo) & (r2 < hi))
        def _():
            def go(b, _):
                sum_block(r2, b, b, z == n - 1)
                sum_copy(r2, b, jnp.where(b == z - 1, n, b), left).start()
                return 0

            lax.fori_loop(0, z, go, 0)

    def sum_end(r):
        @pl.when(has_left)
        def _():
            sum_block(r, z, z, False)

        @pl.when(has_right)
        def _():
            sum_block(r, z, n, False)

    def straight_copy(r, b, source):
        return remote(
            kvp_ref.at[r, block(b, T)], rcv_ref.at[r, source], rsend.at[r, b],
            rrecv.at[r, source], {"expert": b},
        )

    def send_straight(r):
        for d in range(1, n):
            straight_copy(r, lax.rem(z + d, n), z).start()

    def end_straight(r):
        at = block(z, T)
        total = kvp_ref[r, at, :].astype(F32)
        for d in range(1, n):
            source = lax.rem(z + d, n)
            straight_copy(r, source, source).wait_recv()
            total = total + rcv_ref[r, source].astype(F32)
        kvp_ref[r, at, :] = total.astype(BF)

    def sums_sent(r):
        for b in range(n):
            @pl.when(z != b)
            def _(b=b):
                sum_copy(r, b, b, right).wait_send()

    def pair(axis, b, wait):
        return (axis, 2**b, 2, wait)

    def line(axis, wait):
        return (axis, 1, lax.axis_size(axis), wait)

    def pairs(axis, waits):
        count = (lax.axis_size(axis) - 1).bit_length()
        return [pair(axis, b, waits[min(b, len(waits) - 1)]) for b in range(count)]

    def digit_of(stage):
        axis, stride, radix, _ = stage
        return lax.rem(lax.axis_index(axis) // stride, radix)

    def peer_of(stage, d):
        axis, stride, radix, _ = stage
        digit = digit_of(stage)
        other = lax.rem(digit + d, radix)
        return other, {axis: lax.axis_index(axis) + (other - digit) * stride}

    def chain(number, w, rr, ga, stages, collect, done):
        deep = len(stages)
        total = w.shape[0] if w is not None else ga.shape[0]
        kept = ga.shape[0]
        sem_at = [0]
        for stage in stages:
            sem_at.append(sem_at[-1] + stage[2] - 1)

        def size_of(s, size):
            for k in range(s):
                size = size // stages[k][2]
            return size

        def start_of(s, size):
            off = 0
            for k in range(s):
                size = size // stages[k][2]
                off = off + digit_of(stages[k]) * size
            return off

        def part(ref, off, size):
            return ref.at[pl.ds(pl.multiple_of(off, 16), size)]

        def slot(s, d):
            return total - size_of(s, total) + (d - 1) * size_of(s + 1, total)

        def reduce_copies(s):
            size = size_of(s + 1, total)
            for d in range(1, stages[s][2]):
                other, where = peer_of(stages[s], d)
                yield remote(
                    part(w, start_of(s, total) + other * size, size), part(rr, slot(s, d), size),
                    csend.at[number, sem_at[s] + d - 1], crecv.at[number, sem_at[s] + d - 1], where,
                )

        def collect_copies(s):
            at = part(ga, start_of(s + 1, kept), size_of(s + 1, kept))
            for d in range(1, stages[s][2]):
                _, where = peer_of(stages[s], d)
                k = sem_at[deep] + sem_at[s] + d - 1
                yield remote(at, at, csend.at[number, k], crecv.at[number, k], where)

        def own_part():
            return pl.ds(pl.multiple_of(start_of(collect, kept), 16), size_of(collect, kept))

        def advance(u, only_send=False):
            if 0 < u <= deep and not only_send:
                s = u - 1
                size = size_of(u, total)
                for c in reduce_copies(s):
                    c.wait_recv()
                mine = pl.ds(pl.multiple_of(start_of(u, total), 16), size)
                added = w[mine, :].astype(F32)
                for d in range(1, stages[s][2]):
                    added = added + rr[pl.ds(slot(s, d), size), :].astype(F32)
                if u < deep:
                    w[mine, :] = added.astype(BF)
                else:
                    ga[own_part(), :] = added.astype(BF)
            if u < deep:
                for c in reduce_copies(u):
                    c.start()
            if deep < u <= deep + collect:
                for c in collect_copies(collect - (u - deep)):
                    c.wait_recv()
            if deep <= u < deep + collect:
                for c in collect_copies(collect - 1 - (u - deep)):
                    c.start()
            if u == deep + collect:
                done()

        def sent_all(reduced=True):
            for s in range(deep if reduced else 0):
                for c in reduce_copies(s):
                    c.wait_send()
            for s in range(collect):
                for c in collect_copies(s):
                    c.wait_send()

        waits = [stage[3] for stage in stages] + [stage[3] for stage in stages[:collect][::-1]] + [0]
        return advance, waits, sent_all, own_part

    core = pairs("dp", (1, 3))
    straight = core + pairs("group", (3, 2)) + pairs("expert", (2, 3))
    turned = core + pairs("group", (2, 3))[::-1] + pairs("expert", (2, 3))
    short = core + [line("group", 3), line("expert", 3)]
    pieces = (2 * H // 16) * (D // 128)
    each = pieces // (lax.axis_size("dp") * lax.axis_size("group"))

    def place(p, e):
        return ((p // each * n + e) * each + p % each) * 16

    g1 = g1_ref[...]
    g2 = g2_ref[...]
    for src, base in ((wq_in, 0), (wo_in, H // 16)):
        for g in range(H // 16):
            for q in range(D // 128):
                at = ((base + g) * (D // 128) + q) * 16
                own_ref[at : at + 16, :] = src[g * 16 : (g + 1) * 16, q * 128 : (q + 1) * 128]
    collect_weights, _, weights_sent, weights_part = chain(
        0, None, None, we_ref, short, len(short), lambda: None
    )
    shard = sum(digit_of(stage) * 2 ** (len(core) - 1 - k) for k, stage in enumerate(core))
    shard = shard * lax.axis_size("group") + lax.axis_index("group")
    we_ref[weights_part(), :] = own_ref[pl.ds(pl.multiple_of(shard * each * 16, 16), each * 16), :]
    collect_weights(len(short), True)
    wst_ref[EH : EH + KV, :] = kvw_ref[...].astype(F32).T.astype(BF)

    def make_kv(r, _):
        sl = rows_of(r)
        tok = tok_ref[sl, :].astype(F32)
        normed = (tok * inv_rms(tok) * g1).astype(BF)
        nrm_ref[sl, :] = normed
        kv_ref[r, block(z, T), :] = nn(normed, kvw_ref[...]).astype(BF)
        return 0

    make_kv(0, 0)
    send_own(row_copies(0))
    lax.fori_loop(1, rows, make_kv, 0)

    seg = seg_ref[...]
    for i in range(2):
        cut_ref[i] = jnp.broadcast_to(
            jnp.sum((seg < i + 1).astype(F32), axis=1, keepdims=True), (rows, 128)
        ).astype(jnp.int32)
    for ref in (g2g_ref, dwst_ref, dwo_ref, wk_ref):
        ref[...] = jnp.zeros_like(ref)
    for k in range(max(n - 2, len(short))):
        if k < n - 2:
            gather_step(k)
        if k < len(short):
            collect_weights(len(short) + k + 1)
    for e in range(n):
        for base, ref in ((0, wst_ref), (H // 16, wo_ref)):
            for g in range(H // 16):
                for q in range(D // 128):
                    at = place((base + g) * (D // 128) + q, e)
                    ref[e * H + g * 16 : e * H + (g + 1) * 16, q * 128 : (q + 1) * 128] = (
                        we_ref[at : at + 16, :]
                    )
    loads[0].wait()

    def pick(all_t, route):
        acc = all_t[0:H]
        for e in range(1, n):
            acc = jnp.where(route == e, all_t[e * H : (e + 1) * H], acc)
        return acc

    def spread(first, second, e0, e1):
        parts = [jnp.where(e0 == e, first, jnp.where(e1 == e, second, 0.0)) for e in range(n)]
        return jnp.concatenate(parts, axis=0).astype(BF)

    def attend(i, r):
        sl, gl = rows_of(r), rows_of(i)
        q_all = nt(wst_ref[0:EH, :], nrm_ref[sl, :])
        e0, e1 = route_ref[z, r, 0:1, :], route_ref[z, r, 1:2, :]
        ga = (gate_ref[r, 0:1, :], gate_ref[r, 1:2, :])
        kv = kv_ref[r]
        kvt = kv.T
        c1, c2 = cut_ref[0, pl.ds(r, 1), :], cut_ref[1, pl.ds(r, 1), :]
        lane = lax.broadcasted_iota(jnp.int32, (seq, KV), 1)
        key_pos = lax.broadcasted_iota(jnp.int32, (seq, KV), 0)
        key_seg = H + (key_pos >= c1).astype(jnp.int32) + (key_pos >= c2).astype(jnp.int32)
        onehot = jnp.where(lane == key_seg, 1.0, 0.0)
        kaug = jnp.where(lane < H, kv.astype(F32), onehot).astype(BF)
        pos = z * T + lax.broadcasted_iota(jnp.int32, (KV - H, T), 1)
        q_seg = (pos >= c1[:, 0:1]).astype(jnp.int32) + (pos >= c2[:, 0:1]).astype(jnp.int32)
        sid = lax.broadcasted_iota(jnp.int32, (KV - H, T), 0)
        bias = jnp.where((sid < 3) & (sid != q_seg), -1e30, 0.0).astype(BF)
        vaug = jnp.concatenate([jnp.ones((16, seq), BF), kvt[H:, :]], axis=0)
        scale = LOG2E / math.sqrt(H)
        mixes = []
        for j, route in enumerate((e0, e1)):
            qt = pick(q_all, route).astype(BF)
            qt_ref[i, j] = qt
            s = nn(kaug, jnp.concatenate([qt, bias], axis=0))
            m = jnp.max(s, axis=0, keepdims=True)
            p = jnp.exp2(s * scale - m * scale).astype(BF)
            p_ref[i, j] = p
            av = nn(vaug, p)
            rinv = 1.0 / av[0:1]
            att = av[16:] * rinv
            rinv_ref[i, j : j + 1, :] = rinv
            att_ref[i, j] = att.astype(BF)
            mixes.append(att * ga[j])
        gt = spread(mixes[0], mixes[1], e0, e1)
        gt_ref[i] = gt
        res = tok_ref[sl, :].astype(F32) + nn(gt.T, wo_ref[...])
        res_ref[gl, :] = res
        sec = (res * inv_rms(res) * g2).astype(BF)
        sec_ref[gl, :] = sec
        sect_ref[:, gl] = sec.T
        cott_ref[:, gl] = cot_ref[sl, :].T

    def feed_forward(grp, fb):
        half = groups[grp] * T
        base = sum(groups[:grp]) * T
        MB = min(512, half)
        fs = pl.ds(fb * fblk, fblk)

        def feed(i, _):
            sl = pl.ds(pl.multiple_of(i * MB, MB), MB)
            al = pl.ds(pl.multiple_of(base + i * MB, T), MB)
            h = nn(sec_ref[sl, :], up_ref[:, fs])
            act, slope = gelu_both(h)
            act = act.astype(BF)
            act_ref[sl, :] = act
            hg = (nt(cot_ref[al, :], dn_ref[fs, :]) * slope).astype(BF)
            hg_ref[sl, :] = hg
            o = nn(act, dn_ref[fs, :])
            s = nt(hg, up_ref[:, fs])
            if fb == 0:
                oacc_ref[sl, :] = res_ref[sl, :] + o
                tg_ref[al, :] = s
            else:
                oacc_ref[sl, :] += o
                tg_ref[al, :] += s
            sites(i, half // MB)
            return 0

        lax.fori_loop(0, half // MB, feed, 0)

        a = nn(sect_ref[:, 0:half], hg_ref[0:half, :])
        b = nn(cott_ref[:, 0:half], act_ref[0:half, :])
        for t in range(fblk // 128):
            at = slice(t * D, (t + 1) * D)
            for k, v in ((2 * fb, a), (2 * fb + 1, b)):
                v = v[:, t * 128 : (t + 1) * 128]
                if grp > 0:
                    v = v + w_ref[k, at, :].astype(F32)
                w_ref[k, at, :] = v.astype(BF)
        site()

    def out_copy(r):
        slot = lax.rem(r, 2)
        return pltpu.make_async_copy(ost_ref.at[slot], out_hbm.at[rows_of(r)], ost_sem.at[slot])

    def grad_copy(r):
        return pltpu.make_async_copy(tg_ref.at[rows_of(r)], tg_hbm.at[rows_of(r)], tg_sem.at[r])

    def back(i, r):
        sl, gl = rows_of(r), rows_of(i)
        @pl.when(r >= 2)
        def _():
            out_copy(r - 2).wait()

        ost_ref[lax.rem(r, 2)] = oacc_ref[gl, :].astype(BF)
        out_copy(r).start()
        dres, dgain = rms_back(res_ref[gl, :], g2, tg_ref[sl, :])
        g2g_ref[...] += fold(dgain)
        rgrad = cot_ref[sl, :].astype(F32) + dres
        tg_ref[sl, :] = rgrad
        rb = rgrad.astype(BF)
        dwo_ref[...] += nn(gt_ref[i], rb)
        ag_all = nt(wo_ref[...], rb)
        e0, e1 = route_ref[z, r, 0:1, :], route_ref[z, r, 1:2, :]
        ga = (gate_ref[r, 0:1, :], gate_ref[r, 1:2, :])
        kv = kv_ref[r]
        kt = kv.T[0:H, :]
        zero = jnp.zeros((H, T), BF)
        kvg = None
        dqs = []
        for j, route in enumerate((e0, e1)):
            rinv = rinv_ref[i, j : j + 1, :]
            da = pick(ag_all, route) * (ga[j] * rinv)
            dd = jnp.sum(da * att_ref[i, j].astype(F32), axis=0, keepdims=True)
            dab = jnp.concatenate([zero, da.astype(BF)], axis=0)
            qb = jnp.concatenate([qt_ref[i, j] * (1.0 / math.sqrt(H)), zero], axis=0).astype(BF)
            p = p_ref[i, j]
            dp = nn(kv, dab)
            ds = (p.astype(F32) * (dp - dd)).astype(BF)
            part = nt(p, dab) + nt(ds, qb)
            kvg = part if kvg is None else kvg + part
            dqs.append(nn(kt, ds) * (1.0 / math.sqrt(H)))
        kvp_ref[r] = kvg.astype(BF)
        qg = spread(dqs[0], dqs[1], e0, e1)
        qg_ref[r] = qg
        dwst_ref[0:EH, :] += nn(qg, nrm_ref[sl, :])

    def key_part(r, direct=False):
        if direct:
            end_straight(r)
        else:
            sum_end(r)
        dwst_ref[EH : EH + KV, :] += nn(kvp_ref[r, block(z, T), :].T, nrm_ref[rows_of(r), :])

    def token_part(r):
        sl = rows_of(r)
        tok = tok_ref[sl, :].astype(F32)
        stack = jnp.concatenate([qg_ref[r], kvp_ref[r, block(z, T), :].T], axis=0)
        dtok, _ = rms_back(tok, g1, nn(stack.T, wst_ref[...]))
        tg_ref[sl, :] += dtok
        grad_copy(r).start()

    blocks = FF // fblk

    def put_experts():
        for ref, base in ((dwst_ref, 0), (dwo_ref, H)):
            for e in range(n):
                for g in range(H // 16):
                    tile = ref[e * H + g * 16 : e * H + (g + 1) * 16, :].astype(BF)
                    for q in range(D // 128):
                        at = place((base // 16 + g) * (D // 128) + q, e)
                        we_ref[at : at + 16, :] = tile[:, q * 128 : (q + 1) * 128]

    def experts_done():
        def tile(base, q):
            rows_at = [((base // 16 + g) * (D // 128) + q) * 16 for g in range(H // 16)]
            return jnp.concatenate([gae_ref[a : a + 16, :] for a in rows_at], axis=0).astype(F32)

        for q in range(D // 128):
            wq_out[:, q * 128 : (q + 1) * 128] = tile(0, q)
            wo_out[:, q * 128 : (q + 1) * 128] = tile(H, q)

    tall = wk_ref.shape[0] // (D // 128)

    def put_keys():
        summed = jnp.sum(wst_ref[...].astype(F32) * dwst_ref[...], axis=0, keepdims=True) / g1
        second_gain = jnp.sum(g2g_ref[...], axis=0, keepdims=True)
        gains = jnp.concatenate([summed, second_gain, jnp.zeros((14, D), F32)], axis=0).astype(BF)
        keys = dwst_ref[EH : EH + KV, :].astype(BF)
        for q in range(D // 128):
            wk_ref[q * tall : q * tall + KV, :] = keys[:, q * 128 : (q + 1) * 128]
            wk_ref[q * tall + KV : q * tall + KV + 16, :] = gains[:, q * 128 : (q + 1) * 128]

    def keys_done():
        for q in range(D // 128):
            lanes = slice(q * 128, (q + 1) * 128)
            kvw_out[lanes, :] = gak_ref[q * tall : q * tall + KV, :].astype(F32).T
            gain_ref[:, lanes] = gak_ref[q * tall + KV : q * tall + KV + 16, :].astype(F32)

    def result_copy(k):
        to = ddn_hbm if k % 2 else dup_hbm
        return pltpu.make_async_copy(ga_ref.at[k], to.at[k // 2], done_sem.at[k])

    chains = []
    for fb in range(blocks):
        chains.append(
            [
                chain(2 * fb + 1, w_ref.at[2 * fb], rr_ref.at[2 * fb], ga_ref.at[2 * fb],
                      straight, len(straight), result_copy(2 * fb).start),
                chain(2 * fb + 2, w_ref.at[2 * fb + 1], rr_ref.at[2 * fb + 1],
                      ga_ref.at[2 * fb + 1], turned, len(turned), result_copy(2 * fb + 1).start),
            ]
        )
    chains.append(
        [chain(2 * blocks + 1, we_ref, rre_ref, gae_ref, short, len(short) - 1, experts_done)]
    )
    chains.append([chain(2 * blocks + 2, wk_ref, rrk_ref, gak_ref, short, len(short), keys_done)])
    at_step = [None] * len(chains)
    count_down = [0] * len(chains)
    gathers, sums, pace = [], [], [0]

    def begin(c):
        at_step[c] = 0
        count_down[c] = chains[c][0][1][0]
        for one in chains[c]:
            one[0](0)

    def under_way(c):
        return at_step[c] is not None and at_step[c] < len(chains[c][0][1]) - 1

    def tick(weight):
        for c in range(len(chains)):
            if under_way(c):
                count_down[c] -= weight
                if count_down[c] <= 0:
                    at_step[c] += 1
                    count_down[c] = chains[c][0][1][at_step[c]]
                    for one in chains[c]:
                        one[0](at_step[c])

    def site(weight=1, adds=1):
        pace[0] += weight
        if gathers and pace[0] >= 4:
            pace[0] = 0
            gather_step(gathers.pop(0))
        for _ in range(adds):
            if sums:
                sum_step(*sums.pop(0))
        tick(weight)

    def sites(i, count, weight=1, adds=1):
        for k in range(count):
            @pl.when(i == k)
            def _():
                site(weight, adds)

    gathers += range(groups[0] + n - 2, rows + n - 2)

    for grp, rg in enumerate(groups):
        lo = sum(groups[:grp])
        hi = lo + rg

        while gathers and grp > 0 and gathers[0] <= hi + n - 3:
            gather_step(gathers.pop(0))

        def attend_row(i, _, grp=grp, lo=lo, rg=rg):
            if grp == 0:
                gather_step(i + n - 2)
            attend(i, lo + i)
            if grp > 0:
                sites(i, rg)
            return 0

        lax.fori_loop(0, rg, attend_row, 0)
        if grp == 0:
            loads[1].wait()
            loads[2].wait()
        for fb in range(blocks):
            feed_forward(grp, fb)
            if grp == len(groups) - 1:
                begin(fb)

        while sums:
            sum_step(*sums.pop(0))
        final = grp == len(groups) - 1
        top = hi - rg // 2 if final else hi
        lag = 1 if final else 4

        def back_row(i, _, lo=lo, rg=rg, top=top, lag=lag, final=final):
            back(i, lo + i)
            sum_step(i, lo, top, lag)
            if final:
                @pl.when(lo + i >= top)
                def _():
                    send_straight(lo + i)

            sites(i, rg, 2)
            return 0

        lax.fori_loop(0, rg, back_row, 0)
        sums += [(k, lo, top, lag) for k in range(rg, top - lo + lag * (n - 1))]

    weights_sent(False)
    put_experts()
    begin(blocks)
    early = rows - groups[-1]

    adds = -(-len(sums) // early)

    def finish_first(i, _):
        key_part(i)
        token_part(i)
        sites(i, early, 1, adds)
        return 0

    lax.fori_loop(0, early, finish_first, 0)

    def finish_keys(r, _):
        key_part(r)
        return 0

    def finish_straight(r, _):
        key_part(r, True)
        return 0

    lax.fori_loop(early, top, finish_keys, 0)
    lax.fori_loop(top, rows, finish_straight, 0)
    put_keys()
    begin(blocks + 1)
    site()

    def finish_second(i, _):
        token_part(early + i)
        sites(i, rows - early)
        return 0

    lax.fori_loop(0, rows - early, finish_second, 0)
    out_copy(rows - 2).wait()
    out_copy(rows - 1).wait()
    def all_sent(r, _):
        sent(row_copies(r))
        sums_sent(r)
        return 0

    lax.fori_loop(0, rows, all_sent, 0)
    while any(under_way(c) for c in range(len(chains))):
        tick(1)

    def grads_out(r, _):
        grad_copy(r).wait()
        return 0

    lax.fori_loop(0, rows, grads_out, 0)
    for parts in chains:
        for one in parts:
            one[2]()
    for k in range(2 * blocks):
        result_copy(k).wait()


def lay_kernel(
    up_ref, dn_ref, tg_ref, o_ref, gain_ref, kvw_ref, wq_ref, wo_ref,
    dup_ref, ddn_ref, tgo_ref, oo_ref, g1_ref, g2_ref, kvwo_ref, wqo_ref, woo_ref,
):
    for t in range(up_ref.shape[0]):
        lanes = slice(t * 128, (t + 1) * 128)
        dup_ref[:, lanes] = up_ref[t].astype(F32)
        ddn_ref[lanes, :] = dn_ref[t].T.astype(F32)
    tgo_ref[...] = tg_ref[...]
    oo_ref[...] = o_ref[...]

    @pl.when(pl.program_id(0) == 0)
    def _():
        g1_ref[...] = gain_ref[0:1, :]
        g2_ref[...] = gain_ref[1:2, :]
        kvwo_ref[...] = kvw_ref[...]
        wqo_ref[...] = wq_ref[...]
        woo_ref[...] = wo_ref[...]


def on_device(
    tokens, segments, routes, gate_values, gain_one, gain_two, kv_weight,
    query_weight, output_weight, up_weight, down_weight, out_grad,
):
    rows, T, D = tokens.shape
    H = query_weight.shape[2]
    n = lax.axis_size("expert")
    EH = n * H
    KV = 2 * H
    seq = n * T
    FF = up_weight.shape[1]
    toks = rows * T
    rg = rows // 2
    half = rg * T
    devices = n * lax.axis_size("group") * lax.axis_size("dp")
    fblk = 512 * max(1, devices // 128)
    tall = fblk * D // 128
    tall_e = n * 2 * H * D // 128
    tall_k = 2 * KV * D // 128
    tall_k = max(tall_k, 16 * devices)
    blocks = FF // fblk
    steps = (devices // n - 1).bit_length() + lax.axis_size("group") + n
    sds = jax.ShapeDtypeStruct
    vmem = pltpu.VMEM
    dma = pltpu.SemaphoreType.DMA

    route = jnp.transpose(routes, (0, 1, 3, 2))
    gate = jnp.transpose(gate_values, (0, 2, 1))
    whole = pl.BlockSpec(memory_space=pltpu.VMEM)
    hbm = pl.BlockSpec(memory_space=pl.ANY)
    out, tg, dup, ddn, gains, kvw_grad, wq_grad, wo_grad = pl.pallas_call(
        functools.partial(mega_kernel, n, rows, T, FF, fblk),
        out_shape=(
            sds((toks, D), BF), sds((toks, D), F32), sds((blocks, tall, 128), BF), sds((blocks, tall, 128), BF),
            sds((16, D), F32), sds((D, KV), F32), sds((H, D), F32), sds((H, D), F32),
        ),
        in_specs=[whole, hbm] + [whole] * 8 + [hbm, hbm],
        out_specs=[hbm] * 4 + [whole] * 4,
        scratch_shapes=[
            vmem((8, D), F32),
            vmem((EH + KV, D), F32),
            vmem((EH, D), F32),
            vmem((2 * blocks, tall, 128), BF),
            vmem((tall_e, 128), BF),
            vmem((tall_k, 128), BF),
            vmem((2 * blocks, tall, 128), BF),
            vmem((tall_e, 128), BF),
            vmem((tall_k, 128), BF),
            vmem((2 * blocks, tall, 128), BF),
            vmem((tall_e // n, 128), BF),
            vmem((tall_k, 128), BF),
            vmem((tall_e // n, 128), BF),
            vmem((toks, D), F32),
            vmem((2, T, D), BF),
            vmem((toks, D), BF),
            vmem((D, FF), BF),
            vmem((FF, D), BF),
            vmem((toks, D), BF),
            vmem((rows, seq, KV), BF),
            vmem((rows, seq, KV), BF),
            vmem((rows, n + 1, T, KV), BF),
            vmem((EH + KV, D), BF),
            vmem((EH, D), BF),
            vmem((2, rows, 128), jnp.int32),
            vmem((rg, 2, seq, T), BF),
            vmem((rg, 2, H, T), BF),
            vmem((rg, 2, H, T), BF),
            vmem((rg, 2, T), F32),
            vmem((rg, EH, T), BF),
            vmem((half, D), F32),
            vmem((half, D), BF),
            vmem((D, half), BF),
            vmem((D, half), BF),
            vmem((half, D), F32),
            vmem((half, fblk), BF),
            vmem((half, fblk), BF),
            vmem((rows, EH, T), BF),
            dma((3,)),
            dma((rows, n + 1)),
            dma((rows, n)),
            dma((rows, n)),
            dma((rows, n + 1)),
            dma((2 * blocks + 3, 2 * steps)),
            dma((2 * blocks + 3, 2 * steps)),
            dma((2 * blocks,)),
            dma((2,)),
            dma((rows,)),
        ],
        compiler_params=pltpu.CompilerParams(
            vmem_limit_bytes=VMEM_LIMIT, collective_id=0, has_side_effects=True
        ),
    )(
        tokens.reshape(toks, D), out_grad.reshape(toks, D), segments, route, gate,
        gain_one.reshape(1, D), gain_two.reshape(1, D), kv_weight, query_weight[0].T,
        output_weight[0], up_weight, down_weight,
    )
    parts = 2
    tiles = FF // 128
    step = tiles // parts
    bt = toks // parts
    row_block = pl.BlockSpec((bt, D), lambda i: (i, 0))
    tile_block = pl.BlockSpec((step, D, 128), lambda i: (i, 0, 0))

    def full(a):
        return pl.BlockSpec(a.shape, lambda i: (0, 0))

    gain = sds((1, D), F32)
    small = (gain, gain, kvw_grad, wq_grad, wo_grad)
    dup, ddn, tg, out, gain_one_grad, gain_two_grad, kvw_grad, wq_grad, wo_grad = pl.pallas_call(
        lay_kernel,
        grid=(parts,),
        out_shape=(
            sds((D, FF), F32), sds((FF, D), F32), sds((toks, D), F32), sds((toks, D), BF),
        ) + tuple(sds(a.shape, F32) for a in small),
        in_specs=[tile_block, tile_block, row_block, row_block, full(gains)]
        + [full(a) for a in small[2:]],
        out_specs=[
            pl.BlockSpec((D, step * 128), lambda i: (0, i)),
            pl.BlockSpec((step * 128, D), lambda i: (i, 0)),
            row_block, row_block,
        ] + [full(a) for a in small],
        compiler_params=pltpu.CompilerParams(vmem_limit_bytes=VMEM_LIMIT),
    )(
        dup.reshape(tiles, D, 128), ddn.reshape(tiles, D, 128), tg, out, gains,
        kvw_grad, wq_grad, wo_grad,
    )
    return (
        out.reshape(tokens.shape),
        tg.reshape(tokens.shape),
        gain_one_grad.reshape(D),
        gain_two_grad.reshape(D),
        kvw_grad,
        wq_grad.T[None],
        wo_grad[None],
        dup,
        ddn,
    )


def solution(mesh):
    rows = P(("group", "dp"), "expert", None)
    in_specs = (
        rows,
        P(("group", "dp"), None),
        P(None, ("group", "dp"), None, None),
        rows,
        P(), P(), P(),
        P("expert", None, None),
        P("expert", None, None),
        P(), P(),
        rows,
    )
    out_specs = (
        rows, rows, P(), P(), P(),
        P("expert", None, None),
        P("expert", None, None),
        P(), P(),
    )
    return jax.shard_map(
        on_device, mesh=mesh, in_specs=in_specs, out_specs=out_specs, check_vma=False
    )
```
